32 devices in a mesh: section: 2 (over x), dp: 16 (over z, y, core).
Axes of the slice: x: 2, y: 2, z: 4, core: 2. Of those that a mesh axis runs over, the one named last changes fastest.
Arguments:
- boundary: bfloat16 [2, 6656, 768], P('section', 'dp'), may hold values from -6 to 6
- counts: int32 [64], P('dp'), may hold values from 26 to 104, as said below
- id_flags: int32 [64], P('dp'), may hold values from 0 to 1
- norm_gains: float32 [2, 2, 768], P('section'), may hold values from 0.25 to 1.75
- biases: float32 [2, 9, 768], P('section'), may hold values from -1.8 to 1.8
- qkv_weight: bfloat16 [2, 768, 2304], P('section'), may hold values from -0.21875 to 0.21875
- proj_weight: bfloat16 [2, 768, 768], P('section'), may hold values from -0.625 to 0.625
- up_weight: bfloat16 [2, 768, 768], P('section'), may hold values from -0.21875 to 0.21875
- down_weight: bfloat16 [2, 768, 768], P('section'), may hold values from -0.21875 to 0.21875
Outputs:
- layer_outputs: bfloat16 [2, 6656, 768], P('section', 'dp')
- input_grads: bfloat16 [2, 6656, 768], P('section', 'dp')
- qkv_grad: float32 [2, 768, 2304], P('section', 'dp')
- proj_grad: float32 [2, 768, 768], P('section', 'dp')
- up_grad: float32 [2, 768, 768], P('section', 'dp')
- down_grad: float32 [2, 768, 768], P('section', 'dp')
- gain_grad: float32 [2, 2, 768], P('section', None, 'dp')
- bias_grad: float32 [2, 9, 768], P('section', None, 'dp')
The draws below stay inside these ranges and needn't reach their ends.
Inputs may be any that keep to these rules, and one draw needn't show every extreme that they name: `counts`: one molecule in every draw fills all 104 slots.
All inputs are finite; a program needn't handle non-finite values.
Results may differ from the reference program's by a relative error of at most 0.015.
Values may be sent and summed in bfloat16 or wider, within the bound.
No kernel may reach another device: no remote copies, remote signals or barrier semaphores. Data moves between devices by JAX's collectives and lax.ppermute only.
A program may use at most 256 MiB of HBM per device.

```python
import math
import jax
import jax.numpy as jnp
from jax import lax

D = 768
HEADS = 32
HEAD_DIM = 24
FF = 768
MOL_LEN = 104
MOL_DEV = 4
MOLECULES = 64
TOKENS = 6656
N_SECTION = 2


def draw_counts(key, part):
    key = jax.random.fold_in(key, 11)
    key_counts, key_place = jax.random.split(key)
    drawn = jax.random.randint(key_counts, (MOLECULES,), MOL_LEN // 4, MOL_LEN + 1)
    place_at = jax.random.randint(key_place, (), 0, MOLECULES)
    return drawn.at[place_at].set(MOL_LEN).astype(jnp.int32)


def place_ends(entries, rng, least, largest):
    extent = entries.shape
    place = [jax.random.randint(jax.random.fold_in(rng, axis), (), 0, extent[axis]) for axis in range(len(extent))]
    entries = entries.at[tuple(place)].set(least)
    longest = extent.index(max(extent))
    place[longest] = (place[longest] + 1) % extent[longest]
    return entries.at[tuple(place)].set(largest)


def strengthened(values, stream_key, source, target, shards_of, factor):
    def block_of(dim):
        return (jnp.arange(values.shape[dim]) // (values.shape[dim] // shards_of)).reshape((-1,) + (1,) * (values.ndim - 1 - dim))

    one_side = jax.random.permutation(stream_key, shards_of)[block_of(target)]
    other_side = (block_of(target) + shards_of // 2) % shards_of
    return jnp.where((block_of(source) == one_side) | (block_of(source) == other_side), factor * values, values)


def block_levels(own_key, dims, cuts, smallest, high):
    factor_of, own = 1.0, jax.random.fold_in(own_key, 6)
    for position, shards_of in cuts:
        heights = jnp.exp(jax.random.uniform(jax.random.fold_in(own, position), (shards_of,), jnp.float32, smallest / len(cuts), high / len(cuts)))
        factor_of = factor_of * jnp.repeat(heights, dims[position] // shards_of).reshape([-1 if axis == position else 1 for axis in range(len(dims))])
    return factor_of


def bell_draw(key, shape, deviation, reach, cuts=(), held_as=jnp.bfloat16):
    entries = jax.random.normal(key, shape, jnp.float32) * deviation
    if len(cuts) > 0:
        entries = block_levels(key, shape, cuts, -0.22, 0.18) * entries
    return jnp.clip(entries, min=-reach, max=reach).astype(held_as)


def gaussian_with(stream_key, shape, deviation, reach, cuts, heavy, dtype=jnp.bfloat16):
    entries = deviation * jax.random.normal(stream_key, shape, jnp.float32)
    if cuts:
        entries = entries * block_levels(stream_key, shape, cuts, -0.22, 0.18)
    return jnp.clip(strengthened(entries, jax.random.fold_in(stream_key, 3), *heavy), -reach, reach).astype(dtype)


def setup_inputs(seed: int = 0) -> dict:
    keys = jax.random.split(jax.random.key(seed), 10)
    return {
        "boundary": gaussian_with(keys[0], (N_SECTION, TOKENS, D), 1.0, 6.0, ((0, 2), (1, 16)), (1, 2, 16, 2.0)),
        "counts": draw_counts(jax.random.fold_in(keys[9], 71), 0),
        "id_flags": place_ends(jax.random.randint(keys[2], (MOLECULES,), 0, 2), jax.random.fold_in(keys[2], 1), 0, 1).astype(jnp.int32),
        "norm_gains": jnp.clip(1.0 + 0.15 * jax.random.normal(keys[3], (N_SECTION, 2, D), jnp.float32), 0.25, 1.75),
        "biases": bell_draw(keys[4], (N_SECTION, 9, D), 0.3, 1.8, ((0, 2),), jnp.float32),
        "qkv_weight": bell_draw(keys[5], (N_SECTION, D, 3 * D), D ** -0.5, 0.21875, ((0, 2),)),
        "proj_weight": bell_draw(keys[6], (N_SECTION, D, D), (D // 8) ** -0.5, 0.625, ((0, 2),)),
        "up_weight": bell_draw(keys[7], (N_SECTION, D, FF), D ** -0.5, 0.21875, ((0, 2),)),
        "down_weight": bell_draw(keys[8], (N_SECTION, FF, D), FF ** -0.5, 0.21875, ((0, 2),)),
    }


@jax.custom_vjp
def low(v):
    return lax.optimization_barrier(v.astype(jnp.bfloat16)).astype(jnp.float32)

@jax.custom_vjp
def low_back(v):
    return v

def low_keep(v):
    return (low(v), None)

def low_pass(kept, grad):
    return (grad,)

def back_keep(v):
    return (v, None)

def back_low(kept, grad):
    return (low(grad),)
low.defvjp(low_keep, low_pass)
low_back.defvjp(back_keep, back_low)
EPSILON = 1e-05
HIGHEST = lax.Precision.HIGHEST

def layer_norm(values):
    centred = values - lax.optimization_barrier(jnp.mean(values, -1, keepdims=True))
    return centred * lax.rsqrt(lax.optimization_barrier(jnp.mean(centred * centred, -1, keepdims=True)) + EPSILON)

def layer_apply(hidden, group_counts, group_flags, gain_rows, bias_rows, qkv_mat, proj_mat, up_mat, down_mat):
    mol_count, seq_len, width = hidden.shape
    id_rows = jnp.where(group_flags[:, None] == 1, bias_rows[7], bias_rows[8])
    residual = hidden + id_rows[:, None, :]
    first_in = low(layer_norm(residual) * gain_rows[0] + bias_rows[0])
    qkv_bias = jnp.concatenate([bias_rows[1], jnp.zeros_like(bias_rows[1]), bias_rows[2]])
    mixed = low_back(low(jnp.einsum('mld,de->mle', first_in, qkv_mat, precision=HIGHEST) + qkv_bias))
    pieces = mixed.reshape(mol_count, seq_len, 3, HEADS, HEAD_DIM)
    scores = low_back(jnp.einsum('mqhd,mkhd->mhqk', pieces[:, :, 0], pieces[:, :, 1], precision=HIGHEST) * (1.0 / math.sqrt(HEAD_DIM)))
    valid_keys = jnp.arange(seq_len)[None, :] < group_counts[:, None]
    scores = jnp.where(valid_keys[:, None, None, :], scores, -1e+30)
    attn_probs = low(jax.nn.softmax(scores, axis=-1))
    attended = jnp.einsum('mhqk,mkhd->mqhd', attn_probs, pieces[:, :, 2], precision=HIGHEST)
    attended = low_back(low(attended.reshape(mol_count, seq_len, width)))
    middle = residual + low_back(jnp.einsum('mld,de->mle', attended, proj_mat, precision=HIGHEST) + bias_rows[3])
    second_in = low(layer_norm(middle) * gain_rows[1] + bias_rows[4])
    pre_act = low_back(jnp.einsum('mld,de->mle', second_in, up_mat, precision=HIGHEST) + bias_rows[5])
    activated = low(jax.nn.gelu(pre_act, approximate=False))
    return middle + jnp.einsum('mle,ed->mld', activated, down_mat, precision=HIGHEST) + bias_rows[6]

def reference(boundary, counts, id_flags, norm_gains, biases, qkv_weight, proj_weight, up_weight, down_weight):
    group_size = MOL_DEV * 4
    n_groups = MOLECULES // group_size
    inputs = boundary[0].astype(jnp.float32).reshape(n_groups, group_size, MOL_LEN, D)
    cotangents = boundary[1].astype(jnp.float32).reshape(n_groups, group_size, MOL_LEN, D)
    weights = (norm_gains.astype(jnp.float32), biases.astype(jnp.float32), qkv_weight.astype(jnp.float32), proj_weight.astype(jnp.float32), up_weight.astype(jnp.float32), down_weight.astype(jnp.float32))

    def one_group(totals, item):
        group_in, group_cot, group_counts, group_flags = item

        def run_pair(first_input, gains_all, biases_all, qkv_all, proj_all, up_all, down_all, extra_in):
            sent = low(layer_apply(first_input, group_counts, group_flags, gains_all[0], biases_all[0], qkv_all[0], proj_all[0], up_all[0], down_all[0]))
            passed = low_back(sent) + extra_in
            last = layer_apply(passed, group_counts, group_flags, gains_all[1], biases_all[1], qkv_all[1], proj_all[1], up_all[1], down_all[1])
            return (sent, last)
        outputs, pullback = jax.vjp(run_pair, group_in, *weights, jnp.zeros_like(group_in))
        gradients = pullback((jnp.zeros_like(outputs[0]), group_cot))
        totals = tuple((total + grad_part for total, grad_part in zip(totals, gradients[1:7])))
        return (totals, (outputs[0], outputs[1], gradients[0], gradients[7]))
    initial = tuple((jnp.zeros(tensor.shape, jnp.float32) for tensor in weights))
    totals, stacked = lax.scan(one_group, initial, (inputs, cotangents, counts.reshape(n_groups, group_size), id_flags.reshape(n_groups, group_size)))
    first_out, last_out, first_grad, last_grad = stacked
    layer_outputs = jnp.stack([first_out.reshape(TOKENS, D), last_out.reshape(TOKENS, D)]).astype(jnp.bfloat16)
    input_grads = jnp.stack([first_grad.reshape(TOKENS, D), last_grad.reshape(TOKENS, D)]).astype(jnp.bfloat16)
    return (layer_outputs, input_grads, totals[2], totals[3], totals[4], totals[5], totals[0], totals[1])
```

```python
import functools
import math

import jax
import jax.numpy as jnp
from jax import lax
from jax.experimental import pallas as pl
from jax.experimental.pallas import tpu as pltpu
from jax.sharding import PartitionSpec as P

HEADS = 32
HEAD_DIM = 24
PAIRS = HEADS // 2
PAIR_ROWS = 2 * HEAD_DIM
LANES = 128
EPSILON = 1e-05
SCALE = 1.0 / math.sqrt(HEAD_DIM)
LOG2E = math.log2(math.e)

low = jnp.bfloat16
wide = jnp.float32

VMEM = pl.BlockSpec(memory_space=pltpu.VMEM)
SMEM = pl.BlockSpec(memory_space=pltpu.SMEM)
ANY = pl.BlockSpec(memory_space=pl.ANY)


def nn(left, right):
    return lax.dot_general(left, right, (((1,), (0,)), ((), ())), preferred_element_type=wide)


def nt(left, right):
    return lax.dot_general(left, right, (((1,), (1,)), ((), ())), preferred_element_type=wide)


def tn(left, right):
    return lax.dot_general(left, right, (((0,), (0,)), ((), ())), preferred_element_type=wide)


def pad_rows(values):
    extra = -values.shape[0] % LANES
    return jnp.concatenate([values, jnp.zeros((extra, values.shape[1]), values.dtype)], 0)


def two_blocks(rows):
    first = lax.broadcasted_iota(jnp.int32, rows.shape, 0) < HEAD_DIM
    zeros = jnp.zeros_like(rows)
    return jnp.concatenate([jnp.where(first, rows, zeros), jnp.where(first, zeros, rows)], 1)


def own_blocks(product):
    return jnp.concatenate([product[:HEAD_DIM, :LANES], product[HEAD_DIM:, LANES:]], 0)


def normalize(values):
    centred = values - jnp.mean(values, -1, keepdims=True)
    rstd = lax.rsqrt(jnp.mean(centred * centred, -1, keepdims=True) + EPSILON)
    return centred * rstd, rstd


def norm_back(scaled, normed, rstd):
    return rstd * (
        scaled
        - jnp.mean(scaled, -1, keepdims=True)
        - normed * jnp.mean(scaled * normed, -1, keepdims=True)
    )


def total(values):
    return jnp.sum(values, 0, keepdims=True)


def molecule_rows(ref, index, length):
    start = index * length
    base = start - start % 16
    stop = start + length
    stop = min(stop + (-stop) % 16, ref.shape[0])
    return ref[base:stop].astype(wide)[start - base : start - base + length]


class Refs:
    def __init__(self, names, refs):
        for name, ref in zip(names, refs, strict=True):
            setattr(self, name, ref)


def forward(r, mol, x, length):
    width = x.shape[1]
    id_row = jnp.where(r.flags[mol] == 1, r.biases[7:8], r.biases[8:9])
    residual = x + id_row
    normed, rstd = normalize(residual)
    r.n1[mol] = normed
    r.r1[mol] = jnp.broadcast_to(rstd, (length, LANES))
    r.residual[...] = residual
    first_in = pad_rows(normed * r.gains[0:1] + r.biases[0:1]).astype(low)
    r.first_in[mol] = first_in
    first_in = first_in[:length]
    for third, bias in enumerate((1, None, 2)):
        part = nn(first_in, r.qkv[:, third * width : (third + 1) * width])
        if bias is not None:
            part = part + r.biases[bias : bias + 1]
        (r.q, r.k, r.v)[third][mol] = pad_rows(part).astype(low).T
    for p in range(PAIRS):
        at = slice(p * PAIR_ROWS, (p + 1) * PAIR_ROWS)
        r.scores[p] = tn(r.k[mol, at, :length], two_blocks(r.q[mol, at, :]))
    key_index = lax.broadcasted_iota(jnp.int32, (length, 2 * LANES), 0)
    key_bias = jnp.where(key_index < r.counts[mol], 0.0, -1e30)
    for p in range(PAIRS):
        scores = r.scores[p] * (SCALE * LOG2E) + key_bias
        weights = jnp.exp2(scores - jnp.max(scores, 0, keepdims=True))
        weights = weights * (1.0 / jnp.sum(weights, 0, keepdims=True))
        r.probs[mol, p] = weights.astype(low)
    for p in range(PAIRS):
        at = slice(p * PAIR_ROWS, (p + 1) * PAIR_ROWS)
        r.att_t[mol, at, :] = own_blocks(nn(r.v[mol, at, :length], r.probs[mol, p])).astype(low)
    attended = r.att_t[mol].T[:length]
    r.attended[mol] = pad_rows(attended.astype(wide)).astype(low)
    middle = r.residual[...] + nn(attended, r.proj[...]) + r.biases[3:4]
    normed, rstd = normalize(middle)
    r.n2[mol] = normed
    r.r2[mol] = jnp.broadcast_to(rstd, (length, LANES))
    r.residual[...] = middle
    second_in = pad_rows(normed * r.gains[1:2] + r.biases[4:5]).astype(low)
    r.second_in[mol] = second_in
    pre_act = nn(second_in[:length], r.up[...]) + r.biases[5:6]
    cdf = 0.5 * (1.0 + lax.erf(pre_act * math.sqrt(0.5)))
    pdf = jnp.exp(-0.5 * pre_act * pre_act) * (1.0 / math.sqrt(2.0 * math.pi))
    r.slope[mol] = cdf + pre_act * pdf
    activated = pad_rows(pre_act * cdf).astype(low)
    r.activated[mol] = activated
    result = r.residual[...] + nn(activated[:length], r.down[...]) + r.biases[6:7]
    result = result.astype(low)
    r.outputs[mol] = result
    r.result[...] = result


def backward_dense(r, mol, out_grad, length):
    out_low = out_grad.astype(low)
    r.out_grad[mol] = pad_rows(out_grad).astype(low)
    pre_grad = nt(out_low, r.down[...]) * r.slope[mol]
    r.pre_grad[mol] = pad_rows(pre_grad).astype(low)
    pre_grad = pre_grad.astype(low)
    second_grad = nt(pre_grad, r.up[...])
    normed = r.n2[mol]
    sums = [
        total(second_grad * normed),
        total(second_grad),
        total(pre_grad.astype(wide)),
        total(out_grad),
    ]
    middle_grad = out_grad + norm_back(second_grad * r.gains[1:2], normed, r.r2[mol][:, :1])
    r.middle_grad[...] = middle_grad
    r.branch_grad[mol] = pad_rows(middle_grad).astype(low)
    branch_grad = middle_grad.astype(low)
    sums.append(total(branch_grad.astype(wide)))
    sums.append(jnp.zeros((3, out_grad.shape[1]), wide))
    r.dense_sums[mol] = jnp.concatenate(sums, 0)
    r.att_grad[...] = pad_rows(nt(branch_grad, r.proj[...])).astype(low).T


def backward_attention(r, mol, length):
    width = r.middle_grad.shape[1]
    products = r.att_t[mol].astype(wide) * r.att_grad[...].astype(wide)
    delta = jnp.sum(products.reshape(HEADS, HEAD_DIM, LANES), 1)
    for p in range(PAIRS):
        at = slice(p * PAIR_ROWS, (p + 1) * PAIR_ROWS)
        r.scores[p] = tn(r.v[mol, at, :length], two_blocks(r.att_grad[at, :]))
    for p in range(PAIRS):
        row = jnp.concatenate([delta[2 * p : 2 * p + 1], delta[2 * p + 1 : 2 * p + 2]], 1)
        grad = r.probs[mol, p].astype(wide) * (r.scores[p] - row)
        r.score_grad[p] = grad.astype(low)
    pad = jnp.zeros((PAIR_ROWS, LANES - length), wide)
    for p in range(PAIRS):
        at = slice(p * PAIR_ROWS, (p + 1) * PAIR_ROWS)
        grad = r.score_grad[p]
        query = own_blocks(nn(r.k[mol, at, :length], grad)) * SCALE
        key = nt(two_blocks(r.q[mol, at, :]), grad) * SCALE
        value = nt(two_blocks(r.att_grad[at, :]), r.probs[mol, p])
        r.mixed_t[0, at, :] = query.astype(low)
        r.mixed_t[1, at, :] = jnp.concatenate([key, pad], 1).astype(low)
        r.mixed_t[2, at, :] = jnp.concatenate([value, pad], 1).astype(low)
    first_grad = None
    mixed_sums = []
    for third in range(3):
        columns = slice(third * width, (third + 1) * width)
        mixed = r.mixed_t[third].T
        r.mixed_grad[mol, :, columns] = mixed
        mixed_sums.append(total(mixed.astype(wide)))
        part = nt(mixed[:length], r.qkv[:, columns])
        first_grad = part if first_grad is None else first_grad + part
    normed = r.n1[mol]
    residual_grad = r.middle_grad[...] + norm_back(
        first_grad * r.gains[0:1], normed, r.r1[mol][:, :1]
    )
    low_grad = residual_grad.astype(low)
    r.grads[mol] = low_grad
    r.grad[...] = low_grad
    kind_sum = total(residual_grad)
    laplace = r.flags[mol] == 1
    zero = jnp.zeros_like(kind_sum)
    r.attn_sums[mol] = jnp.concatenate(
        [
            total(first_grad * normed),
            total(first_grad),
            mixed_sums[0],
            mixed_sums[2],
            jnp.where(laplace, kind_sum, zero),
            jnp.where(laplace, zero, kind_sum),
            zero,
            zero,
        ],
        0,
    )


INFO = ("place", "counts", "flags")
PARAMS = ("gains", "biases", "qkv", "proj", "up", "down")
SAVED = (
    "q", "k", "v", "probs", "att_t", "n1", "r1", "n2", "r2", "slope",
    "first_in", "attended", "second_in", "activated", "outputs",
)
PIECES = ("out_grad", "pre_grad", "branch_grad", "dense_sums")
LATE = ("mixed_grad", "attn_sums", "grads")
CARRY = ("middle_grad", "att_grad")


class Sizes:
    def __init__(self, mols, length, width, hidden):
        self.mols, self.length, self.width, self.hidden = mols, length, width, hidden
        self.padded = length + (-length) % LANES

    def shapes(self):
        m, n, d, f, p = self.mols, self.length, self.width, self.hidden, self.padded
        struct = jax.ShapeDtypeStruct
        return {
            "q": struct((m, d, LANES), low),
            "k": struct((m, d, LANES), low),
            "v": struct((m, d, LANES), low),
            "probs": struct((m, PAIRS, n, 2 * LANES), low),
            "att_t": struct((m, d, LANES), low),
            "n1": struct((m, n, d), wide),
            "r1": struct((m, n, LANES), wide),
            "n2": struct((m, n, d), wide),
            "r2": struct((m, n, LANES), wide),
            "slope": struct((m, n, f), wide),
            "first_in": struct((m, p, d), low),
            "attended": struct((m, p, d), low),
            "second_in": struct((m, p, d), low),
            "activated": struct((m, p, f), low),
            "outputs": struct((m, n, d), low),
            "out_grad": struct((m, p, d), low),
            "pre_grad": struct((m, p, f), low),
            "branch_grad": struct((m, p, d), low),
            "dense_sums": struct((m, 8, d), wide),
            "mixed_grad": struct((m, p, 3 * d), low),
            "attn_sums": struct((m, 8, d), wide),
            "grads": struct((m, n, d), low),
            "middle_grad": struct((n, d), wide),
            "att_grad": struct((d, LANES), low),
            "result": struct((n, d), low),
            "grad": struct((n, d), low),
            "residual": struct((n, d), wide),
            "scores": struct((PAIRS, n, 2 * LANES), wide),
            "score_grad": struct((PAIRS, n, 2 * LANES), low),
            "mixed_t": struct((3, d, LANES), low),
        }


def call(body, sizes, ins, in_specs, kept, fresh, scratch, name):
    shapes = sizes.shapes()
    given = [n for n in kept if kept[n] is not None]
    names = list(ins) + ["_" + n for n in given] + list(kept) + list(fresh) + list(scratch)
    operands = list(ins.values()) + [kept[n] for n in given]
    aliases = {len(ins) + i: list(kept).index(n) for i, n in enumerate(given)}

    def kernel(*refs):
        body(Refs(names, refs))

    outs = pl.pallas_call(
        kernel,
        name=name,
        out_shape=[pltpu.VMEM(shapes[n].shape, shapes[n].dtype) for n in kept]
        + [shapes[n] for n in fresh],
        in_specs=[in_specs.get(n, VMEM) for n in ins] + [VMEM] * len(given),
        out_specs=[VMEM] * (len(kept) + len(fresh)),
        scratch_shapes=[pltpu.VMEM(shapes[n].shape, shapes[n].dtype) for n in scratch],
        input_output_aliases=aliases,
        compiler_params=pltpu.CompilerParams(vmem_limit_bytes=24 << 20),
    )(*operands)
    return dict(zip(list(kept) + list(fresh), outs, strict=True))


def weight_call(sizes, place, lefts, rights, extra, columns, split, name):
    d = sizes.width
    n_left, n_extra = len(lefts), len(extra)
    owners, rows = split
    tokens = sizes.mols * sizes.padded

    def kernel(*refs):
        place_ref = refs[0]
        left_refs = refs[1 : 1 + n_left]
        right_refs = refs[1 + n_left : 1 + 2 * n_left]
        extra_refs = refs[1 + 2 * n_left : 1 + 2 * n_left + n_extra]
        keep, send, result, left_t, sems = refs[1 + 2 * n_left + n_extra :]
        own = place_ref[1]
        copies = []

        def flush(index, at):
            for slot, (target, core) in enumerate(((send, 1 - own), (keep, own))):
                copy = pltpu.make_async_copy(
                    result.at[:, core, :, pl.ds(at[0], at[1])],
                    target.at[:, :, pl.ds(at[0], at[1])],
                    sems.at[index, slot],
                )
                copy.start()
                copies.append(copy)

        done = 0
        position = 0
        index = 0
        if n_extra:
            dense = jnp.sum(extra_refs[0][...], 0)
            attn = jnp.sum(extra_refs[1][...], 0)
            both = jnp.concatenate([dense, attn], 0)
            high = both.astype(low).astype(wide)
            rest = both - high
            zeros = jnp.zeros((LANES - 32, d), wide)
            table = jnp.concatenate([high, rest, zeros], 0).T.astype(low)
            for o in range(owners):
                result[o // 2, o % 2, :, 0:LANES] = table[o * rows : (o + 1) * rows]
            position = LANES
        for left, right in zip(left_refs, right_refs, strict=True):
            left_t[...] = left[...].reshape(tokens, d).T
            for base in range(0, right.shape[2], 256):
                part = right[:, :, base : base + 256].reshape(tokens, 256)
                for half in range(2):
                    size = d // 2
                    out = nn(left_t[half * size : (half + 1) * size], part).astype(low)
                    for b in range(size // rows):
                        o = half * (size // rows) + b
                        result[o // 2, o % 2, :, position : position + 256] = out[
                            b * rows : (b + 1) * rows
                        ]
                position += 256
                if position - done >= 768:
                    flush(index, (done, position - done))
                    done = position
                    index += 1
        if position > done:
            flush(index, (done, position - done))
        for copy in copies:
            copy.wait()

    shape = jax.ShapeDtypeStruct((owners // 2, rows, columns), low)
    return pl.pallas_call(
        kernel,
        name=name,
        out_shape=[shape, shape],
        in_specs=[SMEM] + [VMEM] * (2 * n_left + n_extra),
        out_specs=[ANY, ANY],
        scratch_shapes=[
            pltpu.VMEM((owners // 2, 2, rows, columns), low),
            pltpu.VMEM((d, tokens), low),
            pltpu.SemaphoreType.DMA((8, 2)),
        ],
        compiler_params=pltpu.CompilerParams(vmem_limit_bytes=24 << 20),
    )(place, *lefts, *rights, *extra)


def halve(keep, received, axis, mine):
    whole = keep + received
    send = lax.dynamic_index_in_dim(whole, 1 - mine, axis, keepdims=False)
    own = lax.dynamic_index_in_dim(whole, mine, axis, keepdims=False)
    return send, own


def swap(block, bit):
    devices = lax.axis_size("dp")
    return lax.ppermute(block, "dp", [(i, i ^ bit) for i in range(devices)])


def scatter_rows(keep, send, bits):
    index = lax.axis_index("dp")
    received = swap(send, 1)
    count, rows, columns = keep.shape
    for bit in bits:
        count //= 2
        shape = (count, 2, rows, columns)
        mine = (index // bit) % 2
        send, keep = halve(keep.reshape(shape), received.reshape(shape), 1, mine)
        received = swap(send, bit)
    return (keep.astype(wide) + received.astype(wide))[0]


def weight_sums(sizes, lefts, rights, extra):
    tokens = sizes.mols * sizes.padded
    parts = []
    if extra:
        both = jnp.concatenate([jnp.sum(e, 0) for e in extra], 0)
        parts.append(jnp.pad(both, ((0, LANES - 16), (0, 0))).T)
    for left, right in zip(lefts, rights, strict=True):
        parts.append(tn(left.reshape(tokens, -1), right.reshape(tokens, -1)))
    whole = jnp.concatenate(parts, 1)
    return lax.psum_scatter(whole, "dp", scatter_dimension=0, tiled=True)


def body(
    boundary, counts, id_flags, norm_gains, biases, qkv_weight, proj_weight, up_weight, down_weight
):
    mols = counts.shape[0]
    width = boundary.shape[2]
    length = boundary.shape[1] // mols
    sizes = Sizes(mols, length, width, up_weight.shape[2])
    devices = lax.axis_size("dp")
    section = lax.axis_index("section")
    place = jnp.stack([section, lax.axis_index("dp") % 2]).astype(jnp.int32)
    ins = {
        "place": place,
        "counts": counts,
        "flags": id_flags,
        "ends": boundary[0],
        "gains": norm_gains[0],
        "biases": biases[0],
        "qkv": qkv_weight[0],
        "proj": proj_weight[0],
        "up": up_weight[0],
        "down": down_weight[0],
    }
    specs = {"place": SMEM, "counts": SMEM, "flags": SMEM}
    state = {}

    def kept(names):
        return {n: state.get(n) for n in names}

    def first_forward(mol):
        def run(r):
            @pl.when(r.place[0] == 0)
            def _():
                forward(r, mol, molecule_rows(r.ends, mol, length), length)

        out = call(
            run, sizes, ins, specs, kept(SAVED), ["result"], ["residual", "scores"], f"first_{mol}"
        )
        result = out.pop("result")
        state.update(out)
        return result

    def tick(second_mol, first_mol, received, received_grad, name):
        given = dict(ins)
        if second_mol is not None:
            given["received"] = received
        if first_mol is not None:
            given["received_grad"] = received_grad

        def run(r):
            if second_mol is not None:

                @pl.when(r.place[0] == 1)
                def _():
                    forward(r, second_mol, r.received[...].astype(wide), length)
                    r.cotangent[...] = molecule_rows(r.ends, second_mol, length)

            if first_mol is not None:

                @pl.when(r.place[0] == 0)
                def _():
                    r.cotangent[...] = r.received_grad[...].astype(wide)

            if second_mol is None:
                active = r.place[0] == 0
                mol = first_mol
            elif first_mol is None:
                active = r.place[0] == 1
                mol = second_mol
            else:
                active = None
                mol = jnp.where(r.place[0] == 1, second_mol, first_mol)

            def back():
                backward_dense(r, mol, r.cotangent[...], length)
                backward_attention(r, mol, length)

            if active is None:
                back()
            else:
                pl.when(active)(back)

        names = SAVED if second_mol is not None else ()
        extra = {} if second_mol is not None else kept(SAVED)
        scratch = ["residual", "scores", "score_grad", "mixed_t", "middle_grad", "att_grad"]
        fresh = ["grad"] + (["result"] if second_mol is not None else [])
        out = call(
            functools.partial(with_cotangent, run, length, width),
            sizes,
            given | extra,
            specs,
            kept(names + PIECES + LATE),
            fresh,
            scratch,
            name,
        )
        out.pop("result", None)
        grad = out.pop("grad")
        state.update(out)
        return grad

    def with_cotangent(run, rows, columns, r):
        def inner(ref):
            r.cotangent = ref
            run(r)

        pl.run_scoped(inner, pltpu.VMEM((rows, columns), wide))

    forward_hops = []
    for mol in range(mols):
        result = first_forward(mol)
        forward_hops.append(lax.ppermute(result, "section", [(0, 1)]))
    grad_hops = []
    for step in range(mols + 1):
        second = step if step < mols else None
        first = step - 2 if step >= 2 else None
        grad = tick(
            second,
            first,
            forward_hops[step] if second is not None else None,
            grad_hops[step - 2] if first is not None else None,
            f"tick_{step}",
        )
        if second is not None:
            grad_hops.append(lax.ppermute(grad, "section", [(1, 0)]))

    last = mols - 1

    def last_dense(r):
        @pl.when(r.place[0] == 0)
        def _():
            backward_dense(r, last, r.received_grad[...].astype(wide), length)

    dense_in = dict(ins, received_grad=grad_hops[last])
    dense_in.update({n: state[n] for n in ("slope", "n2", "r2")})
    out = call(last_dense, sizes, dense_in, specs, kept(PIECES), CARRY, [], "last_dense")
    carry = {n: out.pop(n) for n in CARRY}
    state.update(out)

    rows = width // devices
    split = (devices, rows)
    in_kernel = rows % 16 == 0
    dense_pieces = (
        [state["second_in"], state["activated"], state["attended"]],
        [state["pre_grad"], state["out_grad"], state["branch_grad"]],
        [],
    )
    dense_columns = 2 * width + sizes.hidden
    if in_kernel:
        keep, send = weight_call(
            sizes, place, *dense_pieces, dense_columns, split, "dense_weights"
        )

    def last_attention(r):
        @pl.when(r.place[0] == 0)
        def _():
            backward_attention(r, last, length)

    attn_in = dict(ins, **carry)
    attn_in.update({n: state[n] for n in ("q", "k", "v", "probs", "att_t", "n1", "r1")})
    out = call(
        last_attention,
        sizes,
        attn_in,
        specs,
        kept(LATE),
        ["grad"],
        ["scores", "score_grad", "mixed_t"],
        "last_attention",
    )
    out.pop("grad")
    state.update(out)
    late_pieces = (
        [state["first_in"]],
        [state["mixed_grad"]],
        [state["dense_sums"], state["attn_sums"]],
    )
    late_columns = 3 * width + LANES
    if in_kernel:
        keep_late, send_late = weight_call(
            sizes, place, *late_pieces, late_columns, split, "attention_weights"
        )
        bits = [1 << b for b in range(1, devices.bit_length() - 1)]
        dense_total = scatter_rows(keep, send, bits)
        late_total = scatter_rows(keep_late, send_late, bits)
    else:
        dense_total = weight_sums(sizes, *dense_pieces)
        late_total = weight_sums(sizes, *late_pieces)
    up_grad = dense_total[:, : sizes.hidden]
    down_grad = dense_total[:, sizes.hidden : sizes.hidden + width]
    proj_grad = dense_total[:, sizes.hidden + width :]
    table = late_total[:, :16] + late_total[:, 16:32]
    vectors = table.T
    gain_grad = jnp.stack([vectors[8], vectors[0]])
    bias_grad = jnp.stack([vectors[i] for i in (9, 10, 11, 4, 1, 2, 3, 12, 13)])
    return (
        state["outputs"].reshape(boundary.shape),
        state["grads"].reshape(boundary.shape),
        late_total[:, LANES:][None],
        proj_grad[None],
        up_grad[None],
        down_grad[None],
        gain_grad[None],
        bias_grad[None],
    )


def solution(mesh):
    placed = (
        P("section", "dp", None),
        P("dp"),
        P("dp"),
        P("section", None, None),
        P("section", None, None),
        P("section", None, None),
        P("section", None, None),
        P("section", None, None),
        P("section", None, None),
    )
    return jax.shard_map(
        body,
        mesh=mesh,
        in_specs=placed,
        out_specs=(
            P("section", "dp", None),
            P("section", "dp", None),
            P("section", "dp", None),
            P("section", "dp", None),
            P("section", "dp", None),
            P("section", "dp", None),
            P("section", None, "dp"),
            P("section", None, "dp"),
        ),
        check_vma=False,
    )
```

```python
import functools
import math

import jax
import jax.numpy as jnp
from jax import lax
from jax.experimental import pallas as pl
from jax.experimental.pallas import tpu as pltpu
from jax.sharding import PartitionSpec as P

HEADS = 32
HEAD_DIM = 24
PAIRS = HEADS // 2
PAIR_ROWS = 2 * HEAD_DIM
LANES = 128
EPSILON = 1e-05
SCALE = 1.0 / math.sqrt(HEAD_DIM)
LOG2E = math.log2(math.e)

low = jnp.bfloat16
wide = jnp.float32

VMEM = pl.BlockSpec(memory_space=pltpu.VMEM)
SMEM = pl.BlockSpec(memory_space=pltpu.SMEM)
ANY = pl.BlockSpec(memory_space=pl.ANY)


def nn(left, right):
    return lax.dot_general(left, right, (((1,), (0,)), ((), ())), preferred_element_type=wide)


def nt(left, right):
    return lax.dot_general(left, right, (((1,), (1,)), ((), ())), preferred_element_type=wide)


def tn(left, right):
    return lax.dot_general(left, right, (((0,), (0,)), ((), ())), preferred_element_type=wide)


def pad_rows(values):
    extra = -values.shape[0] % LANES
    return jnp.concatenate([values, jnp.zeros((extra, values.shape[1]), values.dtype)], 0)


def two_blocks(rows):
    first = lax.broadcasted_iota(jnp.int32, rows.shape, 0) < HEAD_DIM
    zeros = jnp.zeros_like(rows)
    return jnp.concatenate([jnp.where(first, rows, zeros), jnp.where(first, zeros, rows)], 1)


def own_blocks(product):
    return jnp.concatenate([product[:HEAD_DIM, :LANES], product[HEAD_DIM:, LANES:]], 0)


def normalize(values):
    centred = values - jnp.mean(values, -1, keepdims=True)
    rstd = lax.rsqrt(jnp.mean(centred * centred, -1, keepdims=True) + EPSILON)
    return centred * rstd, rstd


def norm_back(scaled, normed, rstd):
    return rstd * (
        scaled
        - jnp.mean(scaled, -1, keepdims=True)
        - normed * jnp.mean(scaled * normed, -1, keepdims=True)
    )


def total(values):
    return jnp.sum(values, 0, keepdims=True)


def molecule_rows(ref, mols, length):
    start = mols[0] * length
    stop = start + len(mols) * length
    base = start - start % 16
    return ref[base : min(stop + -stop % 16, ref.shape[0])].astype(wide)[start - base : stop - base]


TAIL = (
    "hidden", "hidden1", "middle", "attention", "middle1", "qk", "v", "qk1", "hidden2", "v1", "middle2",
    "hidden3", "middle3", "qk2", "v2", "qk3", "middle4", "v3", "hidden4", "qk4", "v4",
)
CUTS = {
    "hidden": lambda width, hidden: [width, hidden],
    "middle": lambda width, hidden: [width],
    "qk": lambda width, hidden: [2 * width],
    "v": lambda width, hidden: [width, None],
}


class Refs:
    def __init__(self, names, refs):
        for name, ref in zip(names, refs, strict=True):
            setattr(self, name, ref)

    def count(self, mol):
        return self.info[COUNTS + mol]

    def flag(self, mol):
        return self.info[COUNTS + (self.info.shape[0] - COUNTS) // 2 + mol]


def no_wait(name):
    pass


def forward(r, mols, x, length, wait=no_wait):
    width = x.shape[1]
    rows = [slice(i * length, (i + 1) * length) for i in range(len(mols))]
    all_rows = slice(0, len(mols) * length)

    def save(ref, values):
        for mol, at in zip(mols, rows):
            ref[mol] = pad_rows(values[at]).astype(low)

    wait("biases")
    id_rows = [
        jnp.where(r.flag(mol) == 1, r.biases[7], r.biases[8]) for mol in mols
    ]
    residual = jnp.concatenate([x[at] + row for at, row in zip(rows, id_rows)], 0)
    normed, rstd = normalize(residual)
    for mol, at in zip(mols, rows):
        r.n1[mol] = normed[at]
        r.r1[mol] = jnp.broadcast_to(rstd[at], (length, LANES))
    r.residual[all_rows] = residual
    wait("gains")
    first_in = normed * r.gains[0:1] + r.biases[0]
    save(r.first_in, first_in)
    first_in = first_in.astype(low)
    for third, bias in enumerate((1, None, 2)):
        wait(f"qkv_{third}")
        part = nn(first_in, r.qkv[:, third * width : (third + 1) * width])
        if bias is not None:
            part = part + r.biases[bias]
        for mol, at in zip(mols, rows):
            (r.q, r.k, r.v)[third][mol] = pad_rows(part[at]).astype(low).T
    key_index = lax.broadcasted_iota(jnp.int32, (length, 2 * LANES), 0)
    for mol in mols:
        for p in range(PAIRS):
            at = slice(p * PAIR_ROWS, (p + 1) * PAIR_ROWS)
            r.scores[p] = tn(r.k[mol, at, :length], two_blocks(r.q[mol, at, :]))
        key_bias = jnp.where(key_index < r.count(mol), 0.0, -1e30)
        for p in range(PAIRS):
            scores = r.scores[p] * (SCALE * LOG2E) + key_bias
            weights = jnp.exp2(scores - jnp.max(scores, 0, keepdims=True))
            weights = weights * (1.0 / jnp.sum(weights, 0, keepdims=True))
            r.probs[mol, p] = weights.astype(low)
        for p in range(PAIRS):
            at = slice(p * PAIR_ROWS, (p + 1) * PAIR_ROWS)
            product = nn(r.v[mol, at, :length], r.probs[mol, p])
            r.att_t[mol, at, :] = own_blocks(product).astype(low)
    attended = jnp.concatenate([r.att_t[mol].T[:length].astype(wide) for mol in mols], 0)
    wait("proj")
    middle = r.residual[all_rows] + nn(attended.astype(low), r.proj[...]) + r.biases[3]
    normed, rstd = normalize(middle)
    for mol, at in zip(mols, rows):
        r.n2[mol] = normed[at]
        r.r2[mol] = jnp.broadcast_to(rstd[at], (length, LANES))
    r.residual[all_rows] = middle
    second_in = normed * r.gains[1:2] + r.biases[4]
    save(r.second_in, second_in)
    wait("up")
    pre_act = nn(second_in.astype(low), r.up[...]) + r.biases[5]
    cdf = 0.5 * (1.0 + lax.erf(pre_act * math.sqrt(0.5)))
    pdf = jnp.exp(-0.5 * pre_act * pre_act) * (1.0 / math.sqrt(2.0 * math.pi))
    slope = cdf + pre_act * pdf
    for mol, at in zip(mols, rows):
        r.slope[mol] = slope[at]
    activated = pre_act * cdf
    save(r.activated, activated)
    wait("down")
    result = r.residual[all_rows] + nn(activated.astype(low), r.down[...]) + r.biases[6]
    for mol, at in zip(mols, rows):
        r.outputs[mol] = result[at].astype(low)
    r.result[...] = result.astype(low)


def by_molecule(ref, mols):
    return jnp.concatenate([ref[mol] for mol in mols], 0)


def save_cotangent(r, mols, out_grad, length):
    for i, mol in enumerate(mols):
        r.out_grad[mol] = pad_rows(out_grad[i * length : (i + 1) * length]).astype(low)


def backward_hidden(r, mols, out_grad, length):
    pre_grad = nt(out_grad.astype(low), r.down[...]) * by_molecule(r.slope, mols)
    for i, mol in enumerate(mols):
        at = slice(i * length, (i + 1) * length)
        r.pre_grad[mol] = pad_rows(pre_grad[at]).astype(low)


def backward_middle(r, mols, out_grad, length):
    rows = [slice(i * length, (i + 1) * length) for i in range(len(mols))]
    pre_grad = jnp.concatenate([r.pre_grad[mol].astype(wide)[:length] for mol in mols], 0)
    second_grad = nt(pre_grad.astype(low), r.up[...])
    normed = by_molecule(r.n2, mols)
    rstd = by_molecule(r.r2, mols)[:, :1]
    middle_grad = out_grad + norm_back(second_grad * r.gains[1:2], normed, rstd)
    r.middle_grad[: len(mols) * length] = middle_grad
    branch_grad = middle_grad.astype(low)
    sums = [
        total(second_grad * normed),
        total(second_grad),
        total(pre_grad),
        total(out_grad),
        total(branch_grad.astype(wide)),
        jnp.zeros((3, out_grad.shape[1]), wide),
    ]
    r.dense_sums[mols[0]] = jnp.concatenate(sums, 0)
    for mol in mols[1:]:
        r.dense_sums[mol] = jnp.zeros((8, out_grad.shape[1]), wide)
    att_grad = nt(branch_grad, r.proj[...])
    for i, (mol, at) in enumerate(zip(mols, rows)):
        r.branch_grad[mol] = pad_rows(middle_grad[at]).astype(low)
        r.att_grad[i] = pad_rows(att_grad[at]).astype(low).T


def backward_attention(r, mols, length):
    width = r.middle_grad.shape[1]
    pad = jnp.zeros((PAIR_ROWS, LANES - length), wide)
    for i, mol in enumerate(mols):
        products = r.att_t[mol].astype(wide) * r.att_grad[i].astype(wide)
        delta = jnp.sum(products.reshape(HEADS, HEAD_DIM, LANES), 1)
        for p in range(PAIRS):
            at = slice(p * PAIR_ROWS, (p + 1) * PAIR_ROWS)
            r.scores[p] = tn(r.v[mol, at, :length], two_blocks(r.att_grad[i, at, :]))
        for p in range(PAIRS):
            row = jnp.concatenate([delta[2 * p : 2 * p + 1], delta[2 * p + 1 : 2 * p + 2]], 1)
            grad = r.probs[mol, p].astype(wide) * (r.scores[p] - row)
            r.score_grad[p] = grad.astype(low)
        for p in range(PAIRS):
            at = slice(p * PAIR_ROWS, (p + 1) * PAIR_ROWS)
            grad = r.score_grad[p]
            query = own_blocks(nn(r.k[mol, at, :length], grad)) * SCALE
            key = nt(two_blocks(r.q[mol, at, :]), grad) * SCALE
            value = nt(two_blocks(r.att_grad[i, at, :]), r.probs[mol, p])
            r.mixed_t[0, at, :] = query.astype(low)
            r.mixed_t[1, at, :] = jnp.concatenate([key, pad], 1).astype(low)
            r.mixed_t[2, at, :] = jnp.concatenate([value, pad], 1).astype(low)
        for third in range(3):
            columns = slice(third * width, (third + 1) * width)
            r.mixed_grad[mol, :, columns] = r.mixed_t[third].T
    first_grad = None
    mixed_sums = []
    for third in range(3):
        columns = slice(third * width, (third + 1) * width)
        mixed = jnp.concatenate(
            [r.mixed_grad[mol, :, columns].astype(wide)[:length] for mol in mols], 0
        )
        mixed_sums.append(total(mixed))
        part = nt(mixed.astype(low), r.qkv[:, columns])
        first_grad = part if first_grad is None else first_grad + part
    normed = by_molecule(r.n1, mols)
    rstd = by_molecule(r.r1, mols)[:, :1]
    residual_grad = r.middle_grad[: len(mols) * length] + norm_back(
        first_grad * r.gains[0:1], normed, rstd
    )
    r.grad[...] = residual_grad.astype(low)
    zero = jnp.zeros((1, width), wide)
    kinds = [zero, zero]
    for i, mol in enumerate(mols):
        one = residual_grad[i * length : (i + 1) * length]
        r.grads[mol] = one.astype(low)
        laplace = r.flag(mol) == 1
        one = total(one)
        kinds[0] = kinds[0] + jnp.where(laplace, one, zero)
        kinds[1] = kinds[1] + jnp.where(laplace, zero, one)
    sums = [total(first_grad * normed), total(first_grad), mixed_sums[0], mixed_sums[2]]
    r.attn_sums[mols[0]] = jnp.concatenate(sums + kinds + [zero, zero], 0)
    for mol in mols[1:]:
        r.attn_sums[mol] = jnp.zeros((8, width), wide)


PARAMS = ("biases", "gains", "qkv", "proj", "up", "down")
SAVED = (
    "q", "k", "v", "probs", "att_t", "n1", "r1", "n2", "r2", "slope",
    "first_in", "second_in", "activated", "outputs",
)
PIECES = ("pre_grad", "branch_grad", "dense_sums")
LATE = ("mixed_grad", "attn_sums", "grads")
CARRY = ("middle_grad", "att_grad")
SECTION, BITS, COUNTS = 0, 1, 8


class Sizes:
    def __init__(self, mols, length, width, hidden, most):
        self.mols, self.length, self.width, self.hidden, self.most = mols, length, width, hidden, most
        self.padded = length + -length % LANES

    def shapes(self, group=1):
        m, n, d, f, p = self.mols, self.length, self.width, self.hidden, self.padded
        most = self.most
        struct = jax.ShapeDtypeStruct
        return {
            "biases": struct((9, 1, d), wide),
            "gains": struct((2, d), wide),
            "qkv": struct((d, 3 * d), low),
            "proj": struct((d, d), low),
            "up": struct((d, f), low),
            "down": struct((f, d), low),
            "ends": struct((m * n, d), low),
            "q": struct((m, d, LANES), low),
            "k": struct((m, d, LANES), low),
            "v": struct((m, d, LANES), low),
            "probs": struct((m, PAIRS, n, 2 * LANES), low),
            "att_t": struct((m, d, LANES), low),
            "n1": struct((m, n, d), wide),
            "r1": struct((m, n, LANES), wide),
            "n2": struct((m, n, d), wide),
            "r2": struct((m, n, LANES), wide),
            "slope": struct((m, n, f), wide),
            "first_in": struct((m, p, d), low),
            "second_in": struct((m, p, d), low),
            "activated": struct((m, p, f), low),
            "outputs": struct((m, n, d), low),
            "out_grad": struct((m, p, d), low),
            "pre_grad": struct((m, p, f), low),
            "branch_grad": struct((m, p, d), low),
            "dense_sums": struct((m, 8, d), wide),
            "mixed_grad": struct((m, p, 3 * d), low),
            "attn_sums": struct((m, 8, d), wide),
            "grads": struct((m, n, d), low),
            "middle_grad": struct((most * n, d), wide),
            "att_grad": struct((most, d, LANES), low),
            "result": struct((group * n, d), low),
            "grad": struct((group * n, d), low),
            "residual": struct((most * n, d), wide),
            "scores": struct((PAIRS, n, 2 * LANES), wide),
            "score_grad": struct((PAIRS, n, 2 * LANES), low),
            "mixed_t": struct((3, d, LANES), low),
            "left_t": struct((2, d, m * p), low),
        }


TIMES = {
    "first": 3.0, "tick_0": 0.2, "tick_1": 0.2, "tick_2": 1.0, "hidden": 100,
    "middle": 100, "attention": 100, "qk": 10, "v": 100, "halve_hidden_1": 100, "halve_hidden_2": 20,
    "halve_hidden_3": 20, "halve_middle_1": 100, "halve_middle_2": 100, "halve_middle_3": 1, "halve_qk_1": 2,
    "halve_qk_2": 0.3, "halve_qk_3": 20, "halve_v_1": 1, "halve_v_2": 10, "halve_v_3": 20,
    "finish_hidden": 0.02, "finish_middle": 5, "finish_qk": 100, "finish_v": 1,
}


def cost(name):
    micros = TIMES.get(name) or TIMES.get(name.split("_")[0], 1.0)
    return pl.CostEstimate(
        flops=int(micros * 0.2 * 1.15e9), bytes_accessed=1, transcendentals=0
    )


ROOM = {"tick": 8, "attention": 8, "first": 6, "halve": 2}


def settings(name):
    room = next((size for start, size in ROOM.items() if name.startswith(start)), 4)
    return pltpu.CompilerParams(vmem_limit_bytes=room << 20)


def call(body, shapes, ins, kept, fresh, scratch, name, specs=None, after=()):
    ins = ins | {f"after_{i}": array for i, array in enumerate(after)}
    given = [n for n in kept if kept[n] is not None]
    names = list(ins) + ["_" + n for n in given] + list(kept) + list(fresh)
    extra = [n for n in scratch if not isinstance(n, str)]
    named = [n for n in scratch if isinstance(n, str)]
    operands = list(ins.values()) + [kept[n] for n in given]
    aliases = {len(ins) + i: list(kept).index(n) for i, n in enumerate(given)}
    in_spec = {"info": SMEM} | (specs or {}) | {f"after_{i}": ANY for i in range(len(after))}

    def kernel(*refs):
        r = Refs(names + named + [n for n, _ in extra], refs)
        body(r)

    outs = pl.pallas_call(
        kernel,
        name=name,
        out_shape=[pltpu.VMEM(shapes[n].shape, shapes[n].dtype) for n in list(kept) + list(fresh)],
        in_specs=[in_spec.get(n, VMEM) for n in ins] + [VMEM] * len(given),
        out_specs=[VMEM] * (len(kept) + len(fresh)),
        scratch_shapes=[pltpu.VMEM(shapes[n].shape, shapes[n].dtype) for n in named]
        + [shape for _, shape in extra],
        input_output_aliases=aliases,
        compiler_params=settings(name),
        cost_estimate=cost(name),
    )(*operands)
    return dict(zip(list(kept) + list(fresh), outs, strict=True))


def weight_product(r, slot, left, right, targets, position, owners, core):
    mols, tokens, _ = right.shape
    width = left.shape[1] if slot is None else left.shape[2]
    rows = width // owners
    if slot is not None:
        r.left_t[slot] = left[...].reshape(mols * tokens, width).T
    for target, parity in zip(targets, (1 - core, core)):
        blocks = [block_rows(o, parity, rows) for o in range(owners // 2)]
        if slot is None:
            parts = [jnp.concatenate([left[m, at] for at in blocks], 0) for m in range(mols)]
            own = jnp.concatenate(parts, 1)
        else:
            own = jnp.concatenate([r.left_t[slot, at] for at in blocks], 0)
        for base in range(0, right.shape[2], 256):
            part = right[:, :, base : base + 256].reshape(mols * tokens, 256)
            out = nn(own, part).astype(low)
            target[:, :, position + base : position + base + 256] = out.reshape(
                owners // 2, rows, 256
            )


def block_rows(pair, parity, rows):
    return pl.ds(pl.multiple_of((2 * pair + parity) * rows, 16), rows)


def sum_table(r, targets, position, owners, core):
    both = jnp.concatenate([jnp.sum(r.dense_sums[...], 0), jnp.sum(r.attn_sums[...], 0)], 0)
    width = both.shape[1]
    rows = width // owners
    high = both.astype(low).astype(wide)
    zeros = jnp.zeros((LANES - 32, width), wide)
    r.table[...] = jnp.concatenate([high, both - high, zeros], 0).T.astype(low)
    for target, parity in zip(targets, (1 - core, core)):
        for o in range(owners // 2):
            target[o, :, position : position + LANES] = r.table[block_rows(o, parity, rows)]


def swap(block, bit):
    devices = lax.axis_size("dp")
    return lax.ppermute(block, "dp", [(i, i ^ bit) for i in range(devices)])


def halve(info, keep, received, bit, name, after):
    count, rows, columns = keep.shape

    def kernel(info, keep, received, after, send, own):
        mine = info[BITS + bit]
        for j in range(count // 2):
            for target, index in ((send, 2 * j + 1 - mine), (own, 2 * j + mine)):
                target[j] = (keep[index].astype(wide) + received[index].astype(wide)).astype(low)

    shape = pltpu.VMEM((count // 2, rows, columns), low)
    return pl.pallas_call(
        kernel,
        name=name,
        out_shape=[shape, shape],
        in_specs=[SMEM, VMEM, VMEM, ANY],
        out_specs=[VMEM, VMEM],
        compiler_params=settings(name),
        cost_estimate=cost(name),
    )(info, keep, received, after)


class Scatter:
    def __init__(self, info, keep, send, name):
        self.info, self.keep, self.name, self.bit = info, keep, name, 0
        self.received = swap(send, 1)

    def step(self, after):
        self.bit += 1
        name = f"halve_{self.name}_{self.bit}"
        send, self.keep = halve(self.info, self.keep, self.received, self.bit, name, after)
        self.received = swap(send, 1 << self.bit)
        return send

    def finish(self, after, cuts):
        rows = self.keep.shape[1]

        def kernel(keep, received, after, *outs):
            start = 0
            for cut, out in zip(cuts, outs, strict=True):
                stop = start + (cut or LANES)
                at = slice(start, stop)
                part = keep[0, :, at].astype(wide) + received[0, :, at].astype(wide)
                if cut:
                    out[...] = part
                else:
                    out[...] = part.T[:16] + part.T[16:32]
                start = stop

        shapes = [(rows, cut) if cut else (16, rows) for cut in cuts]
        name = f"finish_{self.name}"
        return pl.pallas_call(
            kernel,
            name=name,
            out_shape=[jax.ShapeDtypeStruct(shape, wide) for shape in shapes],
            in_specs=[VMEM, VMEM, ANY],
            out_specs=[VMEM] * len(cuts),
            compiler_params=settings(name),
            cost_estimate=cost(name),
        )(self.keep, self.received, after)


def weight_sums(sizes, lefts, rights, extra):
    tokens = sizes.mols * sizes.padded
    parts = []
    if extra:
        both = jnp.concatenate([jnp.sum(e, 0) for e in extra], 0)
        parts.append(jnp.pad(both, ((0, LANES - 16), (0, 0))).T)
    for left, right in zip(lefts, rights, strict=True):
        parts.append(tn(left.reshape(tokens, -1), right.reshape(tokens, -1)))
    whole = jnp.concatenate(parts, 1)
    return lax.psum_scatter(whole, "dp", scatter_dimension=0, tiled=True)


def groups_of(mols):
    half = (mols + 1) // 2
    return [g for g in (list(range(half)), list(range(half, mols))) if g]


def body(
    boundary, counts, id_flags, norm_gains, biases, qkv_weight, proj_weight, up_weight, down_weight
):
    mols = counts.shape[0]
    width = boundary.shape[2]
    length = boundary.shape[1] // mols
    groups = groups_of(mols)
    sizes = Sizes(mols, length, width, up_weight.shape[2], max(len(g) for g in groups))
    devices = lax.axis_size("dp")
    index = lax.axis_index("dp")
    assert devices.bit_length() <= COUNTS
    info = jnp.concatenate(
        [
            lax.axis_index("section")[None],
            (index >> jnp.arange(COUNTS - BITS)) & 1,
            counts,
            id_flags,
        ]
    ).astype(jnp.int32)
    state = {}

    def kept(names):
        return {n: state.get(n) for n in names}

    loads = {
        "ends": boundary[0],
        "biases": jnp.transpose(biases, (1, 0, 2)),
        "gains": norm_gains[0],
        "qkv": qkv_weight[0],
        "proj": proj_weight[0],
        "up": up_weight[0],
        "down": down_weight[0],
    }
    hbm = pl.BlockSpec(memory_space=pltpu.HBM)
    forward_arrays = ("ends", "biases", "gains", "qkv", "proj", "up", "down")
    backward_arrays = ("gains", "qkv", "proj", "up", "down")

    def first_forward(group, load):
        def copies_of(r):
            parts = []
            start = 0
            for n in loads:
                source, target = getattr(r, n + "_in"), getattr(r, n)
                if n == "ends":
                    stop = -(-(group[-1] + 1) * length // 16) * 16
                    parts.append(("ends", source.at[:stop], target.at[:stop]))
                    rest = (source.at[stop:], target.at[stop:])
                elif n == "qkv":
                    for third in range(3):
                        at = slice(third * width, (third + 1) * width)
                        parts.append((f"qkv_{third}", source.at[:, at], target.at[:, at]))
                else:
                    parts.append((n, source, target))
            if rest[0].shape[0]:
                parts.append(("rest", *rest))
            return {
                n: pltpu.make_async_copy(source, target, r.sems.at[i])
                for i, (n, source, target) in enumerate(parts)
            }

        def run(r):
            copies = copies_of(r) if load else {}
            if load:
                scalars = (
                    pltpu.make_async_copy(r.counts_in, r.counts, r.scalar_sems.at[0]),
                    pltpu.make_async_copy(r.flags_in, r.flags, r.scalar_sems.at[1]),
                )
                for copy in (*scalars, *copies.values()):
                    copy.start()
                for copy in scalars:
                    copy.wait()
                r.count = lambda mol: r.counts[mol]
                r.flag = lambda mol: r.flags[mol]
                section = r.info[SECTION]
            else:
                section = r.info[SECTION]

            def wait(n):
                if load:
                    copies[n].wait()

            @pl.when(section == 0)
            def _():
                wait("ends")
                forward(r, group, molecule_rows(r.ends, group, length), length, wait)
                if "rest" in copies:
                    wait("rest")

            if load:

                @pl.when(section != 0)
                def _():
                    for n in copies:
                        wait(n)

        ins = {}
        specs = {}
        names = SAVED
        scratch = ["residual", "scores"]
        if load:
            for n in loads:
                ins[n + "_in"] = pltpu.with_memory_space_constraint(loads[n], pltpu.HBM)
            ins["counts_in"] = pltpu.with_memory_space_constraint(counts, pltpu.HBM)
            ins["flags_in"] = pltpu.with_memory_space_constraint(id_flags, pltpu.HBM)
            specs = {n: hbm for n in ins} | {"section": SMEM}
            ins["info"] = info
            names = tuple(loads) + SAVED
            scratch.append(("counts", pltpu.SMEM((mols,), jnp.int32)))
            scratch.append(("flags", pltpu.SMEM((mols,), jnp.int32)))
            scratch.append(("sems", pltpu.SemaphoreType.DMA((len(loads) + 3,))))
            scratch.append(("scalar_sems", pltpu.SemaphoreType.DMA((2,))))
        else:
            ins["info"] = info
            ins.update({n: state[n] for n in forward_arrays})
        out = call(
            run,
            sizes.shapes(len(group)),
            ins,
            kept(names),
            ["result"],
            scratch,
            f"first_{group[0]}",
            specs,
        )
        result = out.pop("result")
        state.update(out)
        return result

    def tick(second, first, received, received_grad, name):
        ins = {"info": info} | {n: state[n] for n in backward_arrays}
        if second:
            ins.update({n: state[n] for n in forward_arrays})
            ins["received"] = received
        if first:
            ins["received_grad"] = received_grad

        def run(r):
            if second:

                @pl.when(r.info[SECTION] == 1)
                def _():
                    forward(r, second, r.received[...].astype(wide), length)
                    out_grad = molecule_rows(r.ends, second, length)
                    save_cotangent(r, second, out_grad, length)
                    backward_hidden(r, second, out_grad, length)
                    backward_middle(r, second, out_grad, length)
                    backward_attention(r, second, length)

            if first:

                @pl.when(r.info[SECTION] == 0)
                def _():
                    r.grad = r.first_grad
                    out_grad = r.received_grad[...].astype(wide)
                    save_cotangent(r, first, out_grad, length)
                    backward_hidden(r, first, out_grad, length)
                    backward_middle(r, first, out_grad, length)
                    backward_attention(r, first, length)

        shapes = sizes.shapes(len(second or first))
        if second:
            names = SAVED
        else:
            names = ()
            ins.update({n: state[n] for n in SAVED})
        scratch = ["residual", "scores", "score_grad", "mixed_t", "middle_grad", "att_grad"]
        if first:
            scratch.append(("first_grad", pltpu.VMEM((len(first) * length, width), low)))
        if second:
            scratch.append(("result", pltpu.VMEM((len(second) * length, width), low)))
        out = call(
            run,
            shapes,
            ins,
            kept(names + ("out_grad",) + PIECES + LATE),
            ["grad"],
            scratch,
            name,
        )
        grad = out.pop("grad")
        state.update(out)
        return grad

    forward_hops = []
    for i, group in enumerate(groups):
        result = first_forward(group, i == 0)
        forward_hops.append(lax.ppermute(result, "section", [(0, 1)]))
    grad_hops = []
    for step in range(len(groups) + 1):
        second = groups[step] if step < len(groups) else None
        first = groups[step - 2] if step >= 2 else None
        if not (second or first):
            continue
        grad = tick(
            second,
            first,
            forward_hops[step] if second else None,
            grad_hops[step - 2] if first else None,
            f"tick_{step}",
        )
        if second:
            grad_hops.append(lax.ppermute(grad, "section", [(1, 0)]))

    last = groups[-1]
    rows = width // devices
    in_kernel = rows % 16 == 0
    shapes = sizes.shapes(len(last))

    def chunk(columns):
        shape = jax.ShapeDtypeStruct((devices // 2, rows, columns), low)
        return {"send": shape, "keep": shape}

    def product(r, slot, left, right, position):
        weight_product(r, slot, left, right, (r.send, r.keep), position, devices, r.info[BITS])

    def last_hidden(r):
        @pl.when(r.info[SECTION] == 0)
        def _():
            out_grad = r.received_grad[...].astype(wide)
            save_cotangent(r, last, out_grad, length)
            backward_hidden(r, last, out_grad, length)

        if in_kernel:
            product(r, 0, r.activated, r.out_grad, 0)
            product(r, 1, r.second_in, r.pre_grad, width)

    def last_middle(r):
        @pl.when(r.info[SECTION] == 0)
        def _():
            backward_middle(r, last, r.received_grad[...].astype(wide), length)

        if in_kernel:
            product(r, None, r.att_t, r.branch_grad, 0)

    def last_attention(r):
        @pl.when(r.info[SECTION] == 0)
        def _():
            backward_attention(r, last, length)

    def qk_weight(r):
        product(r, 0, r.first_in, r.mixed_grad.at[:, :, : 2 * width], 0)

    def v_weight(r):
        product(r, 0, r.first_in, r.mixed_grad.at[:, :, 2 * width :], 0)
        sum_table(r, (r.send, r.keep), width, devices, r.info[BITS])

    fresh = ["send", "keep"] if in_kernel else []
    order = []

    def run(body, columns, ins, kept_names, made, scratch, name):
        out = call(
            body,
            shapes | chunk(columns),
            {"info": info} | {n: state[n] for n in ins},
            kept(kept_names),
            made,
            scratch,
            name,
            after=order[-1:],
        )
        state.update({n: out[n] for n in list(kept_names) + list(made)})
        order.append(out["send"] if "send" in out else next(iter(out.values())))
        if "send" in out:
            scatters[name] = Scatter(info, out["keep"], out["send"], name)

    state["received_grad"] = grad_hops[-1]
    kernels = {
        "hidden": lambda: run(
            last_hidden,
            width + sizes.hidden,
            ("received_grad", "activated", "second_in", "slope", "down"),
            ("out_grad", "pre_grad"),
            fresh,
            ["left_t"],
            "hidden",
        ),
        "middle": lambda: run(
            last_middle,
            width,
            ("received_grad", "gains", "proj", "up", "n2", "r2", "pre_grad", "att_t"),
            ("branch_grad", "dense_sums"),
            list(CARRY) + fresh,
            [],
            "middle",
        ),
        "attention": lambda: run(
            last_attention,
            width,
            ("gains", "qkv", "q", "k", "v", "probs", "att_t", "n1", "r1", *CARRY),
            LATE,
            ["grad"],
            ["scores", "score_grad", "mixed_t"],
            "attention",
        ),
        "qk": lambda: run(
            qk_weight, 2 * width, ("first_in", "mixed_grad"), (), fresh, ["left_t"], "qk"
        ),
        "v": lambda: run(
            v_weight,
            width + LANES,
            ("first_in", "mixed_grad", "dense_sums", "attn_sums"),
            (),
            fresh,
            ["left_t", ("table", pltpu.VMEM((width, LANES), low))],
            "v",
        ),
    }
    scatters, finished = {}, {}
    for step in TAIL:
        if step in kernels:
            if in_kernel or step in ("hidden", "middle", "attention"):
                kernels[step]()
        elif in_kernel and step[-1] == "4":
            name = step[:-1]
            finished[name] = scatters[name].finish(order[-1], CUTS[name](width, sizes.hidden))
            order.append(finished[name][0])
        elif in_kernel:
            order.append(scatters[step[:-1]].step(order[-1]))
    if in_kernel:
        down_grad, up_grad = finished["hidden"]
        (proj_grad,) = finished["middle"]
        (qk_grad,) = finished["qk"]
        v_grad, vectors = finished["v"]
        qkv_grad = jnp.concatenate([qk_grad, v_grad], 1)
    else:
        left = [state[n] for n in ("second_in", "activated", "att_t", "first_in")]
        left[2] = jnp.swapaxes(left[2], 1, 2)
        right = [state[n] for n in ("pre_grad", "out_grad", "branch_grad", "mixed_grad")]
        whole = weight_sums(sizes, left, right, [state["dense_sums"], state["attn_sums"]])
        ends = [LANES, sizes.hidden, width, width, 3 * width]
        cuts = [sum(ends[:i]) for i in range(1, 5)]
        table, up_grad, down_grad, proj_grad, qkv_grad = jnp.split(whole, cuts, 1)
        vectors = table.T
    gain_grad = jnp.stack([vectors[8], vectors[0]])
    bias_grad = jnp.stack([vectors[i] for i in (9, 10, 11, 4, 1, 2, 3, 12, 13)])
    return (
        state["outputs"].reshape(boundary.shape),
        state["grads"].reshape(boundary.shape),
        qkv_grad[None],
        proj_grad[None],
        up_grad[None],
        down_grad[None],
        gain_grad[None],
        bias_grad[None],
    )


def solution(mesh):
    placed = (
        P("section", "dp", None),
        P("dp"),
        P("dp"),
        P("section", None, None),
        P("section", None, None),
        P("section", None, None),
        P("section", None, None),
        P("section", None, None),
        P("section", None, None),
    )
    return jax.shard_map(
        body,
        mesh=mesh,
        in_specs=placed,
        out_specs=(
            P("section", "dp", None),
            P("section", "dp", None),
            P("section", "dp", None),
            P("section", "dp", None),
            P("section", "dp", None),
            P("section", "dp", None),
            P("section", None, "dp"),
            P("section", None, "dp"),
        ),
        check_vma=False,
    )
```

```python
import math

import jax
import jax.numpy as jnp
from jax import lax
from jax.experimental import pallas as pl
from jax.experimental.pallas import tpu as pltpu
from jax.sharding import PartitionSpec as P

HEADS = 32
HEAD_DIM = 24
PAIRS = HEADS // 2
PAIR_ROWS = 2 * HEAD_DIM
LANES = 128
EPSILON = 1e-05
SCALE = 1.0 / math.sqrt(HEAD_DIM)
LOG2E = math.log2(math.e)

low = jnp.bfloat16
wide = jnp.float32

VMEM = pl.BlockSpec(memory_space=pltpu.VMEM)
SMEM = pl.BlockSpec(memory_space=pltpu.SMEM)
HBM = pl.BlockSpec(memory_space=pltpu.HBM)
ANY = pl.BlockSpec(memory_space=pl.ANY)

SECTION, BITS, COUNTS = 0, 1, 8


def nn(left, right):
    return lax.dot_general(left, right, (((1,), (0,)), ((), ())), preferred_element_type=wide)


def nt(left, right):
    return lax.dot_general(left, right, (((1,), (1,)), ((), ())), preferred_element_type=wide)


def tn(left, right):
    return lax.dot_general(left, right, (((0,), (0,)), ((), ())), preferred_element_type=wide)


def pad_rows(values):
    extra = -values.shape[0] % LANES
    return jnp.concatenate([values, jnp.zeros((extra, values.shape[1]), values.dtype)], 0)


def pair_rows(pair):
    return slice(pair * PAIR_ROWS, (pair + 1) * PAIR_ROWS)


def two_blocks(rows):
    first = lax.broadcasted_iota(jnp.int32, rows.shape, 0) < HEAD_DIM
    zeros = jnp.zeros_like(rows)
    return jnp.concatenate([jnp.where(first, rows, zeros), jnp.where(first, zeros, rows)], 1)


def own_blocks(product):
    return jnp.concatenate([product[:HEAD_DIM, :LANES], product[HEAD_DIM:, LANES:]], 0)


def normalize(values):
    centred = values - jnp.mean(values, -1, keepdims=True)
    rstd = lax.rsqrt(jnp.mean(centred * centred, -1, keepdims=True) + EPSILON)
    return centred * rstd, rstd


def norm_back(scaled, normed, rstd):
    return rstd * (
        scaled
        - jnp.mean(scaled, -1, keepdims=True)
        - normed * jnp.mean(scaled * normed, -1, keepdims=True)
    )


def total(values):
    return jnp.sum(values, 0, keepdims=True)


def staged(count, *stages):
    for step in range(count + len(stages) - 1):
        for pair in range(PAIRS):
            for behind, stage in enumerate(stages):
                if 0 <= step - behind < count:
                    stage(step - behind, pair)


PLAN = (
    "h", "m", "h1", "t", "v", "m1", "q", "v1", "k", "h2", "k1", "m2", "v2", "q1", "h3", "k2", "v3", "q2", "m3", "k3", "h4", "q3", "v4", "m4", "k4", "q4",
)
ROUTES = ((1, 2, 3), (2, 3, 1))


class Refs:
    def __init__(self, names, refs):
        for name, ref in zip(names, refs, strict=True):
            setattr(self, name, ref)

    def count(self, mol):
        return self.info[COUNTS + mol]

    def flag(self, mol):
        return self.info[COUNTS + (self.info.shape[0] - COUNTS) // 2 + mol]


def rows_of(group, length):
    start = group[0] * length
    each = [slice(i * length, (i + 1) * length) for i in range(len(group))]
    return slice(start, start + len(group) * length), each


def no_wait(ref):
    pass


def forward(r, group, x, length, wait=no_wait):
    width = x.shape[1]
    whole, each = rows_of(group, length)
    here = slice(0, len(group) * length)

    def save(ref, values):
        for mol, at in zip(group, each):
            ref[mol] = pad_rows(values[at]).astype(low)

    wait("biases")
    kinds = [jnp.where(r.flag(mol) == 1, r.biases[7], r.biases[8]) for mol in group]
    residual = jnp.concatenate([x[at] + kind for at, kind in zip(each, kinds)], 0)
    normed, rstd = normalize(residual)
    for mol, at in zip(group, each):
        r.n1[mol] = normed[at]
        r.r1[mol] = jnp.broadcast_to(rstd[at], (length, LANES))
    r.residual[here] = residual
    wait("gains")
    first_in = normed * r.gains[0:1] + r.biases[0]
    save(r.first_in, first_in)
    first_in = first_in.astype(low)
    for third, bias in enumerate((1, None, 2)):
        wait(third)
        part = nn(first_in, r.qkv[:, third * width : (third + 1) * width])
        if bias is not None:
            part = part + r.biases[bias]
        for mol, at in zip(group, each):
            (r.q, r.k, r.v)[third][mol] = pad_rows(part[at]).astype(low).T
    key_index = lax.broadcasted_iota(jnp.int32, (length, 2 * LANES), 0)
    key_bias = [jnp.where(key_index < r.count(mol), 0.0, -1e30) for mol in group]

    def multiply(i, pair):
        at = pair_rows(pair)
        r.scores[i, pair] = tn(r.k[group[i], at, :length], two_blocks(r.q[group[i], at, :]))

    def softmax(i, pair):
        scores = r.scores[i, pair] * (SCALE * LOG2E) + key_bias[i]
        weights = jnp.exp2(scores - jnp.max(scores, 0, keepdims=True))
        weights = weights * (1.0 / jnp.sum(weights, 0, keepdims=True))
        r.probs[group[i], pair] = weights.astype(low)

    def attend(i, pair):
        at = pair_rows(pair)
        product = nn(r.v[group[i], at, :length], r.probs[group[i], pair])
        r.att_t[group[i], at, :] = own_blocks(product).astype(low)

    staged(len(group), multiply, softmax, attend)
    attended = jnp.concatenate([r.att_t[mol].T[:length].astype(wide) for mol in group], 0)
    wait("proj")
    middle = r.residual[here] + nn(attended.astype(low), r.proj[...]) + r.biases[3]
    normed, rstd = normalize(middle)
    for mol, at in zip(group, each):
        r.n2[mol] = normed[at]
        r.r2[mol] = jnp.broadcast_to(rstd[at], (length, LANES))
    r.residual[here] = middle
    second_in = normed * r.gains[1:2] + r.biases[4]
    save(r.second_in, second_in)
    wait("up")
    pre_act = nn(second_in.astype(low), r.up[...]) + r.biases[5]
    cdf = 0.5 * (1.0 + lax.erf(pre_act * math.sqrt(0.5)))
    pdf = jnp.exp(-0.5 * pre_act * pre_act) * (1.0 / math.sqrt(2.0 * math.pi))
    slope = cdf + pre_act * pdf
    for mol, at in zip(group, each):
        r.slope[mol] = slope[at]
    activated = pre_act * cdf
    save(r.activated, activated)
    wait("down")
    result = r.residual[here] + nn(activated.astype(low), r.down[...]) + r.biases[6]
    result = result.astype(low)
    r.outputs[whole] = result
    r.result[...] = result


def by_molecule(ref, group):
    return jnp.concatenate([ref[mol].astype(wide) for mol in group], 0)


def save_cotangent(r, group, out_grad, length):
    for mol, at in zip(group, rows_of(group, length)[1]):
        r.out_grad[mol] = pad_rows(out_grad[at]).astype(low)


def backward_hidden(r, group, out_grad, length):
    pre_grad = nt(out_grad.astype(low), r.down[...]) * by_molecule(r.slope, group)
    for mol, at in zip(group, rows_of(group, length)[1]):
        r.pre_grad[mol] = pad_rows(pre_grad[at]).astype(low)


def backward_middle(r, group, out_grad, length):
    each = rows_of(group, length)[1]
    pre_grad = jnp.concatenate([r.pre_grad[mol].astype(wide)[:length] for mol in group], 0)
    second_grad = nt(pre_grad.astype(low), r.up[...])
    normed = by_molecule(r.n2, group)
    rstd = by_molecule(r.r2, group)[:, :1]
    middle_grad = out_grad + norm_back(second_grad * r.gains[1:2], normed, rstd)
    r.middle_grad[: len(group) * length] = middle_grad
    branch_grad = middle_grad.astype(low)
    zeros = jnp.zeros((8, out_grad.shape[1]), wide)
    sums = [
        total(second_grad * normed),
        total(second_grad),
        total(pre_grad),
        total(out_grad),
        total(branch_grad.astype(wide)),
        zeros[:3],
    ]
    r.dense_sums[group[0]] = jnp.concatenate(sums, 0)
    for mol in group[1:]:
        r.dense_sums[mol] = zeros
    att_grad = nt(branch_grad, r.proj[...])
    for i, (mol, at) in enumerate(zip(group, each)):
        r.branch_grad[mol] = pad_rows(middle_grad[at]).astype(low)
        r.att_grad[i] = pad_rows(att_grad[at]).astype(low).T


def backward_attention(r, group, length):
    width = r.middle_grad.shape[1]
    whole, each = rows_of(group, length)
    pad = jnp.zeros((PAIR_ROWS, LANES - length), wide)
    deltas = []
    for i, mol in enumerate(group):
        products = r.att_t[mol].astype(wide) * r.att_grad[i].astype(wide)
        deltas.append(jnp.sum(products.reshape(HEADS, HEAD_DIM, LANES), 1))

    def multiply(i, pair):
        at = pair_rows(pair)
        r.scores[i, pair] = tn(r.v[group[i], at, :length], two_blocks(r.att_grad[i, at, :]))

    def through_softmax(i, pair):
        at = pair_rows(pair)
        first, second = deltas[i][2 * pair : 2 * pair + 1], deltas[i][2 * pair + 1 : 2 * pair + 2]
        probs = r.probs[group[i], pair]
        row = jnp.concatenate([first, second], 1)
        r.score_grad[i, pair] = (probs.astype(wide) * (r.scores[i, pair] - row)).astype(low)
        value = nt(two_blocks(r.att_grad[i, at, :]), probs)
        r.mixed_t[i, 2, at, :] = jnp.concatenate([value, pad], 1).astype(low)

    def to_inputs(i, pair):
        at = pair_rows(pair)
        grad = r.score_grad[i, pair]
        query = own_blocks(nn(r.k[group[i], at, :length], grad)) * SCALE
        key = nt(two_blocks(r.q[group[i], at, :]), grad) * SCALE
        r.mixed_t[i, 0, at, :] = query.astype(low)
        r.mixed_t[i, 1, at, :] = jnp.concatenate([key, pad], 1).astype(low)

    staged(len(group), multiply, through_softmax, to_inputs)
    first_grad = None
    mixed_sums = []
    for third in range(3):
        columns = slice(third * width, (third + 1) * width)
        for i, mol in enumerate(group):
            r.mixed_grad[mol, :, columns] = r.mixed_t[i, third].T
        mixed = jnp.concatenate(
            [r.mixed_grad[mol, :, columns].astype(wide)[:length] for mol in group], 0
        )
        mixed_sums.append(total(mixed))
        part = nt(mixed.astype(low), r.qkv[:, columns])
        first_grad = part if first_grad is None else first_grad + part
    normed = by_molecule(r.n1, group)
    rstd = by_molecule(r.r1, group)[:, :1]
    residual_grad = r.middle_grad[: len(group) * length] + norm_back(
        first_grad * r.gains[0:1], normed, rstd
    )
    low_grad = residual_grad.astype(low)
    r.grads[whole] = low_grad
    r.grad[...] = low_grad
    zeros = jnp.zeros((8, width), wide)
    kinds = [zeros[:1], zeros[:1]]
    for mol, at in zip(group, each):
        one = total(residual_grad[at])
        laplace = r.flag(mol) == 1
        kinds[0] = kinds[0] + jnp.where(laplace, one, zeros[:1])
        kinds[1] = kinds[1] + jnp.where(laplace, zeros[:1], one)
    sums = [total(first_grad * normed), total(first_grad), mixed_sums[0], mixed_sums[2]]
    r.attn_sums[group[0]] = jnp.concatenate(sums + kinds + [zeros[:2]], 0)
    for mol in group[1:]:
        r.attn_sums[mol] = zeros


def shapes_of(m, n, d, f, most, group):
    p = n + -n % LANES
    shape = jax.ShapeDtypeStruct
    return dict(
        biases=shape((9, 1, d), wide),
        gains=shape((2, d), wide),
        qkv=shape((d, 3 * d), low),
        proj=shape((d, d), low),
        up=shape((d, f), low),
        down=shape((f, d), low),
        ends=shape((m * n, d), low),
        q=shape((m, d, LANES), low),
        k=shape((m, d, LANES), low),
        v=shape((m, d, LANES), low),
        probs=shape((m, PAIRS, n, 2 * LANES), low),
        att_t=shape((m, d, LANES), low),
        n1=shape((m, n, d), wide),
        r1=shape((m, n, LANES), wide),
        n2=shape((m, n, d), wide),
        r2=shape((m, n, LANES), wide),
        slope=shape((m, n, f), wide),
        first_in=shape((m, p, d), low),
        second_in=shape((m, p, d), low),
        activated=shape((m, p, f), low),
        outputs=shape((m * n, d), low),
        out_grad=shape((m, p, d), low),
        pre_grad=shape((m, p, f), low),
        branch_grad=shape((m, p, d), low),
        dense_sums=shape((m, 8, d), wide),
        mixed_grad=shape((m, p, 3 * d), low),
        attn_sums=shape((m, 8, d), wide),
        grads=shape((m * n, d), low),
        middle_grad=shape((most * n, d), wide),
        att_grad=shape((most, d, LANES), low),
        result=shape((group * n, d), low),
        grad=shape((group * n, d), low),
        cotangent=shape((most * n, d), wide),
        residual=shape((most * n, d), wide),
        scores=shape((most, PAIRS, n, 2 * LANES), wide),
        score_grad=shape((most, PAIRS, n, 2 * LANES), low),
        mixed_t=shape((most, 3, d, LANES), low),
        left_t=shape((2, d, m * p), low),
        table=shape((d, LANES), low),
    )


def names(**given):
    return tuple(given)


LOADS = names(ends=1, biases=1, gains=1, qkv=1, proj=1, up=1, down=1)
FORWARD = LOADS
BACKWARD = names(gains=1, qkv=1, proj=1, up=1, down=1)
SAVED = names(
    q=1, k=1, v=1, probs=1, att_t=1, n1=1, r1=1, n2=1, r2=1, slope=1,
    first_in=1, second_in=1, activated=1, outputs=1,
)
HIDDEN = names(out_grad=1, pre_grad=1)
MIDDLE = names(branch_grad=1, dense_sums=1)
CARRY = names(middle_grad=1, att_grad=1)
LATE = names(mixed_grad=1, attn_sums=1, grads=1)
FORWARD_SCRATCH = names(residual=1, scores=1)
BACKWARD_SCRATCH = names(scores=1, score_grad=1, mixed_t=1)


def kernel_settings(mebibytes, micros):
    return dict(
        compiler_params=pltpu.CompilerParams(vmem_limit_bytes=mebibytes << 20),
        cost_estimate=pl.CostEstimate(
            flops=int(micros * 1.15e9), bytes_accessed=1, transcendentals=0
        ),
    )


def call(
    body, shapes, ins, kept, fresh, scratch, name, mebibytes, micros, specs=None, extra=None, after=()
):
    given = [n for n in kept if kept[n] is not None]
    made = list(kept) + list(fresh)
    extra = extra or {}
    in_specs = dict.fromkeys(ins, VMEM) | dict(info=SMEM) | (specs or {})
    first = len(ins) + len(given) + len(after)

    def kernel(*refs):
        visible = list(ins) + made + list(scratch) + list(extra)
        body(Refs(visible, refs[: len(ins)] + refs[first:]))

    outs = pl.pallas_call(
        kernel,
        name=name,
        out_shape=[pltpu.VMEM(shapes[n].shape, shapes[n].dtype) for n in made],
        in_specs=[in_specs[n] for n in ins] + [VMEM] * len(given) + [ANY] * len(after),
        out_specs=[VMEM] * len(made),
        scratch_shapes=[pltpu.VMEM(shapes[n].shape, shapes[n].dtype) for n in scratch]
        + list(extra.values()),
        input_output_aliases={len(ins) + i: made.index(n) for i, n in enumerate(given)},
        **kernel_settings(mebibytes, micros),
    )(*ins.values(), *(kept[n] for n in given), *after)
    return dict(zip(made, outs, strict=True))


def block_rows(pair, parity, rows):
    return pl.ds(pl.multiple_of((2 * pair + parity) * rows, 16), rows)


def weight_product(r, slot, left, right, position, owners):
    mols, tokens, _ = right.shape
    width = left.shape[1] if slot is None else left.shape[2]
    rows = width // owners
    core = r.info[BITS]
    if slot is not None:
        r.left_t[slot] = left[...].reshape(mols * tokens, width).T
    for target, parity in ((r.send, 1 - core), (r.keep, core)):
        blocks = [block_rows(o, parity, rows) for o in range(owners // 2)]
        if slot is None:
            parts = [jnp.concatenate([left[m, at] for at in blocks], 0) for m in range(mols)]
            own = jnp.concatenate(parts, 1)
        else:
            own = jnp.concatenate([r.left_t[slot, at] for at in blocks], 0)
        for base in range(0, right.shape[2], 256):
            part = right[:, :, base : base + 256].reshape(mols * tokens, 256)
            out = nn(own, part).astype(low)
            target[:, :, position + base : position + base + 256] = out.reshape(
                owners // 2, rows, 256
            )


def sum_table(r, position, owners):
    both = jnp.concatenate([jnp.sum(r.dense_sums[...], 0), jnp.sum(r.attn_sums[...], 0)], 0)
    width = both.shape[1]
    rows = width // owners
    core = r.info[BITS]
    high = both.astype(low).astype(wide)
    zeros = jnp.zeros((LANES - 32, width), wide)
    r.table[...] = jnp.concatenate([high, both - high, zeros], 0).T.astype(low)
    for target, parity in ((r.send, 1 - core), (r.keep, core)):
        for o in range(owners // 2):
            target[o, :, position : position + LANES] = r.table[block_rows(o, parity, rows)]


def swap(block, bit):
    devices = lax.axis_size("dp")
    return lax.ppermute(block, "dp", [(i, i ^ (1 << bit)) for i in range(devices)])


def halve(info, keep, received, bits, bit, after):
    count, rows, columns = keep.shape
    place = 1 << bits.index(bit)

    def kernel(info, keep, received, after, send, own):
        mine = info[BITS + bit]
        for j in range(count // 2):
            base = j // place * 2 * place + j % place
            for target, value in ((send, 1 - mine), (own, mine)):
                index = base + value * place
                target[j] = (keep[index].astype(wide) + received[index].astype(wide)).astype(low)

    shape = pltpu.VMEM((count // 2, rows, columns), low)
    return pl.pallas_call(
        kernel,
        name="halve",
        out_shape=[shape, shape],
        in_specs=[SMEM, VMEM, VMEM, ANY],
        out_specs=[VMEM, VMEM],
        **kernel_settings(2, 20),
    )(info, keep, received, after)


class Scatter:
    def __init__(self, info, keep, send, route):
        self.info, self.keep, self.route = info, keep, list(route)
        self.bits = sorted(route)
        self.received = swap(send, 0)

    def step(self, after):
        bit = self.route.pop(0)
        send, self.keep = halve(self.info, self.keep, self.received, self.bits, bit, after)
        self.bits.remove(bit)
        self.received = swap(send, bit)
        return send

    def finish(self, after, shapes, write, extra=()):
        def kernel(keep, received, *rest):
            others, outs = rest[: len(extra)], rest[len(extra) + 1 :]
            write(keep[0].astype(wide) + received[0].astype(wide), others, outs)

        return pl.pallas_call(
            kernel,
            name="finish",
            out_shape=[jax.ShapeDtypeStruct(shape, wide) for shape in shapes],
            in_specs=[VMEM] * (2 + len(extra)) + [ANY],
            out_specs=[VMEM] * len(shapes),
            **kernel_settings(4, 20),
        )(self.keep, self.received, *extra, after)


def write_vectors(table, gain, bias):
    vectors = table.T
    vectors = vectors[:16] + vectors[16:32]
    for i, source in enumerate((8, 0)):
        gain[i : i + 1] = vectors[source : source + 1]
    for i, source in enumerate((9, 10, 11, 4, 1, 2, 3, 12, 13)):
        bias[i] = vectors[source : source + 1]


def plain_sums(state, width, hidden):
    both = [jnp.sum(state[n], 0) for n in names(dense_sums=1, attn_sums=1)]
    parts = [jnp.pad(jnp.concatenate(both, 0), ((0, LANES - 16), (0, 0))).T]
    lefts = [state[n] for n in names(activated=1, second_in=1, first_in=1)]
    lefts.insert(2, jnp.swapaxes(state["att_t"], 1, 2))
    rights = [state[n] for n in names(out_grad=1, pre_grad=1, branch_grad=1, mixed_grad=1)]
    for left, right in zip(lefts, rights, strict=True):
        rows = left.shape[0] * left.shape[1]
        parts.append(tn(left.reshape(rows, -1), right.reshape(rows, -1)))
    sums = lax.psum_scatter(
        jnp.concatenate(parts, 1), "dp", scatter_dimension=0, tiled=True
    )
    sizes = [LANES, width, hidden, width]
    cuts = [sum(sizes[: i + 1]) for i in range(4)]
    table, down, up, proj, qkv = jnp.split(sums, cuts, 1)
    vectors = table.T
    gain = jnp.stack([vectors[8], vectors[0]])
    bias = jnp.stack([vectors[i] for i in (9, 10, 11, 4, 1, 2, 3, 12, 13)])
    return qkv, proj, up, down, gain, bias


def body(
    boundary, counts, id_flags, norm_gains, biases, qkv_weight, proj_weight, up_weight, down_weight
):
    mols = counts.shape[0]
    width = boundary.shape[2]
    hidden = up_weight.shape[2]
    length = boundary.shape[1] // mols
    half = (mols + 1) // 2
    groups = [list(range(half)), list(range(half, mols))]
    devices = lax.axis_size("dp")
    rows = width // devices
    in_kernel = rows % 16 == 0
    assert devices.bit_length() <= COUNTS
    index = lax.axis_index("dp")
    info = jnp.concatenate(
        [
            lax.axis_index("section")[None],
            (index >> jnp.arange(COUNTS - BITS)) & 1,
            counts,
            id_flags,
        ]
    ).astype(jnp.int32)
    state = {}

    def shapes(group):
        return shapes_of(mols, length, width, hidden, half, len(group))

    def take(*lists, **more):
        return {n: state[n] for n in sum(lists, ()) + tuple(more)}

    def kept(*lists):
        return {n: state.get(n) for n in sum(lists, ())}

    def put(out, *lists):
        state.update({n: out[n] for n in sum(lists, ())})

    sources = dict(
        ends=boundary[0],
        biases=jnp.transpose(biases, (1, 0, 2)),
        gains=norm_gains[0],
        qkv=qkv_weight[0],
        proj=proj_weight[0],
        up=up_weight[0],
        down=down_weight[0],
    )

    def first_forward(group, load):
        stop = rows_of(group, length)[0].stop

        def run(r):
            section = r.info[SECTION]
            pieces = {}
            if load:
                pieces["ends"] = (r.from_ends, r.ends, slice(0, stop))
                for name in names(biases=1, gains=1):
                    pieces[name] = (getattr(r, "from_" + name), getattr(r, name), ...)
                for third in range(3):
                    columns = pl.ds(third * width, width)
                    pieces[third] = (r.from_qkv, r.qkv, (slice(None), columns))
                early = list(pieces)
                for name in names(proj=1, up=1, down=1):
                    pieces[name] = (getattr(r, "from_" + name), getattr(r, name), ...)
                pieces[None] = (r.from_ends, r.ends, slice(stop, mols * length))

            def copy(key):
                source, target, at = pieces[key]
                sem = r.sems.at[list(pieces).index(key)]
                return pltpu.make_async_copy(source.at[at], target.at[at], sem)

            def wait(key):
                if load:
                    copy(key).wait()
                    if key == 0:
                        for late in pieces:
                            if late not in early:
                                copy(late).start()

            if load:
                for key in early:
                    copy(key).start()

            @pl.when(section == 0)
            def _():
                wait("ends")
                here = slice(stop - len(group) * length, stop)
                forward(r, group, r.ends[here].astype(wide), length, wait)
                wait(None)

            if load:

                @pl.when(section != 0)
                def _():
                    for key in pieces:
                        wait(key)

        ins = dict(info=info)
        kept_names = SAVED
        specs, extra = {}, {}
        if load:
            sent = {"from_" + n: sources[n] for n in LOADS}
            ins |= {n: pltpu.with_memory_space_constraint(a, pltpu.HBM) for n, a in sent.items()}
            specs = dict.fromkeys(sent, HBM)
            kept_names = LOADS + SAVED
            extra = dict(sems=pltpu.SemaphoreType.DMA((len(LOADS) + 3,)))
        else:
            ins |= take(FORWARD)
        out = call(
            run, shapes(group), ins, kept(kept_names), names(result=1), FORWARD_SCRATCH,
            "first", 8, 3.0, specs, extra,
        )
        put(out, kept_names)
        return out["result"]

    def tick(second, first, received, received_grad, micros):
        def back(r, group, out_grad):
            save_cotangent(r, group, out_grad, length)
            backward_hidden(r, group, out_grad, length)
            backward_middle(r, group, out_grad, length)
            backward_attention(r, group, length)

        def run(r):
            if second:

                @pl.when(r.info[SECTION] == 1)
                def _():
                    forward(r, second, r.received[...].astype(wide), length)
                    back(r, second, r.ends[rows_of(second, length)[0]].astype(wide))

            if first:

                @pl.when(r.info[SECTION] == 0)
                def _():
                    back(r, first, r.received_grad[...].astype(wide))

        ins = dict(info=info) | take(BACKWARD)
        changed = HIDDEN + MIDDLE + LATE
        extra = {}
        if second:
            ins |= take(FORWARD) | dict(received=received)
            changed = SAVED + changed
            extra = dict(result=pltpu.VMEM((len(second) * length, width), low))
        else:
            ins |= take(SAVED)
        if first:
            ins |= dict(received_grad=received_grad)
        out = call(
            run, shapes(second or first), ins, kept(changed), names(grad=1),
            names(residual=1) + BACKWARD_SCRATCH + CARRY, "tick", 16, micros, extra=extra,
        )
        put(out, changed)
        return out["grad"]

    hops = []
    for group in groups:
        result = first_forward(group, group is groups[0])
        hops.append(lax.ppermute(result, "section", [(0, 1)]))
    grad_hops = []
    for group, hop in zip(groups, hops):
        grad = tick(group, None, hop, None, 0.2)
        grad_hops.append(lax.ppermute(grad, "section", [(1, 0)]))
    tick(None, groups[0], None, grad_hops[0], 1.0)

    last = groups[1]
    last_grad = grad_hops[1]
    order = []

    def after():
        return order[-1:]

    def chunk(columns):
        shape = jax.ShapeDtypeStruct((devices // 2, rows, columns), low)
        return shapes(last) | dict(send=shape, keep=shape)

    def run(kernel, columns, ins, changed, made, scratch, name, mebibytes=4):
        fresh = names(send=1, keep=1) if columns and in_kernel else ()
        out = call(
            kernel, chunk(columns), dict(info=info) | ins, kept(changed), made + fresh, scratch,
            name, mebibytes, 20.0, after=after(),
        )
        put(out, changed, made)
        order.append(out["send"] if fresh else out[(changed + made)[0]])
        return out

    def scatter(out, route):
        return Scatter(info, out["keep"], out["send"], route) if in_kernel else None

    def on_first(r, *functions):
        @pl.when(r.info[SECTION] == 0)
        def _():
            for function in functions:
                function()

    def hidden_kernel(r):
        def back():
            out_grad = r.received_grad[...].astype(wide)
            save_cotangent(r, last, out_grad, length)
            backward_hidden(r, last, out_grad, length)

        on_first(r, back)
        if in_kernel:
            weight_product(r, 0, r.activated, r.out_grad, 0, devices)
            weight_product(r, 1, r.second_in, r.pre_grad, width, devices)

    def middle_kernel(r):
        on_first(r, lambda: backward_middle(r, last, r.received_grad[...].astype(wide), length))
        if in_kernel:
            weight_product(r, None, r.att_t, r.branch_grad, 0, devices)

    def attention_kernel(r):
        on_first(r, lambda: backward_attention(r, last, length))

    def part_kernel(third, with_sums):
        def kernel(r):
            columns = slice(third * width, (third + 1) * width)
            weight_product(r, 0, r.first_in, r.mixed_grad.at[:, :, columns], 0, devices)
            if with_sums:
                sum_table(r, width, devices)

        return kernel

    def part(third, with_sums=False):
        ins = take(first_in=1, mixed_grad=1)
        columns = width
        scratch = names(left_t=1)
        if with_sums:
            ins |= take(dense_sums=1, attn_sums=1)
            columns += LANES
            scratch += names(table=1)
        out = run(part_kernel(third, with_sums), columns, ins, (), (), scratch, "part")
        return scatter(out, (1, 2, 3))

    def step(*scatters):
        for one in scatters:
            order.append(one.step(order[-1]))

    def hidden_step():
        ins = take(activated=1, second_in=1, slope=1, down=1) | dict(received_grad=last_grad)
        out = run(hidden_kernel, width + hidden, ins, HIDDEN, (), names(left_t=1), "hidden")
        return scatter(out, ROUTES[0])

    def middle_step():
        ins = take(pre_grad=1, gains=1, proj=1, up=1, n2=1, r2=1, att_t=1)
        ins |= dict(received_grad=last_grad)
        out = run(middle_kernel, width, ins, MIDDLE, CARRY, (), "middle")
        return scatter(out, ROUTES[1])

    def attention_step():
        ins = take(CARRY, gains=1, qkv=1, q=1, k=1, v=1, probs=1, att_t=1, n1=1, r1=1)
        run(attention_kernel, 0, ins, LATE, names(grad=1), BACKWARD_SCRATCH, "attention", 12)

    def write_one(sums, others, outs):
        outs[0][...] = sums

    def write_two(sums, others, outs):
        outs[0][...] = sums[:, :width]
        outs[1][...] = sums[:, width:]

    def write_value(sums, others, outs):
        outs[0][...] = sums[:, :width]
        write_vectors(sums[:, width:], outs[1], outs[2])

    def write_query(sums, others, outs):
        outs[0][:, :width] = sums
        outs[0][:, width : 2 * width] = others[0][...]
        outs[0][:, 2 * width :] = others[1][...]

    def finish(one, write, *shapes, extra=()):
        outs = one.finish(order[-1], shapes, write, extra)
        order.append(outs[0])
        return outs

    one = (rows, width)
    done = {}
    kernels = dict(
        h=hidden_step, m=middle_step, t=attention_step, q=lambda: part(0), k=lambda: part(1),
        v=lambda: part(2, True),
    )
    finishes = dict(
        h=lambda: finish(done["h"], write_two, one, (rows, hidden)),
        m=lambda: finish(done["m"], write_one, one),
        k=lambda: finish(done["k"], write_one, one),
        v=lambda: finish(done["v"], write_value, one, (2, rows), (9, 1, rows)),
        q=lambda: finish(
            done["q"], write_query, (rows, 3 * width), extra=(ended["k"][0], ended["v"][0])
        ),
    )
    ended = {}
    for word in PLAN:
        if len(word) == 1:
            if in_kernel or word in "hmt":
                done[word] = kernels[word]()
        elif in_kernel and word[1] < "4":
            order.append(done[word[0]].step(order[-1]))
        elif in_kernel:
            ended[word[0]] = finishes[word[0]]()
    if in_kernel:
        down_grad, up_grad = ended["h"]
        (proj_grad,) = ended["m"]
        _, gain_grad, bias_grad = ended["v"]
        (qkv_grad,) = ended["q"]
        bias_grad = jnp.squeeze(bias_grad, 1)
    else:
        qkv_grad, proj_grad, up_grad, down_grad, gain_grad, bias_grad = plain_sums(
            state, width, hidden
        )
    return (
        state["outputs"][None],
        state["grads"][None],
        qkv_grad[None],
        proj_grad[None],
        up_grad[None],
        down_grad[None],
        gain_grad[None],
        bias_grad[None],
    )


def solution(mesh):
    rows = P("section", "dp", None)
    columns = P("section", None, "dp")
    weights = P("section", None, None)
    return jax.shard_map(
        body,
        mesh=mesh,
        in_specs=(rows, P("dp"), P("dp")) + (weights,) * 6,
        out_specs=(rows,) * 6 + (columns,) * 2,
        check_vma=False,
    )
```

```python
import math

import jax
import jax.numpy as jnp
from jax import lax
from jax.experimental import pallas as pl
from jax.experimental.pallas import tpu as pltpu
from jax.sharding import PartitionSpec as P

HEADS = 32
HEAD_DIM = 24
PAIRS = HEADS // 2
PAIR_ROWS = 2 * HEAD_DIM
LANES = 128
EPSILON = 1e-05
LAG = 4
SCALE = 1.0 / math.sqrt(HEAD_DIM)
LOG2E = math.log2(math.e)

low = jnp.bfloat16
wide = jnp.float32

VMEM = pl.BlockSpec(memory_space=pltpu.VMEM)
SMEM = pl.BlockSpec(memory_space=pltpu.SMEM)
HBM = pl.BlockSpec(memory_space=pltpu.HBM)
ANY = pl.BlockSpec(memory_space=pl.ANY)

SECTION, BITS, COUNTS = 0, 1, 8


def nn(left, right):
    return lax.dot_general(left, right, (((1,), (0,)), ((), ())), preferred_element_type=wide)


def nt(left, right):
    return lax.dot_general(left, right, (((1,), (1,)), ((), ())), preferred_element_type=wide)


def tn(left, right):
    return lax.dot_general(left, right, (((0,), (0,)), ((), ())), preferred_element_type=wide)


def pad_rows(values):
    extra = -values.shape[0] % LANES
    return jnp.concatenate([values, jnp.zeros((extra, values.shape[1]), values.dtype)], 0)


def pair_rows(pair):
    return slice(pair * PAIR_ROWS, (pair + 1) * PAIR_ROWS)


def two_blocks(rows):
    first = lax.broadcasted_iota(jnp.int32, rows.shape, 0) < HEAD_DIM
    zeros = jnp.zeros_like(rows)
    return jnp.concatenate([jnp.where(first, rows, zeros), jnp.where(first, zeros, rows)], 1)


def first_row(shape):
    return jnp.where(lax.broadcasted_iota(jnp.int32, shape, 0) == 0, 1.0, 0.0).astype(low)


def own_blocks(product):
    return jnp.concatenate([product[:HEAD_DIM, :LANES], product[HEAD_DIM:, LANES:]], 0)


def normalize(values):
    centred = values - jnp.mean(values, -1, keepdims=True)
    rstd = lax.rsqrt(jnp.mean(centred * centred, -1, keepdims=True) + EPSILON)
    return centred * rstd, rstd


def norm_back(scaled, normed, rstd):
    return rstd * (
        scaled
        - jnp.mean(scaled, -1, keepdims=True)
        - normed * jnp.mean(scaled * normed, -1, keepdims=True)
    )


def total(values):
    return jnp.sum(values, 0, keepdims=True)


def staged(count, *stages):
    items = [(i, pair) for i in range(count) for pair in range(PAIRS)]
    for step in range(len(items) + LAG * (len(stages) - 1)):
        for behind in reversed(range(len(stages))):
            if 0 <= step - LAG * behind < len(items):
                stages[behind](*items[step - LAG * behind])


PLAN = (
    "h", "m", "h1", "t", "v", "m1", "q", "v1", "k", "h2", "k1", "m2", "v2", "q1", "h3", "k2", "v3", "q2", "m3",
    "k3", "q3",
)
ROUTES = ((1, 2, 3), (2, 3, 1))


class Refs:
    def __init__(self, names, refs):
        for name, ref in zip(names, refs, strict=True):
            setattr(self, name, ref)

    def count(self, mol):
        return self.info[COUNTS + mol]

    def flag(self, mol):
        return self.info[COUNTS + (self.info.shape[0] - COUNTS) // 2 + mol]


def rows_of(group, length):
    start = group[0] * length
    each = [slice(i * length, (i + 1) * length) for i in range(len(group))]
    return slice(start, start + len(group) * length), each


def no_wait(ref):
    pass


def forward(r, group, x, length, wait=no_wait):
    width = x.shape[1]
    whole, each = rows_of(group, length)
    here = slice(0, len(group) * length)

    def save(ref, values):
        for mol, at in zip(group, each):
            ref[mol] = pad_rows(values[at]).astype(low)

    wait("biases")
    kinds = [jnp.where(r.flag(mol) == 1, r.biases[7], r.biases[8]) for mol in group]
    residual = jnp.concatenate([x[at] + kind for at, kind in zip(each, kinds)], 0)
    normed, rstd = normalize(residual)
    for mol, at in zip(group, each):
        r.n1[mol] = normed[at]
        r.r1[mol] = jnp.broadcast_to(rstd[at], (length, LANES))
    r.residual[here] = residual
    wait("gains")
    first_in = normed * r.gains[0:1] + r.biases[0]
    save(r.first_in, first_in)
    first_in = first_in.astype(low)
    for third, bias in enumerate((1, None, 2)):
        wait(third)
        part = nn(first_in, r.qkv[:, third * width : (third + 1) * width])
        if bias is not None:
            part = part + r.biases[bias]
        for mol, at in zip(group, each):
            (r.q, r.k, r.v)[third][mol] = pad_rows(part[at]).astype(low).T
    one = first_row((16, 2 * LANES))
    masks = [
        jnp.where(lax.broadcasted_iota(jnp.int32, (16, length), 1) < r.count(mol), 0.0, -1e30)
        for mol in group
    ]
    masks = [jnp.where(first_row(mask.shape) > 0, mask, 0.0).astype(low) for mask in masks]

    def multiply(i, pair):
        at = pair_rows(pair)
        keys = jnp.concatenate([r.k[group[i], at, :length], masks[i]], 0)
        queries = jnp.concatenate([two_blocks(r.q[group[i], at, :]), one], 0)
        r.scores[i, pair] = tn(keys, queries)

    def softmax(i, pair):
        scores = r.scores[i, pair]
        weights = jnp.exp2((scores - jnp.max(scores, 0, keepdims=True)) * (SCALE * LOG2E))
        r.probs[group[i], pair] = weights.astype(low)

    def attend(i, pair):
        at = pair_rows(pair)
        values = jnp.concatenate([r.v[group[i], at, :length], one[:, :length]], 0)
        product = nn(values, r.probs[group[i], pair])
        inverse = 1.0 / product[PAIR_ROWS : PAIR_ROWS + 1]
        r.inverse[group[i], pair : pair + 1] = inverse
        r.att_t[group[i], at, :] = own_blocks(product[:PAIR_ROWS] * inverse).astype(low)

    staged(len(group), multiply, softmax, attend)
    attended = jnp.concatenate([r.att_t[mol].T[:length].astype(wide) for mol in group], 0)
    wait("proj")
    middle = r.residual[here] + nn(attended.astype(low), r.proj[...]) + r.biases[3]
    normed, rstd = normalize(middle)
    for mol, at in zip(group, each):
        r.n2[mol] = normed[at]
        r.r2[mol] = jnp.broadcast_to(rstd[at], (length, LANES))
    r.residual[here] = middle
    second_in = normed * r.gains[1:2] + r.biases[4]
    save(r.second_in, second_in)
    wait("up")
    pre_act = nn(second_in.astype(low), r.up[...]) + r.biases[5]
    cdf = 0.5 * (1.0 + lax.erf(pre_act * math.sqrt(0.5)))
    pdf = jnp.exp(-0.5 * pre_act * pre_act) * (1.0 / math.sqrt(2.0 * math.pi))
    slope = cdf + pre_act * pdf
    for mol, at in zip(group, each):
        r.slope[mol] = slope[at]
    activated = pre_act * cdf
    save(r.activated, activated)
    wait("down")
    result = r.residual[here] + nn(activated.astype(low), r.down[...]) + r.biases[6]
    result = result.astype(low)
    r.outputs[whole] = result
    r.result[...] = result


def by_molecule(ref, group):
    return jnp.concatenate([ref[mol].astype(wide) for mol in group], 0)


def save_cotangent(r, group, out_grad, length):
    for mol, at in zip(group, rows_of(group, length)[1]):
        r.out_grad[mol] = pad_rows(out_grad[at]).astype(low)


def backward_hidden(r, group, out_grad, length):
    pre_grad = nt(out_grad.astype(low), r.down[...]) * by_molecule(r.slope, group)
    for mol, at in zip(group, rows_of(group, length)[1]):
        r.pre_grad[mol] = pad_rows(pre_grad[at]).astype(low)


def backward_middle(r, group, out_grad, length):
    each = rows_of(group, length)[1]
    pre_grad = jnp.concatenate([r.pre_grad[mol].astype(wide)[:length] for mol in group], 0)
    second_grad = nt(pre_grad.astype(low), r.up[...])
    normed = by_molecule(r.n2, group)
    rstd = by_molecule(r.r2, group)[:, :1]
    middle_grad = out_grad + norm_back(second_grad * r.gains[1:2], normed, rstd)
    r.middle_grad[: len(group) * length] = middle_grad
    branch_grad = middle_grad.astype(low)
    zeros = jnp.zeros((8, out_grad.shape[1]), wide)
    sums = [
        total(second_grad * normed),
        total(second_grad),
        total(pre_grad),
        total(out_grad),
        total(branch_grad.astype(wide)),
        zeros[:3],
    ]
    r.dense_sums[group[0]] = jnp.concatenate(sums, 0)
    for mol in group[1:]:
        r.dense_sums[mol] = zeros
    att_grad = nt(branch_grad, r.proj[...])
    for i, (mol, at) in enumerate(zip(group, each)):
        r.branch_grad[mol] = pad_rows(middle_grad[at]).astype(low)
        r.att_grad[i] = pad_rows(att_grad[at]).astype(low).T


def backward_attention(r, group, length):
    width = r.middle_grad.shape[1]
    whole, each = rows_of(group, length)
    pad = jnp.zeros((PAIR_ROWS, LANES - length), wide)
    deltas = {}

    def multiply(i, pair):
        at = pair_rows(pair)
        inverse = r.inverse[group[i], pair : pair + 1]
        heads = [
            jnp.broadcast_to(inverse[:, half : half + LANES], (HEAD_DIM, LANES))
            for half in (0, LANES)
        ]
        grad = (r.att_grad[i, at, :].astype(wide) * jnp.concatenate(heads, 0)).astype(low)
        r.att_grad[i, at, :] = grad
        product = r.att_t[group[i], at, :].astype(wide) * grad.astype(wide)
        deltas[i, pair] = jnp.concatenate([total(product[:HEAD_DIM]), total(product[HEAD_DIM:])], 1)
        r.scores[i, pair] = tn(r.v[group[i], at, :length], two_blocks(grad))

    def through_softmax(i, pair):
        at = pair_rows(pair)
        probs = r.probs[group[i], pair]
        grad = probs.astype(wide) * (r.scores[i, pair] - deltas.pop((i, pair)))
        r.score_grad[i, pair] = grad.astype(low)
        value = nt(two_blocks(r.att_grad[i, at, :]), probs)
        r.mixed_t[i, 2, at, :] = jnp.concatenate([value, pad], 1).astype(low)

    def to_inputs(i, pair):
        at = pair_rows(pair)
        grad = r.score_grad[i, pair]
        query = own_blocks(nn(r.k[group[i], at, :length], grad)) * SCALE
        key = nt(two_blocks(r.q[group[i], at, :]), grad) * SCALE
        r.mixed_t[i, 0, at, :] = query.astype(low)
        r.mixed_t[i, 1, at, :] = jnp.concatenate([key, pad], 1).astype(low)

    staged(len(group), multiply, through_softmax, to_inputs)
    first_grad = None
    mixed_sums = []
    for third in range(3):
        columns = slice(third * width, (third + 1) * width)
        for i, mol in enumerate(group):
            r.mixed_grad[mol, :, columns] = r.mixed_t[i, third].T
        mixed = jnp.concatenate(
            [r.mixed_grad[mol, :, columns].astype(wide)[:length] for mol in group], 0
        )
        mixed_sums.append(total(mixed))
        part = nt(mixed.astype(low), r.qkv[:, columns])
        first_grad = part if first_grad is None else first_grad + part
    normed = by_molecule(r.n1, group)
    rstd = by_molecule(r.r1, group)[:, :1]
    residual_grad = r.middle_grad[: len(group) * length] + norm_back(
        first_grad * r.gains[0:1], normed, rstd
    )
    low_grad = residual_grad.astype(low)
    r.grads[whole] = low_grad
    r.grad[...] = low_grad
    zeros = jnp.zeros((8, width), wide)
    kinds = [zeros[:1], zeros[:1]]
    for mol, at in zip(group, each):
        one = total(residual_grad[at])
        laplace = r.flag(mol) == 1
        kinds[0] = kinds[0] + jnp.where(laplace, one, zeros[:1])
        kinds[1] = kinds[1] + jnp.where(laplace, zeros[:1], one)
    sums = [total(first_grad * normed), total(first_grad), mixed_sums[0], mixed_sums[2]]
    r.attn_sums[group[0]] = jnp.concatenate(sums + kinds + [zeros[:2]], 0)
    for mol in group[1:]:
        r.attn_sums[mol] = zeros


def shapes_of(m, n, d, f, most, group):
    p = n + -n % LANES
    shape = jax.ShapeDtypeStruct
    return dict(
        biases=shape((9, 1, d), wide),
        gains=shape((2, d), wide),
        qkv=shape((d, 3 * d), low),
        proj=shape((d, d), low),
        up=shape((d, f), low),
        down=shape((f, d), low),
        ends=shape((m * n, d), low),
        q=shape((m, d, LANES), low),
        k=shape((m, d, LANES), low),
        v=shape((m, d, LANES), low),
        probs=shape((m, PAIRS, n, 2 * LANES), low),
        inverse=shape((m, PAIRS, 2 * LANES), wide),
        att_t=shape((m, d, LANES), low),
        n1=shape((m, n, d), wide),
        r1=shape((m, n, LANES), wide),
        n2=shape((m, n, d), wide),
        r2=shape((m, n, LANES), wide),
        slope=shape((m, n, f), wide),
        first_in=shape((m, p, d), low),
        second_in=shape((m, p, d), low),
        activated=shape((m, p, f), low),
        outputs=shape((m * n, d), low),
        out_grad=shape((m, p, d), low),
        pre_grad=shape((m, p, f), low),
        branch_grad=shape((m, p, d), low),
        dense_sums=shape((m, 8, d), wide),
        mixed_grad=shape((m, p, 3 * d), low),
        attn_sums=shape((m, 8, d), wide),
        grads=shape((m * n, d), low),
        middle_grad=shape((most * n, d), wide),
        att_grad=shape((most, d, LANES), low),
        result=shape((group * n, d), low),
        grad=shape((group * n, d), low),
        far_outputs=shape((m * n, d), low),
        far_grads=shape((m * n, d), low),
        first_t=shape((d, m * p), low),
        second_t=shape((d, m * p), low),
        active_t=shape((f, m * p), low),
        cotangent=shape((most * n, d), wide),
        residual=shape((most * n, d), wide),
        scores=shape((most, PAIRS, n, 2 * LANES), wide),
        score_grad=shape((most, PAIRS, n, 2 * LANES), low),
        mixed_t=shape((most, 3, d, LANES), low),
        table=shape((d, LANES), low),
    )


def names(**given):
    return tuple(given)


LOADS = names(ends=1, biases=1, gains=1, qkv=1, proj=1, up=1, down=1)
FORWARD = LOADS
BACKWARD = names(gains=1, qkv=1, proj=1, up=1, down=1)
SAVED = names(
    q=1, k=1, v=1, probs=1, inverse=1, att_t=1, n1=1, r1=1, n2=1, r2=1, slope=1,
    first_in=1, second_in=1, activated=1, outputs=1,
)
HIDDEN = names(out_grad=1, pre_grad=1)
MIDDLE = names(branch_grad=1, dense_sums=1)
FAR = names(far_outputs=1, far_grads=1)
CARRY = names(middle_grad=1, att_grad=1)
LATE = names(mixed_grad=1, attn_sums=1, grads=1)
FORWARD_SCRATCH = names(residual=1, scores=1)
BACKWARD_SCRATCH = names(scores=1, score_grad=1, mixed_t=1)


def kernel_settings(mebibytes, micros):
    return dict(
        compiler_params=pltpu.CompilerParams(vmem_limit_bytes=mebibytes << 20),
        cost_estimate=pl.CostEstimate(
            flops=int(micros * 1.15e9), bytes_accessed=1, transcendentals=0
        ),
    )


def call(
    body, shapes, ins, kept, fresh, scratch, name, mebibytes, micros, specs=None, extra=None, after=()
):
    given = [n for n in kept if kept[n] is not None]
    made = list(kept) + list(fresh)
    extra = extra or {}
    in_specs = dict.fromkeys(ins, VMEM) | dict(info=SMEM) | (specs or {})
    first = len(ins) + len(given) + len(after)

    def kernel(*refs):
        visible = list(ins) + made + list(scratch) + list(extra)
        body(Refs(visible, refs[: len(ins)] + refs[first:]))

    outs = pl.pallas_call(
        kernel,
        name=name,
        out_shape=[
            shapes[n] if n in FAR else pltpu.VMEM(shapes[n].shape, shapes[n].dtype) for n in made
        ],
        in_specs=[in_specs[n] for n in ins] + [VMEM] * len(given) + [ANY] * len(after),
        out_specs=[HBM if n in FAR else VMEM for n in made],
        scratch_shapes=[pltpu.VMEM(shapes[n].shape, shapes[n].dtype) for n in scratch]
        + list(extra.values()),
        input_output_aliases={len(ins) + i: made.index(n) for i, n in enumerate(given)},
        **kernel_settings(mebibytes, micros),
    )(*ins.values(), *(kept[n] for n in given), *after)
    return dict(zip(made, outs, strict=True))


def block_rows(pair, parity, rows):
    return pl.ds(pl.multiple_of((2 * pair + parity) * rows, 16), rows)


def weight_product(r, left, right, position, owners):
    mols, tokens, _ = right.shape
    rows = left.shape[-2] // owners
    core = r.info[BITS]
    for target, parity in ((r.send, 1 - core), (r.keep, core)):
        blocks = [block_rows(o, parity, rows) for o in range(owners // 2)]
        if len(left.shape) == 2:
            own = jnp.concatenate([left[at] for at in blocks], 0)
        else:
            parts = [jnp.concatenate([left[m, at] for at in blocks], 0) for m in range(mols)]
            own = jnp.concatenate(parts, 1)
        for base in range(0, right.shape[2], 256):
            part = right[:, :, base : base + 256].reshape(mols * tokens, 256)
            out = nn(own, part).astype(low)
            target[:, :, position + base : position + base + 256] = out.reshape(
                owners // 2, rows, 256
            )


def sum_table(r, position, owners):
    both = jnp.concatenate([jnp.sum(r.dense_sums[...], 0), jnp.sum(r.attn_sums[...], 0)], 0)
    width = both.shape[1]
    rows = width // owners
    core = r.info[BITS]
    high = both.astype(low).astype(wide)
    zeros = jnp.zeros((LANES - 32, width), wide)
    r.table[...] = jnp.concatenate([high, both - high, zeros], 0).T.astype(low)
    for target, parity in ((r.send, 1 - core), (r.keep, core)):
        for o in range(owners // 2):
            target[o, :, position : position + LANES] = r.table[block_rows(o, parity, rows)]


def swap(block, bit):
    devices = lax.axis_size("dp")
    return lax.ppermute(block, "dp", [(i, i ^ (1 << bit)) for i in range(devices)])


def halve(info, keep, received, bits, bit, after):
    count, rows, columns = keep.shape
    place = 1 << bits.index(bit)

    def kernel(info, keep, received, after, send, own):
        mine = info[BITS + bit]
        for j in range(count // 2):
            base = j // place * 2 * place + j % place
            for target, value in ((send, 1 - mine), (own, mine)):
                index = base + value * place
                target[j] = (keep[index].astype(wide) + received[index].astype(wide)).astype(low)

    shape = pltpu.VMEM((count // 2, rows, columns), low)
    return pl.pallas_call(
        kernel,
        name="halve",
        out_shape=[shape, shape],
        in_specs=[SMEM, VMEM, VMEM, ANY],
        out_specs=[VMEM, VMEM],
        **kernel_settings(2, 20),
    )(info, keep, received, after)


class Scatter:
    def __init__(self, info, keep, send, route):
        self.info, self.keep, self.route = info, keep, list(route)
        self.bits = sorted(route)
        self.received = swap(send, 0)

    def step(self, after):
        bit = self.route.pop(0)
        send, self.keep = halve(self.info, self.keep, self.received, self.bits, bit, after)
        self.bits.remove(bit)
        self.received = swap(send, bit)
        return send


def finish(scatters, shapes, write):
    arrays = [array for one in scatters for array in (one.keep, one.received)]

    def kernel(*refs):
        ins, outs = refs[: len(arrays)], refs[len(arrays) :]
        sums = [
            keep[0].astype(wide) + received[0].astype(wide)
            for keep, received in zip(ins[::2], ins[1::2])
        ]
        write(sums, outs)

    return pl.pallas_call(
        kernel,
        name="finish",
        out_shape=[jax.ShapeDtypeStruct(shape, wide) for shape in shapes],
        in_specs=[VMEM] * len(arrays),
        out_specs=[VMEM] * len(shapes),
        **kernel_settings(8, 20),
    )(*arrays)


def write_vectors(table, gain, bias):
    vectors = table.T
    vectors = vectors[:16] + vectors[16:32]
    for i, source in enumerate((8, 0)):
        gain[i : i + 1] = vectors[source : source + 1]
    for i, source in enumerate((9, 10, 11, 4, 1, 2, 3, 12, 13)):
        bias[i] = vectors[source : source + 1]


def plain_sums(state, width, hidden):
    both = [jnp.sum(state[n], 0) for n in names(dense_sums=1, attn_sums=1)]
    parts = [jnp.pad(jnp.concatenate(both, 0), ((0, LANES - 16), (0, 0))).T]
    lefts = [state[n] for n in names(activated=1, second_in=1, first_in=1)]
    lefts.insert(2, jnp.swapaxes(state["att_t"], 1, 2))
    rights = [state[n] for n in names(out_grad=1, pre_grad=1, branch_grad=1, mixed_grad=1)]
    for left, right in zip(lefts, rights, strict=True):
        rows = left.shape[0] * left.shape[1]
        parts.append(tn(left.reshape(rows, -1), right.reshape(rows, -1)))
    sums = lax.psum_scatter(
        jnp.concatenate(parts, 1), "dp", scatter_dimension=0, tiled=True
    )
    sizes = [LANES, width, hidden, width]
    cuts = [sum(sizes[: i + 1]) for i in range(4)]
    table, down, up, proj, qkv = jnp.split(sums, cuts, 1)
    vectors = table.T
    gain = jnp.stack([vectors[8], vectors[0]])
    bias = jnp.stack([vectors[i] for i in (9, 10, 11, 4, 1, 2, 3, 12, 13)])
    return qkv, proj, up, down, gain, bias


def body(
    boundary, counts, id_flags, norm_gains, biases, qkv_weight, proj_weight, up_weight, down_weight
):
    mols = counts.shape[0]
    width = boundary.shape[2]
    hidden = up_weight.shape[2]
    length = boundary.shape[1] // mols
    half = (mols + 1) // 2
    groups = [list(range(half)), list(range(half, mols))]
    devices = lax.axis_size("dp")
    rows = width // devices
    in_kernel = rows % 16 == 0
    assert devices.bit_length() <= COUNTS
    index = lax.axis_index("dp")
    info = jnp.concatenate(
        [
            lax.axis_index("section")[None],
            (index >> jnp.arange(COUNTS - BITS)) & 1,
            counts,
            id_flags,
        ]
    ).astype(jnp.int32)
    state = {}

    def shapes(group):
        return shapes_of(mols, length, width, hidden, half, len(group))

    def take(*lists, **more):
        return {n: state[n] for n in sum(lists, ()) + tuple(more)}

    def kept(*lists):
        return {n: state.get(n) for n in sum(lists, ())}

    def put(out, *lists):
        state.update({n: out[n] for n in sum(lists, ())})

    sources = dict(
        ends=boundary[0],
        biases=jnp.transpose(biases, (1, 0, 2)),
        gains=norm_gains[0],
        qkv=qkv_weight[0],
        proj=proj_weight[0],
        up=up_weight[0],
        down=down_weight[0],
    )

    def first_forward(group, load):
        stop = rows_of(group, length)[0].stop

        def run(r):
            section = r.info[SECTION]
            pieces = {}
            if load:
                pieces["ends"] = (r.from_ends, r.ends, slice(0, stop))
                for name in names(biases=1, gains=1):
                    pieces[name] = (getattr(r, "from_" + name), getattr(r, name), ...)
                for third in range(3):
                    columns = pl.ds(third * width, width)
                    pieces[third] = (r.from_qkv, r.qkv, (slice(None), columns))
                early = list(pieces)
                for name in names(proj=1, up=1, down=1):
                    pieces[name] = (getattr(r, "from_" + name), getattr(r, name), ...)
                pieces[None] = (r.from_ends, r.ends, slice(stop, mols * length))

            def copy(key):
                source, target, at = pieces[key]
                sem = r.sems.at[list(pieces).index(key)]
                return pltpu.make_async_copy(source.at[at], target.at[at], sem)

            def wait(key):
                if load:
                    copy(key).wait()
                    if key == 0:
                        for late in pieces:
                            if late not in early:
                                copy(late).start()

            if load:
                for key in early:
                    copy(key).start()

            @pl.when(section == 0)
            def _():
                wait("ends")
                here = slice(stop - len(group) * length, stop)
                forward(r, group, r.ends[here].astype(wide), length, wait)
                wait(None)

            if load:

                @pl.when(section != 0)
                def _():
                    for key in pieces:
                        wait(key)

        ins = dict(info=info)
        kept_names = SAVED
        specs, extra = {}, {}
        if load:
            sent = {"from_" + n: sources[n] for n in LOADS}
            ins |= {n: pltpu.with_memory_space_constraint(a, pltpu.HBM) for n, a in sent.items()}
            specs = dict.fromkeys(sent, HBM)
            kept_names = LOADS + SAVED
            extra = dict(sems=pltpu.SemaphoreType.DMA((len(LOADS) + 3,)))
        else:
            ins |= take(FORWARD)
        out = call(
            run, shapes(group), ins, kept(kept_names), names(result=1), FORWARD_SCRATCH,
            "first", 8, 3.0, specs, extra,
        )
        put(out, kept_names)
        return out["result"]

    def tick(second, first, received, received_grad, micros):
        def back(r, group, out_grad):
            save_cotangent(r, group, out_grad, length)
            backward_hidden(r, group, out_grad, length)
            backward_middle(r, group, out_grad, length)
            backward_attention(r, group, length)

        def run(r):
            if second:

                @pl.when(r.info[SECTION] == 1)
                def _():
                    forward(r, second, r.received[...].astype(wide), length)
                    back(r, second, r.ends[rows_of(second, length)[0]].astype(wide))

            if first:

                @pl.when(r.info[SECTION] == 0)
                def _():
                    back(r, first, r.received_grad[...].astype(wide))

        ins = dict(info=info) | take(BACKWARD)
        changed = HIDDEN + MIDDLE + LATE
        extra = {}
        if second:
            ins |= take(FORWARD) | dict(received=received)
            changed = SAVED + changed
            extra = dict(result=pltpu.VMEM((len(second) * length, width), low))
        else:
            ins |= take(SAVED)
        if first:
            ins |= dict(received_grad=received_grad)
        out = call(
            run, shapes(second or first), ins, kept(changed), names(grad=1),
            names(residual=1) + BACKWARD_SCRATCH + CARRY, "tick", 16, micros, extra=extra,
        )
        put(out, changed)
        return out["grad"]

    hops = []
    for group in groups:
        result = first_forward(group, group is groups[0])
        hops.append(lax.ppermute(result, "section", [(0, 1)]))
    grad_hops = []
    for group, hop in zip(groups, hops):
        grad = tick(group, None, hop, None, 0.2)
        grad_hops.append(lax.ppermute(grad, "section", [(1, 0)]))
    done_grad = tick(None, groups[0], None, grad_hops[0], 1.0)

    def turn(r):
        for source, target in (
            (r.activated, r.active_t),
            (r.second_in, r.second_t),
            (r.first_in, r.first_t),
        ):
            target[...] = source[...].reshape(-1, source.shape[2]).T

    if in_kernel:
        turned = names(active_t=1, second_t=1, first_t=1)
        ins = take(activated=1, second_in=1, first_in=1)
        out = call(turn, shapes(groups[1]), ins, {}, turned, (), "turn", 4, 1.0, after=[done_grad])
        put(out, turned)

    last = groups[1]
    last_grad = grad_hops[1]
    order = []

    def after():
        return order[-1:]

    def chunk(columns):
        shape = jax.ShapeDtypeStruct((devices // 2, rows, columns), low)
        return shapes(last) | dict(send=shape, keep=shape)

    def run(kernel, columns, ins, changed, made, scratch, name, mebibytes=4, extra=None):
        fresh = names(send=1, keep=1) if columns and in_kernel else ()
        out = call(
            kernel, chunk(columns), dict(info=info) | ins, kept(changed), made + fresh, scratch,
            name, mebibytes, 20.0, extra=extra, after=after(),
        )
        put(out, changed, made)
        order.append(out["send"] if fresh else out[(changed + made)[0]])
        return out

    def scatter(out, route):
        return Scatter(info, out["keep"], out["send"], route) if in_kernel else None

    def on_first(r, *functions):
        @pl.when(r.info[SECTION] == 0)
        def _():
            for function in functions:
                function()

    def hidden_kernel(r):
        def back():
            out_grad = r.received_grad[...].astype(wide)
            save_cotangent(r, last, out_grad, length)
            backward_hidden(r, last, out_grad, length)

        on_first(r, back)
        if in_kernel:
            weight_product(r, r.active_t, r.out_grad, 0, devices)
            weight_product(r, r.second_t, r.pre_grad, width, devices)

    def middle_kernel(r):
        on_first(r, lambda: backward_middle(r, last, r.received_grad[...].astype(wide), length))
        if in_kernel:
            weight_product(r, r.att_t, r.branch_grad, 0, devices)

    def attention_kernel(r):
        on_first(r, lambda: backward_attention(r, last, length))

    def part(third):
        ins = take(first_t=1, mixed_grad=1)
        columns, made, scratch = width, (), ()
        if third == 2:
            ins |= take(dense_sums=1, attn_sums=1, outputs=1, grads=1)
            columns, made, scratch = width + LANES, names(far_outputs=1, far_grads=1), names(table=1)

        def kernel(r):
            if third == 2:
                copies = [
                    pltpu.make_async_copy(r.outputs, r.far_outputs, r.sems.at[0]),
                    pltpu.make_async_copy(r.grads, r.far_grads, r.sems.at[1]),
                ]
                for copy in copies:
                    copy.start()
                sum_table(r, width, devices)
            at = slice(third * width, (third + 1) * width)
            weight_product(r, r.first_t, r.mixed_grad.at[:, :, at], 0, devices)
            if third == 2:
                for copy in copies:
                    copy.wait()

        extra = dict(sems=pltpu.SemaphoreType.DMA((2,)))
        out = run(kernel, columns, ins, (), made, scratch, "part", 4, extra if made else None)
        return scatter(out, (1, 2, 3))

    def hidden_step():
        ins = take(slope=1, down=1) | dict(received_grad=last_grad)
        if in_kernel:
            ins |= take(active_t=1, second_t=1)
        out = run(hidden_kernel, width + hidden, ins, HIDDEN, (), (), "hidden")
        return scatter(out, ROUTES[0])

    def middle_step():
        ins = take(pre_grad=1, gains=1, proj=1, up=1, n2=1, r2=1, att_t=1)
        ins |= dict(received_grad=last_grad)
        out = run(middle_kernel, width, ins, MIDDLE, CARRY, (), "middle")
        return scatter(out, ROUTES[1])

    def attention_step():
        ins = take(CARRY, gains=1, qkv=1, q=1, k=1, v=1, probs=1, inverse=1, att_t=1)
        ins |= take(n1=1, r1=1)
        run(attention_kernel, 0, ins, LATE, names(grad=1), BACKWARD_SCRATCH, "attention", 12)

    kernels = dict(
        h=hidden_step, m=middle_step, t=attention_step, q=lambda: part(0), k=lambda: part(1),
        v=lambda: part(2),
    )
    done = {}
    for word in PLAN:
        if len(word) == 1:
            if in_kernel or word in "hmt":
                done[word] = kernels[word]()
        elif in_kernel:
            order.append(done[word[0]].step(order[-1]))
    one = (rows, width)
    if in_kernel:

        def write(sums, outs):
            h, m, q, k, v = sums
            down, up, proj, qkv, gain, bias = outs
            down[...] = h[:, :width]
            up[...] = h[:, width:]
            proj[...] = m
            qkv[:, :width] = q
            qkv[:, width : 2 * width] = k
            qkv[:, 2 * width :] = v[:, :width]
            write_vectors(v[:, width:], gain, bias)

        down_grad, up_grad, proj_grad, qkv_grad, gain_grad, bias_grad = finish(
            [done[word] for word in "hmqkv"],
            [one, (rows, hidden), one, (rows, 3 * width), (2, rows), (9, 1, rows)],
            write,
        )
        bias_grad = jnp.squeeze(bias_grad, 1)
    else:
        qkv_grad, proj_grad, up_grad, down_grad, gain_grad, bias_grad = plain_sums(
            state, width, hidden
        )
    return (
        state["far_outputs" if in_kernel else "outputs"][None],
        state["far_grads" if in_kernel else "grads"][None],
        qkv_grad[None],
        proj_grad[None],
        up_grad[None],
        down_grad[None],
        gain_grad[None],
        bias_grad[None],
    )


def solution(mesh):
    rows = P("section", "dp", None)
    columns = P("section", None, "dp")
    weights = P("section", None, None)
    return jax.shard_map(
        body,
        mesh=mesh,
        in_specs=(rows, P("dp"), P("dp")) + (weights,) * 6,
        out_specs=(rows,) * 6 + (columns,) * 2,
        check_vma=False,
    )
```

```python
import math

import jax
import jax.numpy as jnp
from jax import lax
from jax.experimental import pallas as pl
from jax.experimental.pallas import tpu as pltpu
from jax.sharding import PartitionSpec as P

HEADS = 32
HEAD_DIM = 24
PAIRS = HEADS // 2
PAIR_ROWS = 2 * HEAD_DIM
LANES = 128
EPSILON = 1e-05
LAG = 4
SCALE = 1.0 / math.sqrt(HEAD_DIM)
LOG2E = math.log2(math.e)

low = jnp.bfloat16
wide = jnp.float32

VMEM = pl.BlockSpec(memory_space=pltpu.VMEM)
SMEM = pl.BlockSpec(memory_space=pltpu.SMEM)
HBM = pl.BlockSpec(memory_space=pltpu.HBM)
ANY = pl.BlockSpec(memory_space=pl.ANY)

SECTION, BITS, COUNTS = 0, 1, 8


def nn(left, right):
    return lax.dot_general(left, right, (((1,), (0,)), ((), ())), preferred_element_type=wide)


def nt(left, right):
    return lax.dot_general(left, right, (((1,), (1,)), ((), ())), preferred_element_type=wide)


def tn(left, right):
    return lax.dot_general(left, right, (((0,), (0,)), ((), ())), preferred_element_type=wide)


def pad_rows(values):
    extra = -values.shape[0] % LANES
    return jnp.concatenate([values, jnp.zeros((extra, values.shape[1]), values.dtype)], 0)


def pair_rows(pair):
    return slice(pair * PAIR_ROWS, (pair + 1) * PAIR_ROWS)


def two_blocks(rows):
    first = lax.broadcasted_iota(jnp.int32, rows.shape, 0) < HEAD_DIM
    zeros = jnp.zeros_like(rows)
    return jnp.concatenate([jnp.where(first, rows, zeros), jnp.where(first, zeros, rows)], 1)


def first_row(shape):
    return jnp.where(lax.broadcasted_iota(jnp.int32, shape, 0) == 0, 1.0, 0.0).astype(low)


def own_blocks(product):
    return jnp.concatenate([product[:HEAD_DIM, :LANES], product[HEAD_DIM:, LANES:]], 0)


def normalize(values):
    centred = values - jnp.mean(values, -1, keepdims=True)
    rstd = lax.rsqrt(jnp.mean(centred * centred, -1, keepdims=True) + EPSILON)
    return centred * rstd, rstd


def norm_back(scaled, normed, rstd):
    return rstd * (
        scaled
        - jnp.mean(scaled, -1, keepdims=True)
        - normed * jnp.mean(scaled * normed, -1, keepdims=True)
    )


def total(values):
    return jnp.sum(values, 0, keepdims=True)


def staged(count, *stages):
    items = [(i, pair) for i in range(count) for pair in range(PAIRS)]
    for step in range(len(items) + LAG * (len(stages) - 1)):
        for behind in reversed(range(len(stages))):
            if 0 <= step - LAG * behind < len(items):
                stages[behind](*items[step - LAG * behind])


PLAN = (
    "h", "m", "h1", "t", "v", "m1", "q", "v1", "k", "h2", "k1", "m2", "v2", "q1", "h3", "k2", "v3", "q2", "m3",
    "k3", "q3",
)
ROUTES = ((1, 2, 3), (2, 3, 1))


class Refs:
    def __init__(self, names, refs):
        for name, ref in zip(names, refs, strict=True):
            setattr(self, name, ref)

    def count(self, mol):
        return self.info[COUNTS + mol]

    def flag(self, mol):
        return self.info[COUNTS + (self.info.shape[0] - COUNTS) // 2 + mol]


def rows_of(group, length):
    start = group[0] * length
    each = [slice(i * length, (i + 1) * length) for i in range(len(group))]
    return slice(start, start + len(group) * length), each


def no_wait(ref):
    pass


def forward(r, group, x, length, wait=no_wait):
    width = x.shape[1]
    whole, each = rows_of(group, length)
    here = slice(0, len(group) * length)

    def save(ref, values):
        for mol, at in zip(group, each):
            ref[mol] = pad_rows(values[at]).astype(low)

    wait("biases")
    kinds = [jnp.where(r.flag(mol) == 1, r.biases[7], r.biases[8]) for mol in group]
    residual = jnp.concatenate([x[at] + kind for at, kind in zip(each, kinds)], 0)
    normed, rstd = normalize(residual)
    for mol, at in zip(group, each):
        r.n1[mol] = normed[at]
        r.r1[mol] = jnp.broadcast_to(rstd[at], (length, LANES))
    r.residual[here] = residual
    wait("gains")
    first_in = normed * r.gains[0:1] + r.biases[0]
    save(r.first_in, first_in)
    first_in = first_in.astype(low)
    for third, bias in enumerate((1, None, 2)):
        wait(third)
        part = nn(first_in, r.qkv[:, third * width : (third + 1) * width])
        if bias is not None:
            part = part + r.biases[bias]
        for mol, at in zip(group, each):
            (r.q, r.k, r.v)[third][mol] = pad_rows(part[at]).astype(low).T
    one = first_row((16, 2 * LANES))
    masks = [
        jnp.where(lax.broadcasted_iota(jnp.int32, (16, length), 1) < r.count(mol), 0.0, -1e30)
        for mol in group
    ]
    masks = [jnp.where(first_row(mask.shape) > 0, mask, 0.0).astype(low) for mask in masks]

    def multiply(i, pair):
        at = pair_rows(pair)
        keys = jnp.concatenate([r.k[group[i], at, :length], masks[i]], 0)
        queries = jnp.concatenate([two_blocks(r.q[group[i], at, :]), one], 0)
        r.scores[i, pair] = tn(keys, queries)

    def softmax(i, pair):
        scores = r.scores[i, pair]
        weights = jnp.exp2((scores - jnp.max(scores, 0, keepdims=True)) * (SCALE * LOG2E))
        r.probs[group[i], pair] = weights.astype(low)

    def attend(i, pair):
        at = pair_rows(pair)
        values = jnp.concatenate([r.v[group[i], at, :length], one[:, :length]], 0)
        product = nn(values, r.probs[group[i], pair])
        inverse = 1.0 / product[PAIR_ROWS : PAIR_ROWS + 1]
        r.inverse[group[i], pair : pair + 1] = inverse
        r.att_t[group[i], at, :] = own_blocks(product[:PAIR_ROWS] * inverse).astype(low)

    staged(len(group), multiply, softmax, attend)
    attended = jnp.concatenate([r.att_t[mol].T[:length].astype(wide) for mol in group], 0)
    wait("proj")
    middle = r.residual[here] + nn(attended.astype(low), r.proj[...]) + r.biases[3]
    normed, rstd = normalize(middle)
    for mol, at in zip(group, each):
        r.n2[mol] = normed[at]
        r.r2[mol] = jnp.broadcast_to(rstd[at], (length, LANES))
    r.residual[here] = middle
    second_in = normed * r.gains[1:2] + r.biases[4]
    save(r.second_in, second_in)
    wait("up")
    pre_act = nn(second_in.astype(low), r.up[...]) + r.biases[5]
    cdf = 0.5 * (1.0 + lax.erf(pre_act * math.sqrt(0.5)))
    pdf = jnp.exp(-0.5 * pre_act * pre_act) * (1.0 / math.sqrt(2.0 * math.pi))
    slope = cdf + pre_act * pdf
    for mol, at in zip(group, each):
        r.slope[mol] = slope[at]
    activated = pre_act * cdf
    save(r.activated, activated)
    wait("down")
    result = r.residual[here] + nn(activated.astype(low), r.down[...]) + r.biases[6]
    result = result.astype(low)
    r.outputs[whole] = result
    r.result[...] = result


def by_molecule(ref, group):
    return jnp.concatenate([ref[mol].astype(wide) for mol in group], 0)


def save_cotangent(r, group, out_grad, length):
    for mol, at in zip(group, rows_of(group, length)[1]):
        r.out_grad[mol] = pad_rows(out_grad[at]).astype(low)


def backward_hidden(r, group, out_grad, length):
    pre_grad = nn(out_grad.astype(low), r.down_t[...]) * by_molecule(r.slope, group)
    for mol, at in zip(group, rows_of(group, length)[1]):
        r.pre_grad[mol] = pad_rows(pre_grad[at]).astype(low)


def backward_middle(r, group, out_grad, length):
    each = rows_of(group, length)[1]
    pre_grad = jnp.concatenate([r.pre_grad[mol].astype(wide)[:length] for mol in group], 0)
    second_grad = nn(pre_grad.astype(low), r.up_t[...])
    normed = by_molecule(r.n2, group)
    rstd = by_molecule(r.r2, group)[:, :1]
    middle_grad = out_grad + norm_back(second_grad * r.gains[1:2], normed, rstd)
    r.middle_grad[: len(group) * length] = middle_grad
    branch_grad = middle_grad.astype(low)
    zeros = jnp.zeros((8, out_grad.shape[1]), wide)
    sums = [
        total(second_grad * normed),
        total(second_grad),
        total(pre_grad),
        total(out_grad),
        total(branch_grad.astype(wide)),
        zeros[:3],
    ]
    r.dense_sums[group[0]] = jnp.concatenate(sums, 0)
    for mol in group[1:]:
        r.dense_sums[mol] = zeros
    att_grad = nn(branch_grad, r.proj_t[...])
    for i, (mol, at) in enumerate(zip(group, each)):
        r.branch_grad[mol] = pad_rows(middle_grad[at]).astype(low)
        r.att_grad[i] = pad_rows(att_grad[at]).astype(low).T


def backward_attention(r, group, length):
    width = r.middle_grad.shape[1]
    whole, each = rows_of(group, length)
    pad = jnp.zeros((PAIR_ROWS, LANES - length), wide)
    deltas = {}

    def multiply(i, pair):
        at = pair_rows(pair)
        inverse = r.inverse[group[i], pair : pair + 1]
        heads = [
            jnp.broadcast_to(inverse[:, half : half + LANES], (HEAD_DIM, LANES))
            for half in (0, LANES)
        ]
        grad = (r.att_grad[i, at, :].astype(wide) * jnp.concatenate(heads, 0)).astype(low)
        r.att_grad[i, at, :] = grad
        product = r.att_t[group[i], at, :].astype(wide) * grad.astype(wide)
        deltas[i, pair] = jnp.concatenate([total(product[:HEAD_DIM]), total(product[HEAD_DIM:])], 1)
        r.scores[i, pair] = tn(r.v[group[i], at, :length], two_blocks(grad))

    def through_softmax(i, pair):
        at = pair_rows(pair)
        probs = r.probs[group[i], pair]
        grad = probs.astype(wide) * (r.scores[i, pair] - deltas.pop((i, pair)))
        r.score_grad[i, pair] = grad.astype(low)
        value = nt(two_blocks(r.att_grad[i, at, :]), probs)
        r.mixed_t[i, 2, at, :] = jnp.concatenate([value, pad], 1).astype(low)

    def to_inputs(i, pair):
        at = pair_rows(pair)
        grad = r.score_grad[i, pair]
        query = own_blocks(nn(r.k[group[i], at, :length], grad)) * SCALE
        key = nt(two_blocks(r.q[group[i], at, :]), grad) * SCALE
        r.mixed_t[i, 0, at, :] = query.astype(low)
        r.mixed_t[i, 1, at, :] = jnp.concatenate([key, pad], 1).astype(low)

    staged(len(group), multiply, through_softmax, to_inputs)
    first_grad = None
    mixed_sums = []
    for third in range(3):
        columns = slice(third * width, (third + 1) * width)
        for i, mol in enumerate(group):
            r.mixed_grad[mol, :, columns] = r.mixed_t[i, third].T
        mixed = jnp.concatenate(
            [r.mixed_grad[mol, :, columns].astype(wide)[:length] for mol in group], 0
        )
        mixed_sums.append(total(mixed))
        part = nt(mixed.astype(low), r.qkv[:, columns])
        first_grad = part if first_grad is None else first_grad + part
    normed = by_molecule(r.n1, group)
    rstd = by_molecule(r.r1, group)[:, :1]
    residual_grad = r.middle_grad[: len(group) * length] + norm_back(
        first_grad * r.gains[0:1], normed, rstd
    )
    low_grad = residual_grad.astype(low)
    r.grads[whole] = low_grad
    r.grad[...] = low_grad
    zeros = jnp.zeros((8, width), wide)
    kinds = [zeros[:1], zeros[:1]]
    for mol, at in zip(group, each):
        one = total(residual_grad[at])
        laplace = r.flag(mol) == 1
        kinds[0] = kinds[0] + jnp.where(laplace, one, zeros[:1])
        kinds[1] = kinds[1] + jnp.where(laplace, zeros[:1], one)
    sums = [total(first_grad * normed), total(first_grad), mixed_sums[0], mixed_sums[2]]
    r.attn_sums[group[0]] = jnp.concatenate(sums + kinds + [zeros[:2]], 0)
    for mol in group[1:]:
        r.attn_sums[mol] = zeros


def shapes_of(m, n, d, f, most, group):
    p = n + -n % LANES
    shape = jax.ShapeDtypeStruct
    return dict(
        biases=shape((9, 1, d), wide),
        gains=shape((2, d), wide),
        qkv=shape((d, 3 * d), low),
        proj=shape((d, d), low),
        up=shape((d, f), low),
        down=shape((f, d), low),
        qkv_t=shape((3 * d, d), low),
        proj_t=shape((d, d), low),
        up_t=shape((f, d), low),
        down_t=shape((d, f), low),
        ends=shape((m * n, d), low),
        q=shape((m, d, LANES), low),
        k=shape((m, d, LANES), low),
        v=shape((m, d, LANES), low),
        probs=shape((m, PAIRS, n, 2 * LANES), low),
        inverse=shape((m, PAIRS, 2 * LANES), wide),
        att_t=shape((m, d, LANES), low),
        n1=shape((m, n, d), wide),
        r1=shape((m, n, LANES), wide),
        n2=shape((m, n, d), wide),
        r2=shape((m, n, LANES), wide),
        slope=shape((m, n, f), wide),
        first_in=shape((m, p, d), low),
        second_in=shape((m, p, d), low),
        activated=shape((m, p, f), low),
        outputs=shape((m * n, d), low),
        out_grad=shape((m, p, d), low),
        pre_grad=shape((m, p, f), low),
        branch_grad=shape((m, p, d), low),
        dense_sums=shape((m, 8, d), wide),
        mixed_grad=shape((m, p, 3 * d), low),
        attn_sums=shape((m, 8, d), wide),
        grads=shape((m * n, d), low),
        middle_grad=shape((most * n, d), wide),
        att_grad=shape((most, d, LANES), low),
        result=shape((group * n, d), low),
        grad=shape((group * n, d), low),
        far_outputs=shape((m * n, d), low),
        far_grads=shape((m * n, d), low),
        first_t=shape((d, m * p), low),
        second_t=shape((d, m * p), low),
        active_t=shape((f, m * p), low),
        cotangent=shape((most * n, d), wide),
        residual=shape((most * n, d), wide),
        scores=shape((most, PAIRS, n, 2 * LANES), wide),
        score_grad=shape((most, PAIRS, n, 2 * LANES), low),
        mixed_t=shape((most, 3, d, LANES), low),
        table=shape((d, LANES), low),
    )


def names(**given):
    return tuple(given)


LOADS = names(ends=1, biases=1, gains=1, qkv=1, proj=1, up=1, down=1)
FORWARD = LOADS
BACKWARD = names(gains=1, qkv=1, proj_t=1, up_t=1, down_t=1)
SAVED = names(
    q=1, k=1, v=1, probs=1, inverse=1, att_t=1, n1=1, r1=1, n2=1, r2=1, slope=1,
    first_in=1, second_in=1, activated=1, outputs=1,
)
HIDDEN = names(out_grad=1, pre_grad=1)
MIDDLE = names(branch_grad=1, dense_sums=1)
FAR = names(far_outputs=1, far_grads=1)
CARRY = names(middle_grad=1, att_grad=1)
LATE = names(mixed_grad=1, attn_sums=1, grads=1)
FORWARD_SCRATCH = names(residual=1, scores=1)
BACKWARD_SCRATCH = names(scores=1, score_grad=1, mixed_t=1)


def kernel_settings(mebibytes, micros):
    return dict(
        compiler_params=pltpu.CompilerParams(vmem_limit_bytes=mebibytes << 20),
        cost_estimate=pl.CostEstimate(
            flops=int(micros * 1.15e9), bytes_accessed=1, transcendentals=0
        ),
    )


def call(
    body, shapes, ins, kept, fresh, scratch, name, mebibytes, micros, specs=None, extra=None, after=()
):
    given = [n for n in kept if kept[n] is not None]
    made = list(kept) + list(fresh)
    extra = extra or {}
    in_specs = dict.fromkeys(ins, VMEM) | dict(info=SMEM) | (specs or {})
    first = len(ins) + len(given) + len(after)

    def kernel(*refs):
        visible = list(ins) + made + list(scratch) + list(extra)
        body(Refs(visible, refs[: len(ins)] + refs[first:]))

    outs = pl.pallas_call(
        kernel,
        name=name,
        out_shape=[
            shapes[n] if n in FAR else pltpu.VMEM(shapes[n].shape, shapes[n].dtype) for n in made
        ],
        in_specs=[in_specs[n] for n in ins] + [VMEM] * len(given) + [ANY] * len(after),
        out_specs=[HBM if n in FAR else VMEM for n in made],
        scratch_shapes=[pltpu.VMEM(shapes[n].shape, shapes[n].dtype) for n in scratch]
        + list(extra.values()),
        input_output_aliases={len(ins) + i: made.index(n) for i, n in enumerate(given)},
        **kernel_settings(mebibytes, micros),
    )(*ins.values(), *(kept[n] for n in given), *after)
    return dict(zip(made, outs, strict=True))


def block_rows(pair, parity, rows):
    return pl.ds(pl.multiple_of((2 * pair + parity) * rows, 16), rows)


def weight_product(r, left, right, position, owners):
    mols, tokens, _ = right.shape
    rows = left.shape[-2] // owners
    core = r.info[BITS]
    for target, parity in ((r.send, 1 - core), (r.keep, core)):
        blocks = [block_rows(o, parity, rows) for o in range(owners // 2)]
        if len(left.shape) == 2:
            own = jnp.concatenate([left[at] for at in blocks], 0)
        else:
            parts = [jnp.concatenate([left[m, at] for at in blocks], 0) for m in range(mols)]
            own = jnp.concatenate(parts, 1)
        for base in range(0, right.shape[2], 256):
            part = right[:, :, base : base + 256].reshape(mols * tokens, 256)
            out = nn(own, part).astype(low)
            target[:, :, position + base : position + base + 256] = out.reshape(
                owners // 2, rows, 256
            )


def sum_table(r, position, owners):
    both = jnp.concatenate([jnp.sum(r.dense_sums[...], 0), jnp.sum(r.attn_sums[...], 0)], 0)
    width = both.shape[1]
    rows = width // owners
    core = r.info[BITS]
    high = both.astype(low).astype(wide)
    zeros = jnp.zeros((LANES - 32, width), wide)
    r.table[...] = jnp.concatenate([high, both - high, zeros], 0).T.astype(low)
    for target, parity in ((r.send, 1 - core), (r.keep, core)):
        for o in range(owners // 2):
            target[o, :, position : position + LANES] = r.table[block_rows(o, parity, rows)]


def swap(block, bit):
    devices = lax.axis_size("dp")
    return lax.ppermute(block, "dp", [(i, i ^ (1 << bit)) for i in range(devices)])


def halve(info, keep, received, bits, bit, after):
    count, rows, columns = keep.shape
    place = 1 << bits.index(bit)

    def kernel(info, keep, received, after, send, own):
        mine = info[BITS + bit]
        for j in range(count // 2):
            base = j // place * 2 * place + j % place
            for target, value in ((send, 1 - mine), (own, mine)):
                index = base + value * place
                target[j] = (keep[index].astype(wide) + received[index].astype(wide)).astype(low)

    shape = pltpu.VMEM((count // 2, rows, columns), low)
    return pl.pallas_call(
        kernel,
        name="halve",
        out_shape=[shape, shape],
        in_specs=[SMEM, VMEM, VMEM, ANY],
        out_specs=[VMEM, VMEM],
        **kernel_settings(2, 20),
    )(info, keep, received, after)


class Scatter:
    def __init__(self, info, keep, send, route):
        self.info, self.keep, self.route = info, keep, list(route)
        self.bits = sorted(route)
        self.received = swap(send, 0)

    def step(self, after):
        bit = self.route.pop(0)
        send, self.keep = halve(self.info, self.keep, self.received, self.bits, bit, after)
        self.bits.remove(bit)
        self.received = swap(send, bit)
        return send


def finish(scatters, shapes, write):
    arrays = [array for one in scatters for array in (one.keep, one.received)]

    def kernel(*refs):
        ins, outs = refs[: len(arrays)], refs[len(arrays) :]
        sums = [
            keep[0].astype(wide) + received[0].astype(wide)
            for keep, received in zip(ins[::2], ins[1::2])
        ]
        write(sums, outs)

    return pl.pallas_call(
        kernel,
        name="finish",
        out_shape=[jax.ShapeDtypeStruct(shape, wide) for shape in shapes],
        in_specs=[VMEM] * len(arrays),
        out_specs=[VMEM] * len(shapes),
        **kernel_settings(8, 20),
    )(*arrays)


def write_vectors(table, gain, bias):
    vectors = table.T
    vectors = vectors[:16] + vectors[16:32]
    for i, source in enumerate((8, 0)):
        gain[i : i + 1] = vectors[source : source + 1]
    for i, source in enumerate((9, 10, 11, 4, 1, 2, 3, 12, 13)):
        bias[i] = vectors[source : source + 1]


def plain_sums(state, width, hidden):
    both = [jnp.sum(state[n], 0) for n in names(dense_sums=1, attn_sums=1)]
    parts = [jnp.pad(jnp.concatenate(both, 0), ((0, LANES - 16), (0, 0))).T]
    lefts = [state[n] for n in names(activated=1, second_in=1, first_in=1)]
    lefts.insert(2, jnp.swapaxes(state["att_t"], 1, 2))
    rights = [state[n] for n in names(out_grad=1, pre_grad=1, branch_grad=1, mixed_grad=1)]
    for left, right in zip(lefts, rights, strict=True):
        rows = left.shape[0] * left.shape[1]
        parts.append(tn(left.reshape(rows, -1), right.reshape(rows, -1)))
    sums = lax.psum_scatter(
        jnp.concatenate(parts, 1), "dp", scatter_dimension=0, tiled=True
    )
    sizes = [LANES, width, hidden, width]
    cuts = [sum(sizes[: i + 1]) for i in range(4)]
    table, down, up, proj, qkv = jnp.split(sums, cuts, 1)
    vectors = table.T
    gain = jnp.stack([vectors[8], vectors[0]])
    bias = jnp.stack([vectors[i] for i in (9, 10, 11, 4, 1, 2, 3, 12, 13)])
    return qkv, proj, up, down, gain, bias


def body(
    boundary, counts, id_flags, norm_gains, biases, qkv_weight, proj_weight, up_weight, down_weight
):
    mols = counts.shape[0]
    width = boundary.shape[2]
    hidden = up_weight.shape[2]
    length = boundary.shape[1] // mols
    half = (mols + 1) // 2
    groups = [list(range(half)), list(range(half, mols))]
    devices = lax.axis_size("dp")
    rows = width // devices
    in_kernel = rows % 16 == 0
    assert devices.bit_length() <= COUNTS
    index = lax.axis_index("dp")
    info = jnp.concatenate(
        [
            lax.axis_index("section")[None],
            (index >> jnp.arange(COUNTS - BITS)) & 1,
            counts,
            id_flags,
        ]
    ).astype(jnp.int32)
    state = {}

    def shapes(group):
        return shapes_of(mols, length, width, hidden, half, len(group))

    def take(*lists, **more):
        return {n: state[n] for n in sum(lists, ()) + tuple(more)}

    def kept(*lists):
        return {n: state.get(n) for n in sum(lists, ())}

    def put(out, *lists):
        state.update({n: out[n] for n in sum(lists, ())})

    sources = dict(
        ends=boundary[0],
        biases=jnp.transpose(biases, (1, 0, 2)),
        gains=norm_gains[0],
        qkv=qkv_weight[0],
        proj=proj_weight[0],
        up=up_weight[0],
        down=down_weight[0],
    )

    def first_forward(group, load):
        stop = rows_of(group, length)[0].stop

        def run(r):
            section = r.info[SECTION]
            pieces = {}
            if load:
                pieces["ends"] = (r.from_ends, r.ends, slice(0, stop))
                for name in names(biases=1, gains=1):
                    pieces[name] = (getattr(r, "from_" + name), getattr(r, name), ...)
                for third in range(3):
                    columns = pl.ds(third * width, width)
                    pieces[third] = (r.from_qkv, r.qkv, (slice(None), columns))
                early = list(pieces)
                for name in names(proj=1, up=1, down=1):
                    pieces[name] = (getattr(r, "from_" + name), getattr(r, name), ...)
                pieces[None] = (r.from_ends, r.ends, slice(stop, mols * length))

            def copy(key):
                source, target, at = pieces[key]
                sem = r.sems.at[list(pieces).index(key)]
                return pltpu.make_async_copy(source.at[at], target.at[at], sem)

            def wait(key):
                if load:
                    copy(key).wait()
                    if key == 0:
                        for late in pieces:
                            if late not in early:
                                copy(late).start()

            if load:
                for key in early:
                    copy(key).start()

            @pl.when(section == 0)
            def _():
                wait("ends")
                here = slice(stop - len(group) * length, stop)
                forward(r, group, r.ends[here].astype(wide), length, wait)
                wait(None)

            if load:

                @pl.when(section != 0)
                def _():
                    for key in pieces:
                        wait(key)

        ins = dict(info=info)
        kept_names = SAVED
        specs, extra = {}, {}
        if load:
            sent = {"from_" + n: sources[n] for n in LOADS}
            ins |= {n: pltpu.with_memory_space_constraint(a, pltpu.HBM) for n, a in sent.items()}
            specs = dict.fromkeys(sent, HBM)
            kept_names = LOADS + SAVED
            extra = dict(sems=pltpu.SemaphoreType.DMA((len(LOADS) + 3,)))
        else:
            ins |= take(FORWARD)
        out = call(
            run, shapes(group), ins, kept(kept_names), names(result=1), FORWARD_SCRATCH,
            "first", 8, 3.0, specs, extra,
        )
        put(out, kept_names)
        return out["result"]

    def tick(second, first, received, received_grad, micros):
        def back(r, group, out_grad):
            save_cotangent(r, group, out_grad, length)
            backward_hidden(r, group, out_grad, length)
            backward_middle(r, group, out_grad, length)
            backward_attention(r, group, length)

        def run(r):
            if second:

                @pl.when(r.info[SECTION] == 1)
                def _():
                    forward(r, second, r.received[...].astype(wide), length)
                    back(r, second, r.ends[rows_of(second, length)[0]].astype(wide))

            if first:

                @pl.when(r.info[SECTION] == 0)
                def _():
                    back(r, first, r.received_grad[...].astype(wide))

        ins = dict(info=info) | take(BACKWARD)
        changed = HIDDEN + MIDDLE + LATE
        extra = {}
        if second:
            ins |= take(FORWARD) | dict(received=received)
            changed = SAVED + changed
            extra = dict(result=pltpu.VMEM((len(second) * length, width), low))
        else:
            ins |= take(SAVED)
        if first:
            ins |= dict(received_grad=received_grad)
        out = call(
            run, shapes(second or first), ins, kept(changed), names(grad=1),
            names(residual=1) + BACKWARD_SCRATCH + CARRY, "tick", 16, micros, extra=extra,
        )
        put(out, changed)
        return out["grad"]

    hops = []
    for group in groups:
        result = first_forward(group, group is groups[0])
        hops.append(lax.ppermute(result, "section", [(0, 1)]))
    turned_weights = names(down_t=1, up_t=1, proj_t=1)

    def turn_weights(r):
        for source, target in ((r.down, r.down_t), (r.up, r.up_t), (r.proj, r.proj_t),):
            target[...] = source[...].T

    out = call(
        turn_weights, shapes(groups[1]), take(down=1, up=1, proj=1), {}, turned_weights, (), "turn", 4, 0.2,
        after=[result],
    )
    put(out, turned_weights)
    grad_hops = []
    for group, hop in zip(groups, hops):
        grad = tick(group, None, hop, None, 0.2)
        grad_hops.append(lax.ppermute(grad, "section", [(1, 0)]))
    done_grad = tick(None, groups[0], None, grad_hops[0], 1.0)

    def turn(r):
        for source, target in (
            (r.activated, r.active_t),
            (r.second_in, r.second_t),
            (r.first_in, r.first_t),
        ):
            target[...] = source[...].reshape(-1, source.shape[2]).T

    if in_kernel:
        turned = names(active_t=1, second_t=1, first_t=1)
        ins = take(activated=1, second_in=1, first_in=1)
        out = call(turn, shapes(groups[1]), ins, {}, turned, (), "turn", 4, 1.0, after=[done_grad])
        put(out, turned)

    last = groups[1]
    last_grad = grad_hops[1]
    order = []

    def after():
        return order[-1:]

    def chunk(columns):
        shape = jax.ShapeDtypeStruct((devices // 2, rows, columns), low)
        return shapes(last) | dict(send=shape, keep=shape)

    def run(kernel, columns, ins, changed, made, scratch, name, mebibytes=4, extra=None):
        fresh = names(send=1, keep=1) if columns and in_kernel else ()
        out = call(
            kernel, chunk(columns), dict(info=info) | ins, kept(changed), made + fresh, scratch,
            name, mebibytes, 20.0, extra=extra, after=after(),
        )
        put(out, changed, made)
        order.append(out["send"] if fresh else out[(changed + made)[0]])
        return out

    def scatter(out, route):
        return Scatter(info, out["keep"], out["send"], route) if in_kernel else None

    def on_first(r, *functions):
        @pl.when(r.info[SECTION] == 0)
        def _():
            for function in functions:
                function()

    def hidden_kernel(r):
        def back():
            out_grad = r.received_grad[...].astype(wide)
            save_cotangent(r, last, out_grad, length)
            backward_hidden(r, last, out_grad, length)

        on_first(r, back)
        if in_kernel:
            weight_product(r, r.active_t, r.out_grad, 0, devices)
            weight_product(r, r.second_t, r.pre_grad, width, devices)

    def middle_kernel(r):
        on_first(r, lambda: backward_middle(r, last, r.received_grad[...].astype(wide), length))
        if in_kernel:
            weight_product(r, r.att_t, r.branch_grad, 0, devices)

    def attention_kernel(r):
        on_first(r, lambda: backward_attention(r, last, length))

    def part(third):
        ins = take(first_t=1, mixed_grad=1)
        columns, made, scratch = width, (), ()
        if third == 2:
            ins |= take(dense_sums=1, attn_sums=1, outputs=1, grads=1)
            columns, made, scratch = width + LANES, names(far_outputs=1, far_grads=1), names(table=1)

        def kernel(r):
            if third == 2:
                copies = [
                    pltpu.make_async_copy(r.outputs, r.far_outputs, r.sems.at[0]),
                    pltpu.make_async_copy(r.grads, r.far_grads, r.sems.at[1]),
                ]
                for copy in copies:
                    copy.start()
                sum_table(r, width, devices)
            at = slice(third * width, (third + 1) * width)
            weight_product(r, r.first_t, r.mixed_grad.at[:, :, at], 0, devices)
            if third == 2:
                for copy in copies:
                    copy.wait()

        extra = dict(sems=pltpu.SemaphoreType.DMA((2,)))
        out = run(kernel, columns, ins, (), made, scratch, "part", 4, extra if made else None)
        return scatter(out, (1, 2, 3))

    def hidden_step():
        ins = take(slope=1, down_t=1) | dict(received_grad=last_grad)
        if in_kernel:
            ins |= take(active_t=1, second_t=1)
        out = run(hidden_kernel, width + hidden, ins, HIDDEN, (), (), "hidden")
        return scatter(out, ROUTES[0])

    def middle_step():
        ins = take(pre_grad=1, gains=1, proj_t=1, up_t=1, n2=1, r2=1, att_t=1)
        ins |= dict(received_grad=last_grad)
        out = run(middle_kernel, width, ins, MIDDLE, CARRY, (), "middle")
        return scatter(out, ROUTES[1])

    def attention_step():
        ins = take(CARRY, gains=1, qkv=1, q=1, k=1, v=1, probs=1, inverse=1, att_t=1)
        ins |= take(n1=1, r1=1)
        run(attention_kernel, 0, ins, LATE, names(grad=1), BACKWARD_SCRATCH, "attention", 12)

    kernels = dict(
        h=hidden_step, m=middle_step, t=attention_step, q=lambda: part(0), k=lambda: part(1),
        v=lambda: part(2),
    )
    done = {}
    for word in PLAN:
        if len(word) == 1:
            if in_kernel or word in "hmt":
                done[word] = kernels[word]()
        elif in_kernel:
            order.append(done[word[0]].step(order[-1]))
    one = (rows, width)
    if in_kernel:

        def write(sums, outs):
            h, m, q, k, v = sums
            down, up, proj, qkv, gain, bias = outs
            down[...] = h[:, :width]
            up[...] = h[:, width:]
            proj[...] = m
            qkv[:, :width] = q
            qkv[:, width : 2 * width] = k
            qkv[:, 2 * width :] = v[:, :width]
            write_vectors(v[:, width:], gain, bias)

        down_grad, up_grad, proj_grad, qkv_grad, gain_grad, bias_grad = finish(
            [done[word] for word in "hmqkv"],
            [one, (rows, hidden), one, (rows, 3 * width), (2, rows), (9, 1, rows)],
            write,
        )
        bias_grad = jnp.squeeze(bias_grad, 1)
    else:
        qkv_grad, proj_grad, up_grad, down_grad, gain_grad, bias_grad = plain_sums(
            state, width, hidden
        )
    return (
        state["far_outputs" if in_kernel else "outputs"][None],
        state["far_grads" if in_kernel else "grads"][None],
        qkv_grad[None],
        proj_grad[None],
        up_grad[None],
        down_grad[None],
        gain_grad[None],
        bias_grad[None],
    )


def solution(mesh):
    rows = P("section", "dp", None)
    columns = P("section", None, "dp")
    weights = P("section", None, None)
    return jax.shard_map(
        body,
        mesh=mesh,
        in_specs=(rows, P("dp"), P("dp")) + (weights,) * 6,
        out_specs=(rows,) * 6 + (columns,) * 2,
        check_vma=False,
    )
```

```python
import math

import jax
import jax.numpy as jnp
from jax import lax
from jax.experimental import pallas as pl
from jax.experimental.pallas import tpu as pltpu
from jax.sharding import PartitionSpec as P

HEADS = 32
HEAD_DIM = 24
PAIRS = HEADS // 2
PAIR_ROWS = 2 * HEAD_DIM
LANES = 128
EPSILON = 1e-05
LAG = 4
SCALE = 1.0 / math.sqrt(HEAD_DIM)
LOG2E = math.log2(math.e)

low = jnp.bfloat16
wide = jnp.float32

VMEM = pl.BlockSpec(memory_space=pltpu.VMEM)
SMEM = pl.BlockSpec(memory_space=pltpu.SMEM)
HBM = pl.BlockSpec(memory_space=pltpu.HBM)
ANY = pl.BlockSpec(memory_space=pl.ANY)

SECTION, BITS, COUNTS = 0, 1, 8


def nn(left, right):
    return lax.dot_general(left, right, (((1,), (0,)), ((), ())), preferred_element_type=wide)


def nt(left, right):
    return lax.dot_general(left, right, (((1,), (1,)), ((), ())), preferred_element_type=wide)


def tn(left, right):
    return lax.dot_general(left, right, (((0,), (0,)), ((), ())), preferred_element_type=wide)


def pad_rows(values):
    extra = -values.shape[0] % LANES
    return jnp.concatenate([values, jnp.zeros((extra, values.shape[1]), values.dtype)], 0)


def pair_rows(pair):
    return slice(pair * PAIR_ROWS, (pair + 1) * PAIR_ROWS)


def two_blocks(rows):
    first = lax.broadcasted_iota(jnp.int32, rows.shape, 0) < HEAD_DIM
    zeros = jnp.zeros_like(rows)
    return jnp.concatenate([jnp.where(first, rows, zeros), jnp.where(first, zeros, rows)], 1)


def first_row(shape):
    return jnp.where(lax.broadcasted_iota(jnp.int32, shape, 0) == 0, 1.0, 0.0).astype(low)


def own_blocks(product):
    return jnp.concatenate([product[:HEAD_DIM, :LANES], product[HEAD_DIM:, LANES:]], 0)


def normalize(values):
    centred = values - jnp.mean(values, -1, keepdims=True)
    rstd = lax.rsqrt(jnp.mean(centred * centred, -1, keepdims=True) + EPSILON)
    return centred * rstd, rstd


def norm_back(scaled, normed, rstd):
    return rstd * (
        scaled
        - jnp.mean(scaled, -1, keepdims=True)
        - normed * jnp.mean(scaled * normed, -1, keepdims=True)
    )


def total(values):
    return jnp.sum(values, 0, keepdims=True)


def staged(count, *stages):
    items = [(i, pair) for i in range(count) for pair in range(PAIRS)]
    for step in range(len(items) + LAG * (len(stages) - 1)):
        for behind in reversed(range(len(stages))):
            if 0 <= step - LAG * behind < len(items):
                stages[behind](*items[step - LAG * behind])


PLAN = (
    "h", "m", "h1", "t", "v", "m1", "q", "v1", "k", "h2", "k1", "m2", "q1", "v2", "h3", "k2", "v3", "q2", "m3", "k3", "q3",
)
ROUTES = ((1, 2, 3), (2, 3, 1))


class Refs:
    def __init__(self, names, refs):
        for name, ref in zip(names, refs, strict=True):
            setattr(self, name, ref)

    def count(self, mol):
        return self.info[COUNTS + mol]

    def flag(self, mol):
        return self.info[COUNTS + (self.info.shape[0] - COUNTS) // 2 + mol]


def rows_of(group, length):
    start = group[0] * length
    each = [slice(i * length, (i + 1) * length) for i in range(len(group))]
    return slice(start, start + len(group) * length), each


def no_wait(ref):
    pass


def forward(r, group, x, length, wait=no_wait):
    width = x.shape[1]
    whole, each = rows_of(group, length)
    here = slice(0, len(group) * length)

    def save(ref, values):
        for mol, at in zip(group, each):
            ref[mol] = pad_rows(values[at]).astype(low)

    wait("biases")
    kinds = [jnp.where(r.flag(mol) == 1, r.biases[7], r.biases[8]) for mol in group]
    residual = jnp.concatenate([x[at] + kind for at, kind in zip(each, kinds)], 0)
    normed, rstd = normalize(residual)
    for mol, at in zip(group, each):
        r.n1[mol] = normed[at]
        r.r1[mol] = jnp.broadcast_to(rstd[at], (length, LANES))
    r.residual[here] = residual
    wait("gains")
    first_in = normed * r.gains[0:1] + r.biases[0]
    save(r.first_in, first_in)
    first_in = first_in.astype(low)
    for third, bias in enumerate((1, None, 2)):
        wait(third)
        part = nn(first_in, r.qkv[:, third * width : (third + 1) * width])
        if bias is not None:
            part = part + r.biases[bias]
        for mol, at in zip(group, each):
            (r.q, r.k, r.v)[third][mol] = pad_rows(part[at]).astype(low).T
    one = first_row((16, 2 * LANES))
    masks = [
        jnp.where(lax.broadcasted_iota(jnp.int32, (16, length), 1) < r.count(mol), 0.0, -1e30)
        for mol in group
    ]
    masks = [jnp.where(first_row(mask.shape) > 0, mask, 0.0).astype(low) for mask in masks]

    def multiply(i, pair):
        at = pair_rows(pair)
        keys = jnp.concatenate([r.k[group[i], at, :length], masks[i]], 0)
        queries = jnp.concatenate([two_blocks(r.q[group[i], at, :]), one], 0)
        r.scores[i, pair] = tn(keys, queries)

    def softmax(i, pair):
        scores = r.scores[i, pair]
        weights = jnp.exp2((scores - jnp.max(scores, 0, keepdims=True)) * (SCALE * LOG2E))
        r.probs[group[i], pair] = weights.astype(low)

    def attend(i, pair):
        at = pair_rows(pair)
        values = jnp.concatenate([r.v[group[i], at, :length], one[:, :length]], 0)
        product = nn(values, r.probs[group[i], pair])
        inverse = 1.0 / product[PAIR_ROWS : PAIR_ROWS + 1]
        r.inverse[group[i], pair : pair + 1] = inverse
        r.att_t[group[i], at, :] = own_blocks(product[:PAIR_ROWS] * inverse).astype(low)

    staged(len(group), multiply, softmax, attend)
    attended = jnp.concatenate([r.att_t[mol].T[:length].astype(wide) for mol in group], 0)
    wait("proj")
    middle = r.residual[here] + nn(attended.astype(low), r.proj[...]) + r.biases[3]
    normed, rstd = normalize(middle)
    for mol, at in zip(group, each):
        r.n2[mol] = normed[at]
        r.r2[mol] = jnp.broadcast_to(rstd[at], (length, LANES))
    r.residual[here] = middle
    second_in = normed * r.gains[1:2] + r.biases[4]
    save(r.second_in, second_in)
    wait("up")
    pre_act = nn(second_in.astype(low), r.up[...]) + r.biases[5]
    cdf = 0.5 * (1.0 + lax.erf(pre_act * math.sqrt(0.5)))
    pdf = jnp.exp(-0.5 * pre_act * pre_act) * (1.0 / math.sqrt(2.0 * math.pi))
    slope = cdf + pre_act * pdf
    for mol, at in zip(group, each):
        r.slope[mol] = slope[at]
    activated = pre_act * cdf
    save(r.activated, activated)
    wait("down")
    result = r.residual[here] + nn(activated.astype(low), r.down[...]) + r.biases[6]
    result = result.astype(low)
    r.outputs[whole] = result
    r.result[...] = result


def by_molecule(ref, group):
    return jnp.concatenate([ref[mol].astype(wide) for mol in group], 0)


def save_cotangent(r, group, out_grad, length):
    for mol, at in zip(group, rows_of(group, length)[1]):
        r.out_grad[mol] = pad_rows(out_grad[at]).astype(low)


def backward_hidden(r, group, out_grad, length):
    pre_grad = nn(out_grad.astype(low), r.down_t[...]) * by_molecule(r.slope, group)
    for mol, at in zip(group, rows_of(group, length)[1]):
        r.pre_grad[mol] = pad_rows(pre_grad[at]).astype(low)


def backward_middle(r, group, out_grad, length):
    each = rows_of(group, length)[1]
    pre_grad = jnp.concatenate([r.pre_grad[mol].astype(wide)[:length] for mol in group], 0)
    second_grad = nn(pre_grad.astype(low), r.up_t[...])
    normed = by_molecule(r.n2, group)
    rstd = by_molecule(r.r2, group)[:, :1]
    middle_grad = out_grad + norm_back(second_grad * r.gains[1:2], normed, rstd)
    r.middle_grad[: len(group) * length] = middle_grad
    branch_grad = middle_grad.astype(low)
    zeros = jnp.zeros((8, out_grad.shape[1]), wide)
    sums = [
        total(second_grad * normed),
        total(second_grad),
        total(pre_grad),
        total(out_grad),
        total(branch_grad.astype(wide)),
        zeros[:3],
    ]
    r.dense_sums[group[0]] = jnp.concatenate(sums, 0)
    for mol in group[1:]:
        r.dense_sums[mol] = zeros
    att_grad = nn(branch_grad, r.proj_t[...])
    for i, (mol, at) in enumerate(zip(group, each)):
        r.branch_grad[mol] = pad_rows(middle_grad[at]).astype(low)
        r.att_grad[i] = pad_rows(att_grad[at]).astype(low).T


def backward_attention(r, group, length):
    width = r.middle_grad.shape[1]
    whole, each = rows_of(group, length)
    pad = jnp.zeros((PAIR_ROWS, LANES - length), wide)
    deltas = {}

    def multiply(i, pair):
        at = pair_rows(pair)
        inverse = r.inverse[group[i], pair : pair + 1]
        heads = [
            jnp.broadcast_to(inverse[:, half : half + LANES], (HEAD_DIM, LANES))
            for half in (0, LANES)
        ]
        grad = (r.att_grad[i, at, :].astype(wide) * jnp.concatenate(heads, 0)).astype(low)
        r.att_grad[i, at, :] = grad
        product = r.att_t[group[i], at, :].astype(wide) * grad.astype(wide)
        deltas[i, pair] = jnp.concatenate([total(product[:HEAD_DIM]), total(product[HEAD_DIM:])], 1)
        r.scores[i, pair] = tn(r.v[group[i], at, :length], two_blocks(grad))

    def through_softmax(i, pair):
        at = pair_rows(pair)
        probs = r.probs[group[i], pair]
        grad = probs.astype(wide) * (r.scores[i, pair] - deltas.pop((i, pair)))
        r.score_grad[i, pair] = grad.astype(low)
        value = nt(two_blocks(r.att_grad[i, at, :]), probs)
        r.mixed_t[i, 2, at, :] = jnp.concatenate([value, pad], 1).astype(low)

    def to_inputs(i, pair):
        at = pair_rows(pair)
        grad = r.score_grad[i, pair]
        query = own_blocks(nn(r.k[group[i], at, :length], grad)) * SCALE
        key = nt(two_blocks(r.q[group[i], at, :]), grad) * SCALE
        r.mixed_t[i, 0, at, :] = query.astype(low)
        r.mixed_t[i, 1, at, :] = jnp.concatenate([key, pad], 1).astype(low)

    staged(len(group), multiply, through_softmax, to_inputs)
    first_grad = None
    mixed_sums = []
    for third in range(3):
        columns = slice(third * width, (third + 1) * width)
        for i, mol in enumerate(group):
            r.mixed_grad[mol, :, columns] = r.mixed_t[i, third].T
        mixed = jnp.concatenate(
            [r.mixed_grad[mol, :, columns].astype(wide)[:length] for mol in group], 0
        )
        mixed_sums.append(total(mixed))
        part = nt(mixed.astype(low), r.qkv[:, columns])
        first_grad = part if first_grad is None else first_grad + part
    normed = by_molecule(r.n1, group)
    rstd = by_molecule(r.r1, group)[:, :1]
    residual_grad = r.middle_grad[: len(group) * length] + norm_back(
        first_grad * r.gains[0:1], normed, rstd
    )
    low_grad = residual_grad.astype(low)
    r.grads[whole] = low_grad
    r.grad[...] = low_grad
    zeros = jnp.zeros((8, width), wide)
    kinds = [zeros[:1], zeros[:1]]
    for mol, at in zip(group, each):
        one = total(residual_grad[at])
        laplace = r.flag(mol) == 1
        kinds[0] = kinds[0] + jnp.where(laplace, one, zeros[:1])
        kinds[1] = kinds[1] + jnp.where(laplace, zeros[:1], one)
    sums = [total(first_grad * normed), total(first_grad), mixed_sums[0], mixed_sums[2]]
    r.attn_sums[group[0]] = jnp.concatenate(sums + kinds + [zeros[:2]], 0)
    for mol in group[1:]:
        r.attn_sums[mol] = zeros


def shapes_of(m, n, d, f, most, group):
    p = n + -n % LANES
    shape = jax.ShapeDtypeStruct
    return dict(
        biases=shape((9, 1, d), wide),
        gains=shape((2, d), wide),
        qkv=shape((d, 3 * d), low),
        proj=shape((d, d), low),
        up=shape((d, f), low),
        down=shape((f, d), low),
        qkv_t=shape((3 * d, d), low),
        proj_t=shape((d, d), low),
        up_t=shape((f, d), low),
        down_t=shape((d, f), low),
        ends=shape((m * n, d), low),
        q=shape((m, d, LANES), low),
        k=shape((m, d, LANES), low),
        v=shape((m, d, LANES), low),
        probs=shape((m, PAIRS, n, 2 * LANES), low),
        inverse=shape((m, PAIRS, 2 * LANES), wide),
        att_t=shape((m, d, LANES), low),
        n1=shape((m, n, d), wide),
        r1=shape((m, n, LANES), wide),
        n2=shape((m, n, d), wide),
        r2=shape((m, n, LANES), wide),
        slope=shape((m, n, f), wide),
        first_in=shape((m, p, d), low),
        second_in=shape((m, p, d), low),
        activated=shape((m, p, f), low),
        outputs=shape((m * n, d), low),
        out_grad=shape((m, p, d), low),
        pre_grad=shape((m, p, f), low),
        branch_grad=shape((m, p, d), low),
        dense_sums=shape((m, 8, d), wide),
        mixed_grad=shape((m, p, 3 * d), low),
        attn_sums=shape((m, 8, d), wide),
        grads=shape((m * n, d), low),
        middle_grad=shape((most * n, d), wide),
        att_grad=shape((most, d, LANES), low),
        result=shape((group * n, d), low),
        grad=shape((group * n, d), low),
        far_outputs=shape((m * n, d), low),
        far_grads=shape((m * n, d), low),
        first_t=shape((d, m * p), low),
        second_t=shape((d, m * p), low),
        active_t=shape((f, m * p), low),
        cotangent=shape((most * n, d), wide),
        residual=shape((most * n, d), wide),
        scores=shape((most, PAIRS, n, 2 * LANES), wide),
        score_grad=shape((most, PAIRS, n, 2 * LANES), low),
        mixed_t=shape((most, 3, d, LANES), low),
        table=shape((d, LANES), low),
    )


def names(**given):
    return tuple(given)


LOADS = names(ends=1, biases=1, gains=1, qkv=1, proj=1, up=1, down=1)
FORWARD = LOADS
BACKWARD = names(gains=1, qkv=1, proj_t=1, up_t=1, down_t=1)
SAVED = names(
    q=1, k=1, v=1, probs=1, inverse=1, att_t=1, n1=1, r1=1, n2=1, r2=1, slope=1,
    first_in=1, second_in=1, activated=1, outputs=1,
)
HIDDEN = names(out_grad=1, pre_grad=1)
MIDDLE = names(branch_grad=1, dense_sums=1)
FAR = names(far_outputs=1, far_grads=1)
CARRY = names(middle_grad=1, att_grad=1)
LATE = names(mixed_grad=1, attn_sums=1, grads=1)
FORWARD_SCRATCH = names(residual=1, scores=1)
BACKWARD_SCRATCH = names(scores=1, score_grad=1, mixed_t=1)


def kernel_settings(mebibytes, micros):
    return dict(
        compiler_params=pltpu.CompilerParams(vmem_limit_bytes=mebibytes << 20),
        cost_estimate=pl.CostEstimate(
            flops=int(micros * 1.15e9), bytes_accessed=1, transcendentals=0
        ),
    )


def call(
    body, shapes, ins, kept, fresh, scratch, name, mebibytes, micros, specs=None, extra=None, after=()
):
    given = [n for n in kept if kept[n] is not None]
    made = list(kept) + list(fresh)
    extra = extra or {}
    in_specs = dict.fromkeys(ins, VMEM) | dict(info=SMEM) | (specs or {})
    first = len(ins) + len(given) + len(after)

    def kernel(*refs):
        visible = list(ins) + made + list(scratch) + list(extra)
        body(Refs(visible, refs[: len(ins)] + refs[first:]))

    outs = pl.pallas_call(
        kernel,
        name=name,
        out_shape=[
            shapes[n] if n in FAR else pltpu.VMEM(shapes[n].shape, shapes[n].dtype) for n in made
        ],
        in_specs=[in_specs[n] for n in ins] + [VMEM] * len(given) + [ANY] * len(after),
        out_specs=[HBM if n in FAR else VMEM for n in made],
        scratch_shapes=[pltpu.VMEM(shapes[n].shape, shapes[n].dtype) for n in scratch]
        + list(extra.values()),
        input_output_aliases={len(ins) + i: made.index(n) for i, n in enumerate(given)},
        **kernel_settings(mebibytes, micros),
    )(*ins.values(), *(kept[n] for n in given), *after)
    return dict(zip(made, outs, strict=True))


def block_rows(pair, parity, rows):
    return pl.ds(pl.multiple_of((2 * pair + parity) * rows, 16), rows)


def weight_product(r, left, right, position, owners):
    mols, tokens, _ = right.shape
    rows = left.shape[-2] // owners
    core = r.info[BITS]
    for target, parity in ((r.send, 1 - core), (r.keep, core)):
        blocks = [block_rows(o, parity, rows) for o in range(owners // 2)]
        if len(left.shape) == 2:
            own = jnp.concatenate([left[at] for at in blocks], 0)
        else:
            parts = [jnp.concatenate([left[m, at] for at in blocks], 0) for m in range(mols)]
            own = jnp.concatenate(parts, 1)
        for base in range(0, right.shape[2], 256):
            part = right[:, :, base : base + 256].reshape(mols * tokens, 256)
            out = nn(own, part).astype(low)
            target[:, :, position + base : position + base + 256] = out.reshape(
                owners // 2, rows, 256
            )


def sum_table(r, position, owners):
    both = jnp.concatenate([jnp.sum(r.dense_sums[...], 0), jnp.sum(r.attn_sums[...], 0)], 0)
    width = both.shape[1]
    rows = width // owners
    core = r.info[BITS]
    high = both.astype(low).astype(wide)
    zeros = jnp.zeros((LANES - 32, width), wide)
    r.table[...] = jnp.concatenate([high, both - high, zeros], 0).T.astype(low)
    for target, parity in ((r.send, 1 - core), (r.keep, core)):
        for o in range(owners // 2):
            target[o, :, position : position + LANES] = r.table[block_rows(o, parity, rows)]


def swap(block, bit):
    devices = lax.axis_size("dp")
    return lax.ppermute(block, "dp", [(i, i ^ (1 << bit)) for i in range(devices)])


def halve(info, keep, received, bits, bit, after):
    count, rows, columns = keep.shape
    place = 1 << bits.index(bit)

    def kernel(info, keep, received, after, send, own):
        mine = info[BITS + bit]
        for j in range(count // 2):
            base = j // place * 2 * place + j % place
            for target, value in ((send, 1 - mine), (own, mine)):
                index = base + value * place
                target[j] = (keep[index].astype(wide) + received[index].astype(wide)).astype(low)

    shape = pltpu.VMEM((count // 2, rows, columns), low)
    return pl.pallas_call(
        kernel,
        name="halve",
        out_shape=[shape, shape],
        in_specs=[SMEM, VMEM, VMEM, ANY],
        out_specs=[VMEM, VMEM],
        **kernel_settings(2, 20),
    )(info, keep, received, after)


class Scatter:
    def __init__(self, info, keep, send, route):
        self.info, self.keep, self.route = info, keep, list(route)
        self.bits = sorted(route)
        self.received = swap(send, 0)

    def step(self, after):
        bit = self.route.pop(0)
        send, self.keep = halve(self.info, self.keep, self.received, self.bits, bit, after)
        self.bits.remove(bit)
        self.received = swap(send, bit)
        return send


def finish(scatters, shapes, write):
    arrays = [array for one in scatters for array in (one.keep, one.received)]

    def kernel(*refs):
        ins, outs = refs[: len(arrays)], refs[len(arrays) :]
        sums = [
            keep[0].astype(wide) + received[0].astype(wide)
            for keep, received in zip(ins[::2], ins[1::2])
        ]
        write(sums, outs)

    return pl.pallas_call(
        kernel,
        name="finish",
        out_shape=[jax.ShapeDtypeStruct(shape, wide) for shape in shapes],
        in_specs=[VMEM] * len(arrays),
        out_specs=[VMEM] * len(shapes),
        **kernel_settings(8, 20),
    )(*arrays)


def write_vectors(table, gain, bias):
    vectors = table.T
    vectors = vectors[:16] + vectors[16:32]
    for i, source in enumerate((8, 0)):
        gain[i : i + 1] = vectors[source : source + 1]
    for i, source in enumerate((9, 10, 11, 4, 1, 2, 3, 12, 13)):
        bias[i] = vectors[source : source + 1]


def plain_sums(state, width, hidden):
    both = [jnp.sum(state[n], 0) for n in names(dense_sums=1, attn_sums=1)]
    parts = [jnp.pad(jnp.concatenate(both, 0), ((0, LANES - 16), (0, 0))).T]
    lefts = [state[n] for n in names(activated=1, second_in=1, first_in=1)]
    lefts.insert(2, jnp.swapaxes(state["att_t"], 1, 2))
    rights = [state[n] for n in names(out_grad=1, pre_grad=1, branch_grad=1, mixed_grad=1)]
    for left, right in zip(lefts, rights, strict=True):
        rows = left.shape[0] * left.shape[1]
        parts.append(tn(left.reshape(rows, -1), right.reshape(rows, -1)))
    sums = lax.psum_scatter(
        jnp.concatenate(parts, 1), "dp", scatter_dimension=0, tiled=True
    )
    sizes = [LANES, width, hidden, width]
    cuts = [sum(sizes[: i + 1]) for i in range(4)]
    table, down, up, proj, qkv = jnp.split(sums, cuts, 1)
    vectors = table.T
    gain = jnp.stack([vectors[8], vectors[0]])
    bias = jnp.stack([vectors[i] for i in (9, 10, 11, 4, 1, 2, 3, 12, 13)])
    return qkv, proj, up, down, gain, bias


def body(
    boundary, counts, id_flags, norm_gains, biases, qkv_weight, proj_weight, up_weight, down_weight
):
    mols = counts.shape[0]
    width = boundary.shape[2]
    hidden = up_weight.shape[2]
    length = boundary.shape[1] // mols
    half = (mols + 1) // 2
    groups = [list(range(half)), list(range(half, mols))]
    devices = lax.axis_size("dp")
    rows = width // devices
    in_kernel = rows % 16 == 0
    assert devices.bit_length() <= COUNTS
    index = lax.axis_index("dp")
    info = jnp.concatenate(
        [
            lax.axis_index("section")[None],
            (index >> jnp.arange(COUNTS - BITS)) & 1,
            counts,
            id_flags,
        ]
    ).astype(jnp.int32)
    state = {}

    def shapes(group):
        return shapes_of(mols, length, width, hidden, half, len(group))

    def take(*lists, **more):
        return {n: state[n] for n in sum(lists, ()) + tuple(more)}

    def kept(*lists):
        return {n: state.get(n) for n in sum(lists, ())}

    def put(out, *lists):
        state.update({n: out[n] for n in sum(lists, ())})

    sources = dict(
        ends=boundary[0],
        biases=jnp.transpose(biases, (1, 0, 2)),
        gains=norm_gains[0],
        qkv=qkv_weight[0],
        proj=proj_weight[0],
        up=up_weight[0],
        down=down_weight[0],
    )

    def first_forward(group, load):
        stop = rows_of(group, length)[0].stop

        def run(r):
            section = r.info[SECTION]
            pieces = {}
            if load:
                pieces["ends"] = (r.from_ends, r.ends, slice(0, stop))
                for name in names(biases=1, gains=1):
                    pieces[name] = (getattr(r, "from_" + name), getattr(r, name), ...)
                for third in range(3):
                    columns = pl.ds(third * width, width)
                    pieces[third] = (r.from_qkv, r.qkv, (slice(None), columns))
                early = list(pieces)
                for name in names(proj=1, up=1, down=1):
                    pieces[name] = (getattr(r, "from_" + name), getattr(r, name), ...)
                pieces[None] = (r.from_ends, r.ends, slice(stop, mols * length))

            def copy(key):
                source, target, at = pieces[key]
                sem = r.sems.at[list(pieces).index(key)]
                return pltpu.make_async_copy(source.at[at], target.at[at], sem)

            def wait(key):
                if load:
                    copy(key).wait()
                    if key == 0:
                        for late in pieces:
                            if late not in early:
                                copy(late).start()

            if load:
                for key in early:
                    copy(key).start()

            @pl.when(section == 0)
            def _():
                wait("ends")
                here = slice(stop - len(group) * length, stop)
                forward(r, group, r.ends[here].astype(wide), length, wait)
                wait(None)

            if load:

                @pl.when(section != 0)
                def _():
                    for key in pieces:
                        wait(key)

        ins = dict(info=info)
        kept_names = SAVED
        specs, extra = {}, {}
        if load:
            sent = {"from_" + n: sources[n] for n in LOADS}
            ins |= {n: pltpu.with_memory_space_constraint(a, pltpu.HBM) for n, a in sent.items()}
            specs = dict.fromkeys(sent, HBM)
            kept_names = LOADS + SAVED
            extra = dict(sems=pltpu.SemaphoreType.DMA((len(LOADS) + 3,)))
        else:
            ins |= take(FORWARD)
        out = call(
            run, shapes(group), ins, kept(kept_names), names(result=1), FORWARD_SCRATCH,
            "first", 8, 3.0, specs, extra,
        )
        put(out, kept_names)
        return out["result"]

    def tick(second, first, received, received_grad, micros):
        def back(r, group, out_grad):
            save_cotangent(r, group, out_grad, length)
            backward_hidden(r, group, out_grad, length)
            backward_middle(r, group, out_grad, length)
            backward_attention(r, group, length)

        def run(r):
            if second:

                @pl.when(r.info[SECTION] == 1)
                def _():
                    forward(r, second, r.received[...].astype(wide), length)
                    back(r, second, r.ends[rows_of(second, length)[0]].astype(wide))

            if first:

                @pl.when(r.info[SECTION] == 0)
                def _():
                    back(r, first, r.received_grad[...].astype(wide))

        ins = dict(info=info) | take(BACKWARD)
        changed = HIDDEN + MIDDLE + LATE
        extra = {}
        if second:
            ins |= take(FORWARD) | dict(received=received)
            changed = SAVED + changed
            extra = dict(result=pltpu.VMEM((len(second) * length, width), low))
        else:
            ins |= take(SAVED)
        if first:
            ins |= dict(received_grad=received_grad)
        out = call(
            run, shapes(second or first), ins, kept(changed), names(grad=1),
            names(residual=1) + BACKWARD_SCRATCH + CARRY, "tick", 16, micros, extra=extra,
        )
        put(out, changed)
        return out["grad"]

    hops = []
    for group in groups:
        result = first_forward(group, group is groups[0])
        hops.append(lax.ppermute(result, "section", [(0, 1)]))
    turned_weights = names(down_t=1, up_t=1, proj_t=1)

    def turn_weights(r):
        for source, target in ((r.down, r.down_t), (r.up, r.up_t), (r.proj, r.proj_t),):
            target[...] = source[...].T

    out = call(
        turn_weights, shapes(groups[1]), take(down=1, up=1, proj=1), {}, turned_weights, (), "turn", 4, 0.2,
        after=[result],
    )
    put(out, turned_weights)
    grad_hops = []
    for group, hop in zip(groups, hops):
        grad = tick(group, None, hop, None, 0.2)
        grad_hops.append(lax.ppermute(grad, "section", [(1, 0)]))
    done_grad = tick(None, groups[0], None, grad_hops[0], 1.0)

    def turn(r):
        for source, target in (
            (r.activated, r.active_t),
            (r.second_in, r.second_t),
            (r.first_in, r.first_t),
        ):
            target[...] = source[...].reshape(-1, source.shape[2]).T

    if in_kernel:
        turned = names(active_t=1, second_t=1, first_t=1)
        ins = take(activated=1, second_in=1, first_in=1)
        out = call(turn, shapes(groups[1]), ins, {}, turned, (), "turn", 4, 1.0, after=[done_grad])
        put(out, turned)

    last = groups[1]
    last_grad = grad_hops[1]
    order = []

    def after():
        return order[-1:]

    def chunk(columns):
        shape = jax.ShapeDtypeStruct((devices // 2, rows, columns), low)
        return shapes(last) | dict(send=shape, keep=shape)

    def run(kernel, columns, ins, changed, made, scratch, name, mebibytes=4, extra=None):
        fresh = names(send=1, keep=1) if columns and in_kernel else ()
        out = call(
            kernel, chunk(columns), dict(info=info) | ins, kept(changed), made + fresh, scratch,
            name, mebibytes, 20.0, extra=extra, after=after(),
        )
        put(out, changed, made)
        order.append(out["send"] if fresh else out[(changed + made)[0]])
        return out

    def scatter(out, route):
        return Scatter(info, out["keep"], out["send"], route) if in_kernel else None

    def on_first(r, *functions):
        @pl.when(r.info[SECTION] == 0)
        def _():
            for function in functions:
                function()

    def hidden_kernel(r):
        def back():
            out_grad = r.received_grad[...].astype(wide)
            save_cotangent(r, last, out_grad, length)
            backward_hidden(r, last, out_grad, length)

        on_first(r, back)
        if in_kernel:
            weight_product(r, r.active_t, r.out_grad, 0, devices)
            weight_product(r, r.second_t, r.pre_grad, width, devices)

    def middle_kernel(r):
        on_first(r, lambda: backward_middle(r, last, r.received_grad[...].astype(wide), length))
        if in_kernel:
            weight_product(r, r.att_t, r.branch_grad, 0, devices)

    def attention_kernel(r):
        on_first(r, lambda: backward_attention(r, last, length))

    def part(third):
        ins = take(first_t=1, mixed_grad=1)
        columns, made, scratch = width, (), ()
        if third == 2:
            ins |= take(dense_sums=1, attn_sums=1, outputs=1, grads=1)
            columns, made, scratch = width + LANES, names(far_outputs=1, far_grads=1), names(table=1)

        def kernel(r):
            if third == 2:
                copies = [
                    pltpu.make_async_copy(r.outputs, r.far_outputs, r.sems.at[0]),
                    pltpu.make_async_copy(r.grads, r.far_grads, r.sems.at[1]),
                ]
                for copy in copies:
                    copy.start()
                sum_table(r, width, devices)
            at = slice(third * width, (third + 1) * width)
            weight_product(r, r.first_t, r.mixed_grad.at[:, :, at], 0, devices)
            if third == 2:
                for copy in copies:
                    copy.wait()

        extra = dict(sems=pltpu.SemaphoreType.DMA((2,)))
        out = run(kernel, columns, ins, (), made, scratch, "part", 4, extra if made else None)
        return scatter(out, (1, 2, 3))

    def hidden_step():
        ins = take(slope=1, down_t=1) | dict(received_grad=last_grad)
        if in_kernel:
            ins |= take(active_t=1, second_t=1)
        out = run(hidden_kernel, width + hidden, ins, HIDDEN, (), (), "hidden")
        return scatter(out, ROUTES[0])

    def middle_step():
        ins = take(pre_grad=1, gains=1, proj_t=1, up_t=1, n2=1, r2=1, att_t=1)
        ins |= dict(received_grad=last_grad)
        out = run(middle_kernel, width, ins, MIDDLE, CARRY, (), "middle")
        return scatter(out, ROUTES[1])

    def attention_step():
        ins = take(CARRY, gains=1, qkv=1, q=1, k=1, v=1, probs=1, inverse=1, att_t=1)
        ins |= take(n1=1, r1=1)
        run(attention_kernel, 0, ins, LATE, names(grad=1), BACKWARD_SCRATCH, "attention", 12)

    kernels = dict(
        h=hidden_step, m=middle_step, t=attention_step, q=lambda: part(0), k=lambda: part(1),
        v=lambda: part(2),
    )
    done = {}
    for word in PLAN:
        if len(word) == 1:
            if in_kernel or word in "hmt":
                done[word] = kernels[word]()
        elif in_kernel:
            order.append(done[word[0]].step(order[-1]))
    one = (rows, width)
    if in_kernel:

        def write(sums, outs):
            h, m, q, k, v = sums
            down, up, proj, qkv, gain, bias = outs
            down[...] = h[:, :width]
            up[...] = h[:, width:]
            proj[...] = m
            qkv[:, :width] = q
            qkv[:, width : 2 * width] = k
            qkv[:, 2 * width :] = v[:, :width]
            write_vectors(v[:, width:], gain, bias)

        down_grad, up_grad, proj_grad, qkv_grad, gain_grad, bias_grad = finish(
            [done[word] for word in "hmqkv"],
            [one, (rows, hidden), one, (rows, 3 * width), (2, rows), (9, 1, rows)],
            write,
        )
        bias_grad = jnp.squeeze(bias_grad, 1)
    else:
        qkv_grad, proj_grad, up_grad, down_grad, gain_grad, bias_grad = plain_sums(
            state, width, hidden
        )
    return (
        state["far_outputs" if in_kernel else "outputs"][None],
        state["far_grads" if in_kernel else "grads"][None],
        qkv_grad[None],
        proj_grad[None],
        up_grad[None],
        down_grad[None],
        gain_grad[None],
        bias_grad[None],
    )


def solution(mesh):
    rows = P("section", "dp", None)
    columns = P("section", None, "dp")
    weights = P("section", None, None)
    return jax.shard_map(
        body,
        mesh=mesh,
        in_specs=(rows, P("dp"), P("dp")) + (weights,) * 6,
        out_specs=(rows,) * 6 + (columns,) * 2,
        check_vma=False,
    )
```
